32 devices in a mesh: members: 2 (over x), gy: 8 (over z, y), gx: 2 (over core).
Axes of the slice: x: 2, y: 2, z: 4, core: 2. Of those that a mesh axis runs over, the one named last changes fastest.
Arguments:
- right_side: float32 [2048, 2048], P(('members', 'gy'), 'gx'), parts along dimension 0, may hold values from -60 to 60
- faces: float32 [2, 1024, 2048], P(None, 'gy', 'gx'), may hold values from 0.3 to 3
- ratio: float32 [1024, 2048], P('gy', 'gx'), may hold values from 0.05 to 0.5
- centre: float32 [1024, 2048], P('gy', 'gx'), may hold values from 0.5 to 1
- offdiag: float32 [8, 1024, 2048], P(None, 'gy', 'gx'), may hold values from 0.005 to 0.05
- mask: int32 [1024, 2048], P('gy', 'gx'), may hold values 0 or 1
Outputs:
- solution: float32 [2048, 2048], P(('members', 'gy'), 'gx'), parts along dimension 0
- residual: float32 [2048, 2048], P(('members', 'gy'), 'gx'), parts along dimension 0
The draws below stay inside these ranges and needn't reach their ends.
There are 2 independent parts, one for each index of `members`. The reference program is written for one: setup_inputs(seed, part) draws one part's arguments, and reference() takes and returns one part's arrays. A program takes and returns all parts, laid end to end along the dimension named above; an argument that names none is the same for every part. Nothing has to cross between parts.
All inputs are finite; a program needn't handle non-finite values. No bound on the sum of `mask` on one device may be relied on, other than what follows from the above.
Results may differ from the reference program's by a relative error of at most 0.00012.
Values sent between devices are 32-bit elements; how exact they have to be, the bound alone decides.
No kernel may reach another device: no remote copies, remote signals or barrier semaphores. Data moves between devices by JAX's collectives and lax.ppermute only.
A program may use at most 64 MiB of HBM per device.

```python
import math
import jax
import jax.numpy as jnp

ITERS = 3
NY = 1024
NX = 2048


def draw_right_side(key, part):
    key = jax.random.fold_in(key, 11)
    noise_key = jax.random.fold_in(key, 0)
    growth = 3.0 ** (jnp.arange(NY, dtype=jnp.float32)[:, None] / (NY - 1))
    return jnp.clip(jax.random.normal(noise_key, (NY, NX), jnp.float32), -4.0, 4.0) * growth


def plant(result, rng, least, largest):
    longest = result.shape.index(max(result.shape))
    spots = []
    for shift in (0, 1):
        where = [jax.random.randint(jax.random.fold_in(rng, axis), (), 0, length) for axis, length in enumerate(result.shape)]
        where[longest] = (where[longest] + shift) % result.shape[longest]
        spots.append(tuple(where))
    return result.at[spots[0]].set(least).at[spots[1]].set(largest)


def block_scale(own_key, shape, shards, low, largest):
    gain = 1.0
    for dim, parts in shards:
        heights = jax.random.uniform(jax.random.fold_in(jax.random.fold_in(own_key, 6), dim), (parts,), jnp.float32, low / len(shards), largest / len(shards))
        gain = gain * jnp.repeat(jnp.exp(heights), shape[dim] // parts).reshape((-1,) + (1,) * (len(shape) - 1 - dim))
    return gain


def setup_inputs(seed: int = 0, part: int = 0) -> dict:
    key_list = jax.random.split(jax.random.key(seed), 7)
    own_keys = jax.random.split(jax.random.fold_in(key_list[6], part), 7)
    right_side = draw_right_side(jax.random.fold_in(jax.random.fold_in(key_list[6], part), 71), part)
    faces = jnp.clip(jnp.exp(math.log(3.0) - 2.3025851 * jax.random.uniform(key_list[1], (2, NY, NX), jnp.float32) ** block_scale(key_list[1], (2, NY, NX), ((1, 8), (2, 2)), -0.2, 0.2)), 0.3, 3.0)
    ratio = jnp.clip(jnp.exp(math.log(0.5) - 2.3025851 * jax.random.uniform(key_list[2], (NY, NX), jnp.float32) ** block_scale(key_list[2], (NY, NX), ((0, 8), (1, 2)), -0.2, 0.2)), 0.05, 0.5)
    centre = jnp.clip(0.5 + 0.5 * jax.random.uniform(key_list[3], (NY, NX), jnp.float32) ** block_scale(key_list[3], (NY, NX), ((0, 8), (1, 2)), -0.2, 0.2), 0.5, 1.0)
    offdiag = jnp.clip(0.005 + 0.045 * jax.random.uniform(key_list[4], (8, NY, NX), jnp.float32) ** block_scale(key_list[4], (8, NY, NX), ((1, 8), (2, 2)), -0.2, 0.2), 0.005, 0.05)
    mask = plant((jax.random.randint(key_list[5], (NY, NX), 0, 8) < 7).astype(jnp.int32), jax.random.fold_in(key_list[5], 1), 0, 1)
    return dict(right_side=right_side, faces=faces, ratio=ratio, centre=centre, offdiag=offdiag, mask=mask)


neighbour_steps = [(-1, -1), (-1, 0), (-1, 1), (0, -1), (0, 1), (1, -1), (1, 0), (1, 1)]


def displaced(field, down, across):
    padded = jnp.pad(field, 1)
    height, breadth = field.shape
    return padded[1 + down:1 + down + height, 1 + across:1 + across + breadth]


def operate(field, west_face, east_face, south_face, north_face, diagonal, wet_cells):
    total = diagonal * field - west_face * displaced(field, 0, -1) - east_face * displaced(field, 0, 1)
    total = total - south_face * displaced(field, -1, 0) - north_face * displaced(field, 1, 0)
    return wet_cells * total


def precondition(field, centre, offdiag, wet_cells):
    total = centre * field
    for offset_index, (down, across) in enumerate(neighbour_steps):
        total = total + displaced(offdiag[offset_index] * field, -down, -across)
    return wet_cells * total


def reference(right_side, faces, ratio, centre, offdiag, mask):
    wet_cells = mask.astype(jnp.float32)
    west_face = faces[0]
    south_face = faces[1]
    east_face = displaced(west_face, 0, 1)
    north_face = displaced(south_face, 1, 0)
    diagonal = west_face + east_face + south_face + north_face + ratio
    residual = wet_cells * right_side
    solution = jnp.zeros_like(residual)
    direction = jnp.zeros_like(residual)
    image = jnp.zeros_like(residual)
    rz_before = jnp.float32(1.0)
    for iteration in range(ITERS):
        smoothed = precondition(residual, centre, offdiag, wet_cells)
        applied = operate(smoothed, west_face, east_face, south_face, north_face, diagonal, wet_cells)
        rz_now = jnp.sum(residual * smoothed)
        if iteration == 0:
            direction = smoothed
            image = applied
        else:
            ratio_now = rz_now / rz_before
            direction = smoothed + ratio_now * direction
            image = applied + ratio_now * image
        curvature = jnp.sum(direction * image)
        step_size = rz_now / curvature
        solution = solution + step_size * direction
        residual = residual - step_size * image
        rz_before = rz_now
    return solution, residual
```

```python
import functools

import jax
import jax.numpy as jnp
from jax import lax
from jax.experimental import pallas as pl
from jax.experimental.pallas import tpu as pltpu
from jax.sharding import PartitionSpec as P

ITERS = 3
SHIFT = 1.0
SCALE = 4.0
LANES = 128
STRIP = 8
EDGE = 2 * STRIP

neighbour_steps = [(-1, -1), (-1, 0), (-1, 1), (0, -1), (0, 1), (1, -1), (1, 0), (1, 1)]

FIELDS = 6 + len(neighbour_steps)
REACH = 2 * ITERS
LOW_ROWS = [REACH, REACH - 1, REACH - 1, REACH - 2, REACH - 2, REACH - 2] + [
    REACH - 1 + down for down, _ in neighbour_steps
]
HIGH_ROWS = [REACH, REACH - 1, REACH - 1, REACH - 2, REACH - 2, REACH - 1] + [
    REACH - 1 - down for down, _ in neighbour_steps
]
PACKED = -(-max(sum(LOW_ROWS), sum(HIGH_ROWS)) // STRIP) * STRIP
PRODUCTS = (ITERS + 1) * ITERS
KEPT = 2 * ITERS + 1
VMEM_BYTES = 48 * 1024 * 1024


def field(refs, which, rows):
    right_side, mask, centre, ratio, faces, offdiag = refs
    if which == 0:
        return mask[rows, :].astype(jnp.float32) * right_side[rows, :]
    if which == 1:
        return mask[rows, :].astype(jnp.float32)
    if which == 2:
        return centre[rows, :]
    if which == 3:
        return ratio[rows, :]
    if which < 6:
        return faces[which - 4, rows, :]
    return offdiag[which - 6, rows, :]


def pack_rows_kernel(*refs):
    first, last = refs[0:6], refs[6:12]
    up, down = refs[12:14]
    place = 0
    for which, count in enumerate(LOW_ROWS):
        up[place : place + count, :] = field(last, which, slice(STRIP - count, STRIP))
        place += count
    if place < PACKED:
        up[place:PACKED, :] = jnp.zeros((PACKED - place, up.shape[1]), jnp.float32)
    place = 0
    for which, count in enumerate(HIGH_ROWS):
        down[place : place + count, :] = field(first, which, slice(0, count))
        place += count
    if place < PACKED:
        down[place:PACKED, :] = jnp.zeros((PACKED - place, down.shape[1]), jnp.float32)


def facing(west, east, side):
    lane = lax.broadcasted_iota(jnp.int32, west.shape, west.ndim - 1)
    return jnp.where(
        side == 0,
        jnp.where(lane >= LANES // 2, east, 0.0),
        jnp.where(lane < LANES // 2, west, 0.0),
    )


def pack_columns_kernel(*refs):
    west, east, out = refs[0:6], refs[6:12], refs[12]
    side = lax.axis_index("gx")
    everything = slice(None)
    for which in range(FIELDS):
        out[which] = facing(
            field(west, which, everything), field(east, which, everything), side
        )


def row_above(block, before):
    row = lax.broadcasted_iota(jnp.int32, block.shape, 0)
    return jnp.where(row == 0, pltpu.roll(before, 1, 0), pltpu.roll(block, 1, 0))


def row_below(block, after):
    row = lax.broadcasted_iota(jnp.int32, block.shape, 0)
    last = STRIP - 1
    return jnp.where(row == last, pltpu.roll(after, last, 0), pltpu.roll(block, last, 0))


def strip_rows(strip):
    return pl.ds(pl.multiple_of(strip * STRIP, STRIP), STRIP)


def krylov(load, strips, counted, sums, coef, kept):
    width = kept.shape[2]
    breadth = width - LANES
    zero = jnp.zeros((STRIP, width), jnp.float32)

    def west_of(block):
        return pltpu.roll(block, 1, 1)

    def east_of(block):
        return pltpu.roll(block, width - 1, 1)

    def prepare(step, south_after):
        strip = strips - 1 - step
        rows = strip_rows(strip)
        kept[0, rows, :] = load(0, strip)
        wet = load(1, strip)
        coef[4, rows, :] = load(2, strip)
        for index, (down, across) in enumerate(neighbour_steps):
            weight = load(6 + index, strip)
            if across == 1:
                weight = west_of(weight)
            elif across == -1:
                weight = east_of(weight)
            coef[(down + 1) * 3 + across + 1, rows, :] = weight
        west = load(4, strip)
        south = load(5, strip)
        east = east_of(west)
        north = row_below(south, south_after)
        scaled = wet * (1.0 / SCALE)
        coef[9, rows, :] = wet
        coef[10, rows, :] = scaled * (west + east + south + north + load(3, strip))
        coef[11, rows, :] = scaled * west
        coef[12, rows, :] = scaled * east
        coef[13, rows, :] = scaled * south
        coef[14, rows, :] = scaled * north
        return south

    lax.fori_loop(0, strips, prepare, zero)

    for order in range(ITERS):
        smoothed = ITERS + 1 + order

        def smooth(strip, carried):
            above, partial = carried
            rows = strip_rows(strip)
            block = kept[order, rows, :]
            shifted = {-1: east_of(block), 0: block, 1: west_of(block)}
            totals = []
            for down in range(3):
                totals.append(
                    coef[down * 3, rows, :] * shifted[-1]
                    + coef[down * 3 + 1, rows, :] * shifted[0]
                    + coef[down * 3 + 2, rows, :] * shifted[1]
                )
            row = lax.broadcasted_iota(jnp.int32, block.shape, 0)
            rising = pltpu.roll(totals[0], STRIP - 1, 0)
            falling = pltpu.roll(totals[2], 1, 0)
            done = strip_rows(jnp.maximum(strip - 1, 0))
            kept[smoothed, done, :] = coef[9, done, :] * (
                partial + jnp.where(row == STRIP - 1, rising, 0.0)
            )
            partial = (
                totals[1]
                + jnp.where(row == 0, above, falling)
                + jnp.where(row == STRIP - 1, 0.0, rising)
            )
            return falling, partial

        _, partial = lax.fori_loop(0, strips, smooth, (zero, zero))
        done = slice((strips - 1) * STRIP, strips * STRIP)
        kept[smoothed, done, :] = coef[9, done, :] * partial

        def operate(strip, carried):
            rows = strip_rows(strip)
            block = kept[smoothed, rows, :]
            before = kept[smoothed, strip_rows(jnp.maximum(strip - 1, 0)), :]
            after = kept[smoothed, strip_rows(jnp.minimum(strip + 1, strips - 1)), :]
            kept[order + 1, rows, :] = (
                coef[10, rows, :] * block
                - coef[11, rows, :] * west_of(block)
                - coef[12, rows, :] * east_of(block)
                - coef[13, rows, :] * row_above(block, before)
                - coef[14, rows, :] * row_below(block, after)
                - (SHIFT / SCALE) * kept[order, rows, :]
            )
            return carried

        lax.fori_loop(0, strips, operate, 0)

    def gather(step, totals):
        strip = counted(step)
        rows = strip_rows(strip)
        result = list(totals)
        for start in range(0, breadth, LANES):
            lanes = slice(start, start + LANES)
            bases = [kept[i, rows, lanes] for i in range(KEPT)]
            for i in range(ITERS + 1):
                for j in range(ITERS):
                    result[i * ITERS + j] += bases[i] * bases[ITERS + 1 + j]
        return tuple(result)

    return gather


def tile_kernel(*refs):
    own, columns, kept, sums, coef = refs[0:6], refs[6], refs[7], refs[8], refs[9]
    strips = kept.shape[1] // STRIP

    def load(which, strip):
        rows = strip_rows(strip)
        return jnp.concatenate(
            [field(own, which, rows), columns[which, rows, :]], axis=1
        )

    gather = krylov(load, strips, lambda step: step + 1, None, coef, kept)
    zero = jnp.zeros((STRIP, LANES), jnp.float32)
    totals = lax.fori_loop(0, strips - 2, gather, (zero,) * PRODUCTS)
    for index in range(PRODUCTS):
        sums[index] = totals[index]


def edge_kernel(*refs):
    first, last = refs[0:6], refs[6:12]
    columns_first, columns_last, low, high, corners, sums = refs[12:18]
    kept, gram = refs[18:20]
    joined, coef = refs[20:22]
    breadth = low.shape[1]
    width = breadth + LANES
    rows = kept.shape[1]
    everything = slice(0, EDGE)
    place_low, place_high = 0, PACKED
    for which in range(FIELDS):
        joined[which, 0:STRIP, :] = jnp.zeros((STRIP, width), jnp.float32)
        count = LOW_ROWS[which]
        target = slice(STRIP - count, STRIP)
        joined[which, target, 0:breadth] = low[place_low : place_low + count, :]
        joined[which, target, breadth:width] = corners[place_low : place_low + count, :]
        place_low += count
        target = slice(STRIP, STRIP + EDGE)
        joined[which, target, 0:breadth] = field(first, which, everything)
        joined[which, target, breadth:width] = columns_first[which]
        target = slice(STRIP + EDGE, STRIP + 2 * EDGE)
        joined[which, target, 0:breadth] = field(last, which, everything)
        joined[which, target, breadth:width] = columns_last[which]
        joined[which, rows - STRIP : rows, :] = jnp.zeros((STRIP, width), jnp.float32)
        count = HIGH_ROWS[which]
        target = slice(rows - STRIP, rows - STRIP + count)
        joined[which, target, 0:breadth] = high[
            place_high - PACKED : place_high - PACKED + count, :
        ]
        joined[which, target, breadth:width] = corners[place_high : place_high + count, :]
        place_high += count

    def load(which, strip):
        return joined[which, strip_rows(strip), :]

    gather = krylov(load, rows // STRIP, lambda step: 1 + 3 * step, None, coef, kept)
    totals = lax.fori_loop(0, 2, gather, tuple(sums[i] for i in range(PRODUCTS)))
    gram[...] = jnp.zeros(gram.shape, jnp.float32)
    for index in range(PRODUCTS):
        total = jnp.sum(jnp.sum(totals[index], axis=0, keepdims=True), axis=1, keepdims=True)
        gram[index : index + 1, :] = jnp.broadcast_to(total, (1, LANES))


def recurrences(gram):
    shift, scale = SHIFT, SCALE
    residual = [1.0]
    direction = []
    steps = [0.0] * ITERS
    rz_before = None
    for order in range(ITERS):
        rz = None
        for i in range(order + 1):
            inner = None
            for j in range(order + 1):
                term = residual[j] * gram[i][j]
                inner = term if inner is None else inner + term
            inner = residual[i] * inner
            rz = inner if rz is None else rz + inner
        if order == 0:
            direction = [1.0]
        else:
            ratio = rz / rz_before
            direction = [
                residual[i] + ratio * direction[i] if i < order else residual[i]
                for i in range(order + 1)
            ]
        image = [0.0] * (order + 2)
        for i in range(order + 1):
            image[i] = image[i] + shift * direction[i]
            image[i + 1] = image[i + 1] + scale * direction[i]
        curvature = None
        for i in range(order + 2):
            inner = None
            for j in range(order + 1):
                term = direction[j] * gram[i][j]
                inner = term if inner is None else inner + term
            inner = image[i] * inner
            curvature = inner if curvature is None else curvature + inner
        step = rz / curvature
        for i in range(order + 1):
            steps[i] = steps[i] + step * direction[i]
        residual = [
            (residual[i] if i < order + 1 else 0.0) - step * image[i]
            for i in range(order + 2)
        ]
        rz_before = rz
    return steps, residual


def combine_kernel(gram_ref, kept, edges, solution_ref, residual_ref):
    height, breadth = solution_ref.shape
    gram = [
        [gram_ref[i * ITERS + j : i * ITERS + j + 1, :] for j in range(ITERS)]
        for i in range(ITERS + 1)
    ]
    steps, residual = recurrences(gram)

    def wide(value):
        value = jnp.broadcast_to(value, (STRIP, LANES))
        return jnp.concatenate([value] * (breadth // LANES), axis=1)

    def put(source, rows_from, rows_to):
        total = None
        for j in range(ITERS):
            term = wide(steps[j]) * source[ITERS + 1 + j, rows_from, 0:breadth]
            total = term if total is None else total + term
        solution_ref[rows_to, :] = total
        total = None
        for i in range(ITERS + 1):
            term = wide(residual[i]) * source[i, rows_from, 0:breadth]
            total = term if total is None else total + term
        residual_ref[rows_to, :] = total

    put(edges, slice(STRIP, 2 * STRIP), slice(0, STRIP))
    put(edges, slice(4 * STRIP, 5 * STRIP), slice(height - STRIP, height))

    def middle(strip, carried):
        rows = strip_rows(strip)
        put(kept, rows, rows)
        return carried

    lax.fori_loop(1, height // STRIP - 1, middle, 0)


def params():
    return pltpu.CompilerParams(vmem_limit_bytes=VMEM_BYTES)


def cost(flops, moved):
    return pl.CostEstimate(flops=flops, bytes_accessed=moved, transcendentals=0)


def blocks(shapes, rows, columns, at):
    specs = []
    for shape in shapes:
        lead = tuple(shape[:-2])
        block = lead + (rows, columns)
        index = (0,) * len(lead) + at
        specs.append(pl.BlockSpec(block, lambda step, index=index: index))
    return specs


def whole(*shapes):
    return [pl.BlockSpec(shape, lambda step, n=len(shape): (0,) * n) for shape in shapes]


def body(right_side, faces, ratio, centre, offdiag, mask):
    height, breadth = right_side.shape
    width = breadth + LANES
    args = (right_side, mask, centre, ratio, faces, offdiag)
    shapes = [a.shape for a in args]
    f32 = jnp.float32
    side = lax.axis_index("gx")
    gy = lax.axis_size("gy")
    forward = [(i, i + 1) for i in range(gy - 1)]
    backward = [(b, a) for a, b in forward]
    swap = [(0, 1), (1, 0)]

    packed = jax.ShapeDtypeStruct((PACKED, breadth), f32)
    up, down = pl.pallas_call(
        pack_rows_kernel,
        grid=(1,),
        in_specs=blocks(shapes, STRIP, breadth, (0, 0))
        + blocks(shapes, STRIP, breadth, (height // STRIP - 1, 0)),
        out_specs=whole(packed.shape, packed.shape),
        out_shape=(packed, packed),
        compiler_params=params(),
        cost_estimate=cost(0, 2 * 4 * PACKED * breadth * 2),
        name="pack_rows",
    )(*args, *args)
    low = lax.ppermute(up, "gy", forward)
    high = lax.ppermute(down, "gy", backward)

    columns = jax.ShapeDtypeStruct((FIELDS, height, LANES), f32)
    columns = pl.pallas_call(
        pack_columns_kernel,
        grid=(1,),
        in_specs=blocks(shapes, height, LANES, (0, 0))
        + blocks(shapes, height, LANES, (0, breadth // LANES - 1)),
        out_specs=whole(columns.shape)[0],
        out_shape=columns,
        compiler_params=params(),
        cost_estimate=cost(0, 3 * 4 * FIELDS * height * LANES),
        name="pack_columns",
    )(*args, *args)
    columns = lax.ppermute(columns, "gx", swap)

    cells = height * width
    kept, sums = pl.pallas_call(
        tile_kernel,
        grid=(1,),
        in_specs=whole(*shapes, columns.shape),
        out_specs=whole((KEPT, height, width), (PRODUCTS, STRIP, LANES)),
        out_shape=(
            jax.ShapeDtypeStruct((KEPT, height, width), f32),
            jax.ShapeDtypeStruct((PRODUCTS, STRIP, LANES), f32),
        ),
        scratch_shapes=[pltpu.VMEM((15, height, width), f32)],
        compiler_params=params(),
        cost_estimate=cost(100 * cells, 4 * cells * (FIELDS + KEPT)),
        name="tile",
    )(*args, columns)

    received = jnp.concatenate([low, high], axis=0)
    corners = lax.ppermute(
        facing(received[:, :LANES], received[:, breadth - LANES :], side), "gx", swap
    )

    rows = 2 * (STRIP + EDGE)
    edges, gram = pl.pallas_call(
        edge_kernel,
        grid=(1,),
        in_specs=blocks(shapes, EDGE, breadth, (0, 0))
        + blocks(shapes, EDGE, breadth, (height // EDGE - 1, 0))
        + blocks([columns.shape], EDGE, LANES, (0, 0))
        + blocks([columns.shape], EDGE, LANES, (height // EDGE - 1, 0))
        + whole(low.shape, high.shape, corners.shape, sums.shape),
        out_specs=whole((KEPT, rows, width), (2 * STRIP, LANES)),
        out_shape=(
            jax.ShapeDtypeStruct((KEPT, rows, width), f32),
            jax.ShapeDtypeStruct((2 * STRIP, LANES), f32),
        ),
        scratch_shapes=[
            pltpu.VMEM((FIELDS, rows, width), f32),
            pltpu.VMEM((15, rows, width), f32),
        ],
        compiler_params=params(),
        cost_estimate=cost(100 * rows * width, 4 * rows * width * (FIELDS + KEPT)),
        name="edge",
    )(*args, *args, columns, columns, low, high, corners, sums)

    gram = gram + lax.ppermute(gram, "gx", swap)
    reach = 1
    while reach < gy:
        gram = gram + lax.ppermute(gram, "gy", [(i, i ^ reach) for i in range(gy)])
        reach *= 2

    tile = jax.ShapeDtypeStruct((height, breadth), f32)
    return pl.pallas_call(
        combine_kernel,
        grid=(1,),
        in_specs=whole(gram.shape, kept.shape, edges.shape),
        out_specs=whole(tile.shape, tile.shape),
        out_shape=(tile, tile),
        compiler_params=params(),
        cost_estimate=cost(14 * height * breadth, 4 * height * breadth * (KEPT + 2)),
        name="combine",
    )(gram, kept, edges)


def solution(mesh):
    return jax.shard_map(
        body,
        mesh=mesh,
        in_specs=(
            P(("members", "gy"), "gx"),
            P(None, "gy", "gx"),
            P("gy", "gx"),
            P("gy", "gx"),
            P(None, "gy", "gx"),
            P("gy", "gx"),
        ),
        out_specs=(P(("members", "gy"), "gx"), P(("members", "gy"), "gx")),
        check_vma=False,
    )
```

```python
import functools

import jax
import jax.numpy as jnp
from jax import lax
from jax.experimental import pallas as pl
from jax.experimental.pallas import tpu as pltpu
from jax.sharding import PartitionSpec as P

ITERS = 3
SHIFT = 1.0
SCALE = 4.0
LANES = 128
STRIP = 8
EDGE = 2 * STRIP

neighbour_steps = [(-1, -1), (-1, 0), (-1, 1), (0, -1), (0, 1), (1, -1), (1, 0), (1, 1)]

FIELDS = 6 + len(neighbour_steps)
REACH = 2 * ITERS
LOW_ROWS = [REACH, REACH - 1, REACH - 1, REACH - 2, REACH - 2, REACH - 2] + [
    REACH - 1 + down for down, _ in neighbour_steps
]
HIGH_ROWS = [REACH, REACH - 1, REACH - 1, REACH - 2, REACH - 2, REACH - 1] + [
    REACH - 1 - down for down, _ in neighbour_steps
]
PACKED = -(-max(sum(LOW_ROWS), sum(HIGH_ROWS)) // STRIP) * STRIP
PRODUCTS = (ITERS + 1) * ITERS
KEPT = 2 * ITERS + 1
VMEM_BYTES = 32 * 1024 * 1024
PACK_VMEM_BYTES = 62 * 1024 * 1024


def field(refs, which, rows):
    right_side, mask, centre, ratio, faces, offdiag = refs
    if which == 0:
        return mask[rows, :].astype(jnp.float32) * right_side[rows, :]
    if which == 1:
        return mask[rows, :].astype(jnp.float32)
    if which == 2:
        return centre[rows, :]
    if which == 3:
        return ratio[rows, :]
    if which < 6:
        return faces[which - 4, rows, :]
    return offdiag[which - 6, rows, :]


def pack_rows_kernel(*refs):
    first, last = refs[0:6], refs[6:12]
    up, down = refs[12:14]
    place = 0
    for which, count in enumerate(LOW_ROWS):
        up[place : place + count, :] = field(last, which, slice(STRIP - count, STRIP))
        place += count
    if place < PACKED:
        up[place:PACKED, :] = jnp.zeros((PACKED - place, up.shape[1]), jnp.float32)
    place = 0
    for which, count in enumerate(HIGH_ROWS):
        down[place : place + count, :] = field(first, which, slice(0, count))
        place += count
    if place < PACKED:
        down[place:PACKED, :] = jnp.zeros((PACKED - place, down.shape[1]), jnp.float32)


def facing(west, east, side):
    lane = lax.broadcasted_iota(jnp.int32, west.shape, west.ndim - 1)
    return jnp.where(
        side == 0,
        jnp.where(lane >= LANES // 2, east, 0.0),
        jnp.where(lane < LANES // 2, west, 0.0),
    )


def pack_columns_kernel(*refs):
    west, east, out = refs[0:6], refs[6:12], refs[13]
    side = lax.axis_index("gx")
    everything = slice(None)
    for which in range(FIELDS):
        out[which] = facing(
            field(west, which, everything), field(east, which, everything), side
        )


def row_above(block, before):
    row = lax.broadcasted_iota(jnp.int32, block.shape, 0)
    return jnp.where(row == 0, pltpu.roll(before, 1, 0), pltpu.roll(block, 1, 0))


def row_below(block, after):
    row = lax.broadcasted_iota(jnp.int32, block.shape, 0)
    last = STRIP - 1
    return jnp.where(row == last, pltpu.roll(after, last, 0), pltpu.roll(block, last, 0))


def strip_rows(strip):
    return pl.ds(pl.multiple_of(strip * STRIP, STRIP), STRIP)


def krylov(load, strips, counted, unroll, coef, kept):
    width = kept.shape[2]
    breadth = width - LANES
    zero = jnp.zeros((STRIP, width), jnp.float32)

    def west_of(block):
        return pltpu.roll(block, 1, 1)

    def east_of(block):
        return pltpu.roll(block, width - 1, 1)

    def prepare(step, south_after):
        strip = strips - 1 - step
        rows = strip_rows(strip)
        kept[0, rows, :] = load(0, strip)
        wet = load(1, strip)
        coef[4, rows, :] = load(2, strip)
        for index, (down, across) in enumerate(neighbour_steps):
            weight = load(6 + index, strip)
            if across == 1:
                weight = west_of(weight)
            elif across == -1:
                weight = east_of(weight)
            coef[(down + 1) * 3 + across + 1, rows, :] = weight
        west = load(4, strip)
        south = load(5, strip)
        east = east_of(west)
        north = row_below(south, south_after)
        scaled = wet * (1.0 / SCALE)
        coef[9, rows, :] = wet
        coef[10, rows, :] = scaled * (west + east + south + north + load(3, strip))
        coef[11, rows, :] = scaled * west
        coef[12, rows, :] = scaled * east
        coef[13, rows, :] = scaled * south
        coef[14, rows, :] = scaled * north
        return south

    lax.fori_loop(0, strips, prepare, zero, unroll=unroll)

    for order in range(ITERS):
        smoothed = ITERS + 1 + order

        def smooth(strip, carried):
            above, partial = carried
            rows = strip_rows(strip)
            block = kept[order, rows, :]
            shifted = {-1: east_of(block), 0: block, 1: west_of(block)}
            totals = []
            for down in range(3):
                totals.append(
                    coef[down * 3, rows, :] * shifted[-1]
                    + coef[down * 3 + 1, rows, :] * shifted[0]
                    + coef[down * 3 + 2, rows, :] * shifted[1]
                )
            row = lax.broadcasted_iota(jnp.int32, block.shape, 0)
            rising = pltpu.roll(totals[0], STRIP - 1, 0)
            falling = pltpu.roll(totals[2], 1, 0)
            done = strip_rows(jnp.maximum(strip - 1, 0))
            kept[smoothed, done, :] = coef[9, done, :] * (
                partial + jnp.where(row == STRIP - 1, rising, 0.0)
            )
            partial = (
                totals[1]
                + jnp.where(row == 0, above, falling)
                + jnp.where(row == STRIP - 1, 0.0, rising)
            )
            return falling, partial

        _, partial = lax.fori_loop(0, strips, smooth, (zero, zero), unroll=unroll)
        done = slice((strips - 1) * STRIP, strips * STRIP)
        kept[smoothed, done, :] = coef[9, done, :] * partial

        def operate(strip, carried):
            rows = strip_rows(strip)
            block = kept[smoothed, rows, :]
            before = kept[smoothed, strip_rows(jnp.maximum(strip - 1, 0)), :]
            after = kept[smoothed, strip_rows(jnp.minimum(strip + 1, strips - 1)), :]
            kept[order + 1, rows, :] = (
                coef[10, rows, :] * block
                - coef[11, rows, :] * west_of(block)
                - coef[12, rows, :] * east_of(block)
                - coef[13, rows, :] * row_above(block, before)
                - coef[14, rows, :] * row_below(block, after)
                - (SHIFT / SCALE) * kept[order, rows, :]
            )
            return carried

        lax.fori_loop(0, strips, operate, 0, unroll=unroll)

    def gather(step, totals):
        strip = counted(step)
        rows = strip_rows(strip)
        result = list(totals)
        for start in range(0, breadth, LANES):
            lanes = slice(start, start + LANES)
            bases = [kept[i, rows, lanes] for i in range(KEPT)]
            for i in range(ITERS + 1):
                for j in range(ITERS):
                    result[i * ITERS + j] += bases[i] * bases[ITERS + 1 + j]
        return tuple(result)

    return gather


def tile_kernel(*refs):
    own, columns, kept, sums, coef = refs[0:6], refs[6], refs[7], refs[8], refs[9]
    strips = kept.shape[1] // STRIP

    def load(which, strip):
        rows = strip_rows(strip)
        return jnp.concatenate(
            [field(own, which, rows), columns[which, rows, :]], axis=1
        )

    gather = krylov(load, strips, lambda step: step + 1, 16, coef, kept)
    zero = jnp.zeros((STRIP, LANES), jnp.float32)
    totals = lax.fori_loop(0, strips - 2, gather, (zero,) * PRODUCTS, unroll=2)
    for index in range(PRODUCTS):
        sums[index] = totals[index]


def edge_kernel(*refs):
    first, last = refs[0:6], refs[6:12]
    columns_first, columns_last, low, high, corners, sums = refs[12:18]
    kept, gram = refs[18:20]
    joined, coef = refs[20:22]
    breadth = low.shape[1]
    width = breadth + LANES
    rows = kept.shape[1]
    everything = slice(0, EDGE)
    place_low, place_high = 0, PACKED
    for which in range(FIELDS):
        joined[which, 0:STRIP, :] = jnp.zeros((STRIP, width), jnp.float32)
        count = LOW_ROWS[which]
        target = slice(STRIP - count, STRIP)
        joined[which, target, 0:breadth] = low[place_low : place_low + count, :]
        joined[which, target, breadth:width] = corners[place_low : place_low + count, :]
        place_low += count
        target = slice(STRIP, STRIP + EDGE)
        joined[which, target, 0:breadth] = field(first, which, everything)
        joined[which, target, breadth:width] = columns_first[which]
        target = slice(STRIP + EDGE, STRIP + 2 * EDGE)
        joined[which, target, 0:breadth] = field(last, which, everything)
        joined[which, target, breadth:width] = columns_last[which]
        joined[which, rows - STRIP : rows, :] = jnp.zeros((STRIP, width), jnp.float32)
        count = HIGH_ROWS[which]
        target = slice(rows - STRIP, rows - STRIP + count)
        joined[which, target, 0:breadth] = high[
            place_high - PACKED : place_high - PACKED + count, :
        ]
        joined[which, target, breadth:width] = corners[place_high : place_high + count, :]
        place_high += count

    def load(which, strip):
        return joined[which, strip_rows(strip), :]

    gather = krylov(load, rows // STRIP, lambda step: 1 + 3 * step, 6, coef, kept)
    totals = lax.fori_loop(0, 2, gather, tuple(sums[i] for i in range(PRODUCTS)), unroll=2)
    gram[...] = jnp.zeros(gram.shape, jnp.float32)
    for index in range(PRODUCTS):
        total = jnp.sum(jnp.sum(totals[index], axis=0, keepdims=True), axis=1, keepdims=True)
        gram[index : index + 1, :] = jnp.broadcast_to(total, (1, LANES))


def recurrences(gram):
    shift, scale = SHIFT, SCALE
    residual = [1.0]
    direction = []
    steps = [0.0] * ITERS
    rz_before = None
    for order in range(ITERS):
        rz = None
        for i in range(order + 1):
            inner = None
            for j in range(order + 1):
                term = residual[j] * gram[i][j]
                inner = term if inner is None else inner + term
            inner = residual[i] * inner
            rz = inner if rz is None else rz + inner
        if order == 0:
            direction = [1.0]
        else:
            ratio = rz / rz_before
            direction = [
                residual[i] + ratio * direction[i] if i < order else residual[i]
                for i in range(order + 1)
            ]
        image = [0.0] * (order + 2)
        for i in range(order + 1):
            image[i] = image[i] + shift * direction[i]
            image[i + 1] = image[i + 1] + scale * direction[i]
        curvature = None
        for i in range(order + 2):
            inner = None
            for j in range(order + 1):
                term = direction[j] * gram[i][j]
                inner = term if inner is None else inner + term
            inner = image[i] * inner
            curvature = inner if curvature is None else curvature + inner
        step = rz / curvature
        for i in range(order + 1):
            steps[i] = steps[i] + step * direction[i]
        residual = [
            (residual[i] if i < order + 1 else 0.0) - step * image[i]
            for i in range(order + 2)
        ]
        rz_before = rz
    return steps, residual


def combine_kernel(gram_ref, kept, edges, solution_ref, residual_ref):
    height, breadth = solution_ref.shape
    gram = [
        [gram_ref[i * ITERS + j : i * ITERS + j + 1, :] for j in range(ITERS)]
        for i in range(ITERS + 1)
    ]
    steps, residual = recurrences(gram)

    def wide(value):
        value = jnp.broadcast_to(value, (STRIP, LANES))
        return jnp.concatenate([value] * (breadth // LANES), axis=1)

    def put(source, rows_from, rows_to):
        total = None
        for j in range(ITERS):
            term = wide(steps[j]) * source[ITERS + 1 + j, rows_from, 0:breadth]
            total = term if total is None else total + term
        solution_ref[rows_to, :] = total
        total = None
        for i in range(ITERS + 1):
            term = wide(residual[i]) * source[i, rows_from, 0:breadth]
            total = term if total is None else total + term
        residual_ref[rows_to, :] = total

    put(edges, slice(STRIP, 2 * STRIP), slice(0, STRIP))
    put(edges, slice(4 * STRIP, 5 * STRIP), slice(height - STRIP, height))

    def middle(strip, carried):
        rows = strip_rows(strip)
        put(kept, rows, rows)
        return carried

    lax.fori_loop(1, height // STRIP - 1, middle, 0)


def params(limit=VMEM_BYTES):
    return pltpu.CompilerParams(vmem_limit_bytes=limit)


def cost(flops, moved):
    return pl.CostEstimate(flops=flops, bytes_accessed=moved, transcendentals=0)


def blocks(shapes, rows, columns, at):
    specs = []
    for shape in shapes:
        lead = tuple(shape[:-2])
        block = lead + (rows, columns)
        index = (0,) * len(lead) + at
        specs.append(pl.BlockSpec(block, lambda step, index=index: index))
    return specs


def whole(*shapes):
    return [pl.BlockSpec(shape, lambda step, n=len(shape): (0,) * n) for shape in shapes]


def body(right_side, faces, ratio, centre, offdiag, mask):
    height, breadth = right_side.shape
    width = breadth + LANES
    args = (right_side, mask, centre, ratio, faces, offdiag)
    shapes = [a.shape for a in args]
    f32 = jnp.float32
    side = lax.axis_index("gx")
    gy = lax.axis_size("gy")
    forward = [(i, i + 1) for i in range(gy - 1)]
    backward = [(b, a) for a, b in forward]
    swap = [(0, 1), (1, 0)]

    packed = jax.ShapeDtypeStruct((PACKED, breadth), f32)
    up, down = pl.pallas_call(
        pack_rows_kernel,
        grid=(1,),
        in_specs=blocks(shapes, STRIP, breadth, (0, 0))
        + blocks(shapes, STRIP, breadth, (height // STRIP - 1, 0)),
        out_specs=whole(packed.shape, packed.shape),
        out_shape=(packed, packed),
        compiler_params=params(PACK_VMEM_BYTES),
        cost_estimate=cost(0, 2 * 4 * PACKED * breadth * 2),
        name="pack_rows",
    )(*args, *args)
    low = lax.ppermute(up, "gy", forward)
    high = lax.ppermute(down, "gy", backward)

    columns = jax.ShapeDtypeStruct((FIELDS, height, LANES), f32)
    columns = pl.pallas_call(
        pack_columns_kernel,
        grid=(1,),
        in_specs=blocks(shapes, height, LANES, (0, 0))
        + blocks(shapes, height, LANES, (0, breadth // LANES - 1))
        + [pl.BlockSpec(memory_space=pl.ANY)],
        out_specs=whole(columns.shape)[0],
        out_shape=columns,
        compiler_params=params(PACK_VMEM_BYTES),
        cost_estimate=cost(0, 3 * 4 * FIELDS * height * LANES),
        name="pack_columns",
    )(*args, *args, up)
    columns = lax.ppermute(columns, "gx", swap)

    cells = height * width
    kept, sums = pl.pallas_call(
        tile_kernel,
        grid=(1,),
        in_specs=whole(*shapes, columns.shape),
        out_specs=whole((KEPT, height, width), (PRODUCTS, STRIP, LANES)),
        out_shape=(
            jax.ShapeDtypeStruct((KEPT, height, width), f32),
            jax.ShapeDtypeStruct((PRODUCTS, STRIP, LANES), f32),
        ),
        scratch_shapes=[pltpu.VMEM((15, height, width), f32)],
        compiler_params=params(),
        cost_estimate=cost(100000 * cells, 4 * cells * (FIELDS + KEPT)),
        name="tile",
    )(*args, columns)

    sums, low, high = lax.optimization_barrier((sums, low, high))
    corners = jnp.concatenate(
        [facing(r[:, :LANES], r[:, breadth - LANES :], side) for r in (low, high)], axis=0
    )
    corners = lax.ppermute(corners, "gx", swap)

    rows = 2 * (STRIP + EDGE)
    edges, gram = pl.pallas_call(
        edge_kernel,
        grid=(1,),
        in_specs=blocks(shapes, EDGE, breadth, (0, 0))
        + blocks(shapes, EDGE, breadth, (height // EDGE - 1, 0))
        + blocks([columns.shape], EDGE, LANES, (0, 0))
        + blocks([columns.shape], EDGE, LANES, (height // EDGE - 1, 0))
        + whole(low.shape, high.shape, corners.shape, sums.shape),
        out_specs=whole((KEPT, rows, width), (2 * STRIP, LANES)),
        out_shape=(
            jax.ShapeDtypeStruct((KEPT, rows, width), f32),
            jax.ShapeDtypeStruct((2 * STRIP, LANES), f32),
        ),
        scratch_shapes=[
            pltpu.VMEM((FIELDS, rows, width), f32),
            pltpu.VMEM((15, rows, width), f32),
        ],
        compiler_params=params(),
        cost_estimate=cost(100 * rows * width, 4 * rows * width * (FIELDS + KEPT)),
        name="edge",
    )(*args, *args, columns, columns, low, high, corners, sums)

    gram = gram + lax.ppermute(gram, "gx", swap)
    reach = 1
    while reach < gy:
        gram = gram + lax.ppermute(gram, "gy", [(i, i ^ reach) for i in range(gy)])
        reach *= 2

    tile = jax.ShapeDtypeStruct((height, breadth), f32)
    return pl.pallas_call(
        combine_kernel,
        grid=(1,),
        in_specs=whole(gram.shape, kept.shape, edges.shape),
        out_specs=whole(tile.shape, tile.shape),
        out_shape=(tile, tile),
        compiler_params=params(),
        cost_estimate=cost(14 * height * breadth, 4 * height * breadth * (KEPT + 2)),
        name="combine",
    )(gram, kept, edges)


def solution(mesh):
    return jax.shard_map(
        body,
        mesh=mesh,
        in_specs=(
            P(("members", "gy"), "gx"),
            P(None, "gy", "gx"),
            P("gy", "gx"),
            P("gy", "gx"),
            P(None, "gy", "gx"),
            P("gy", "gx"),
        ),
        out_specs=(P(("members", "gy"), "gx"), P(("members", "gy"), "gx")),
        check_vma=False,
    )
```

```python
import functools

import jax
import jax.numpy as jnp
from jax import lax
from jax.experimental import pallas as pl
from jax.experimental.pallas import tpu as pltpu
from jax.sharding import PartitionSpec as P

ITERS = 3
SHIFT = 1.0
SCALE = 4.0
LANES = 128
STRIP = 8

neighbour_steps = [(-1, -1), (-1, 0), (-1, 1), (0, -1), (0, 1), (1, -1), (1, 0), (1, 1)]

FIELDS = 6 + len(neighbour_steps)
REACH = 2 * ITERS
LOW_ROWS = [REACH, REACH - 1, REACH - 1, REACH - 2, REACH - 2, REACH - 2] + [
    REACH - 1 + down for down, _ in neighbour_steps
]
HIGH_ROWS = [REACH, REACH - 1, REACH - 1, REACH - 2, REACH - 2, REACH - 1] + [
    REACH - 1 - down for down, _ in neighbour_steps
]
PACKED = -(-max(sum(LOW_ROWS), sum(HIGH_ROWS)) // STRIP) * STRIP
PRODUCTS = (ITERS + 1) * ITERS
KEPT = 2 * ITERS + 1
SLOT = 8
COEFFICIENTS = 15
NEAR = 2 * COEFFICIENTS
SOUTH = NEAR + 6
FIRST = SOUTH + 1
BASIS = FIRST + 2
HANDED = BASIS + 2 * KEPT
TILE_VMEM_BYTES = 40 * 1024 * 1024
VMEM_BYTES = 32 * 1024 * 1024
PACK_VMEM_BYTES = 62 * 1024 * 1024


def field(refs, which, rows):
    right_side, mask, centre, ratio, faces, offdiag = refs
    if which == 0:
        return mask[rows, :].astype(jnp.float32) * right_side[rows, :]
    if which == 1:
        return mask[rows, :].astype(jnp.float32)
    if which == 2:
        return centre[rows, :]
    if which == 3:
        return ratio[rows, :]
    if which < 6:
        return faces[which - 4, rows, :]
    return offdiag[which - 6, rows, :]


def trimmed(out, refs, counts, at_end):
    place = 0
    for which, count in enumerate(counts):
        rows = slice(STRIP - count, STRIP) if at_end else slice(0, count)
        out[place : place + count, :] = field(refs, which, rows)
        place += count
    if place < PACKED:
        out[place:PACKED, :] = jnp.zeros((PACKED - place, out.shape[1]), jnp.float32)


def lanes_of(shape):
    return lax.broadcasted_iota(jnp.int32, shape, len(shape) - 1)


def squeezed(near, side):
    start = jnp.where(side == 0, SLOT, 0)
    total = None
    for which in range(FIELDS):
        block = pltpu.roll(near(which), start + SLOT * which, 1)
        if total is None:
            lane = lanes_of(block.shape)
            total = jnp.zeros(block.shape, jnp.float32)
        inside = (lane >= SLOT * which) & (lane < SLOT * (which + 1))
        total = jnp.where(inside, block, total)
    return total


def spread(block, side):
    lane = lanes_of(block.shape)
    start = jnp.where(side == 0, LANES, LANES - SLOT)
    first = jnp.where(side == 0, 0, LANES - SLOT)
    inside = ((lane >= first) & (lane < first + SLOT)).astype(jnp.float32)
    return [
        pltpu.roll(block, start - SLOT * which, 1) * inside for which in range(FIELDS)
    ]


def pack_kernel(*refs):
    args = refs[0:6]
    even, odd, even_corner, odd_corner, columns = refs[6:11]
    ends, sides, end_arrived, side_arrived = refs[11:17], refs[17:23], refs[23], refs[24]
    height, breadth = args[0].shape
    side = lax.axis_index("gx")
    parity = lax.rem(lax.axis_index("gy"), 2)
    beside = pl.multiple_of(jnp.where(side == 0, breadth - LANES, 0), LANES)
    copies, more = [], []
    for index, (arg, end, edge) in enumerate(zip(args, ends, sides)):
        lead = (slice(None),) * (len(arg.shape) - 2)
        for which, start in enumerate((0, height - STRIP)):
            copies.append(
                pltpu.make_async_copy(
                    arg.at[lead + (pl.ds(start, STRIP), slice(None))],
                    end.at[which],
                    end_arrived.at[index, which],
                )
            )
        more.append(
            pltpu.make_async_copy(
                arg.at[lead + (slice(None), pl.ds(beside, LANES))],
                edge,
                side_arrived.at[index],
            )
        )
    for copy in copies + more:
        copy.start()
    for copy in copies:
        copy.wait()
    first = [end.at[0] for end in ends]
    last = [end.at[1] for end in ends]

    @pl.when(parity == 0)
    def _():
        trimmed(even, last, LOW_ROWS, True)
        trimmed(odd, first, HIGH_ROWS, False)

    @pl.when(parity != 0)
    def _():
        trimmed(even, first, HIGH_ROWS, False)
        trimmed(odd, last, LOW_ROWS, True)

    for copy in more:
        copy.wait()
    packed = squeezed(lambda which: field(sides, which, slice(None)), side)
    columns[...] = packed
    corner_first, corner_last = packed[0:STRIP, :], packed[height - STRIP : height, :]
    even_corner[...] = jnp.where(parity == 0, corner_last, corner_first)
    odd_corner[...] = jnp.where(parity == 0, corner_first, corner_last)


def row_above(block, before):
    row = lax.broadcasted_iota(jnp.int32, block.shape, 0)
    return jnp.where(row == 0, pltpu.roll(before, 1, 0), pltpu.roll(block, 1, 0))


def row_below(block, after):
    row = lax.broadcasted_iota(jnp.int32, block.shape, 0)
    last = STRIP - 1
    return jnp.where(row == last, pltpu.roll(after, last, 0), pltpu.roll(block, last, 0))


def strip_rows(strip):
    return pl.ds(pl.multiple_of(strip * STRIP, STRIP), STRIP)


def west_of(block):
    return pltpu.roll(block, 1, 1)


def east_of(block):
    return pltpu.roll(block, block.shape[1] - 1, 1)


def coefficients(get, south_after):
    result = [None] * COEFFICIENTS
    wet = get(1)
    result[4] = get(2)
    for index, (down, across) in enumerate(neighbour_steps):
        weight = get(6 + index)
        if across == 1:
            weight = west_of(weight)
        elif across == -1:
            weight = east_of(weight)
        result[(down + 1) * 3 + across + 1] = weight
    west = get(4)
    south = get(5)
    east = east_of(west)
    north = row_below(south, south_after)
    scaled = wet * (1.0 / SCALE)
    result[9] = wet
    result[10] = scaled * (west + east + south + north + get(3))
    result[11] = scaled * west
    result[12] = scaled * east
    result[13] = scaled * south
    result[14] = scaled * north
    return result, south


def weighted(get, block, downs=(0, 1, 2)):
    left, right = east_of(block), west_of(block)
    return [
        get(down * 3) * left + get(down * 3 + 1) * block + get(down * 3 + 2) * right
        for down in downs
    ]


def applied(get, block, before, after, old):
    return (
        get(10) * block
        - get(11) * west_of(block)
        - get(12) * east_of(block)
        - get(13) * row_above(block, before)
        - get(14) * row_below(block, after)
        - (SHIFT / SCALE) * old
    )


def gathered(totals, kept, rows, breadth):
    result = list(totals)
    for start in range(0, breadth, LANES):
        bases = [kept[i, rows, start : start + LANES] for i in range(KEPT)]
        for i in range(ITERS + 1):
            for j in range(ITERS):
                result[i * ITERS + j] += bases[i] * bases[ITERS + 1 + j]
    return tuple(result)


def krylov(load, strips, coef, kept, arrive):
    width = kept.shape[2]
    zero = jnp.zeros((STRIP, width), jnp.float32)

    def prepare(step, south_after):
        strip = strips - 1 - step
        rows = strip_rows(strip)
        kept[0, rows, :] = load(0, strip)
        values, south = coefficients(lambda which: load(which, strip), south_after)
        for index, value in enumerate(values):
            coef[index, rows, :] = value
        return south

    south = zero
    half = strips // 2
    for start in (0, half):
        arrive(start)
        south = lax.fori_loop(start, start + half, prepare, south, unroll=half)

    for order in range(ITERS):
        smoothed = ITERS + 1 + order

        def smooth(strip, carried):
            above, partial = carried
            rows = strip_rows(strip)
            totals = weighted(lambda k: coef[k, rows, :], kept[order, rows, :])
            row = lax.broadcasted_iota(jnp.int32, totals[0].shape, 0)
            rising = pltpu.roll(totals[0], STRIP - 1, 0)
            falling = pltpu.roll(totals[2], 1, 0)
            done = strip_rows(jnp.maximum(strip - 1, 0))
            kept[smoothed, done, :] = coef[9, done, :] * (
                partial + jnp.where(row == STRIP - 1, rising, 0.0)
            )
            partial = (
                totals[1]
                + jnp.where(row == 0, above, falling)
                + jnp.where(row == STRIP - 1, 0.0, rising)
            )
            return falling, partial

        _, partial = lax.fori_loop(0, strips, smooth, (zero, zero), unroll=strips)
        done = slice((strips - 1) * STRIP, strips * STRIP)
        kept[smoothed, done, :] = coef[9, done, :] * partial

        def operate(strip, carried):
            rows = strip_rows(strip)
            kept[order + 1, rows, :] = applied(
                lambda k: coef[k, rows, :],
                kept[smoothed, rows, :],
                kept[smoothed, strip_rows(jnp.maximum(strip - 1, 0)), :],
                kept[smoothed, strip_rows(jnp.minimum(strip + 1, strips - 1)), :],
                kept[order, rows, :],
            )
            return carried

        lax.fori_loop(0, strips, operate, 0, unroll=strips)


def tile_kernel(*refs):
    args, columns, kept, sums, handed, coef, wide = refs[0:6], *refs[6:12]
    own, arrived = refs[12:18], refs[18]
    strips = kept.shape[1] // STRIP
    half = strips // 2 * STRIP
    side = lax.axis_index("gx")
    copies = []
    for part in (1, 0):
        rows = pl.ds(part * half, half)
        for index, (arg, buffer) in enumerate(zip(args, own)):
            place = (slice(None),) * (len(arg.shape) - 2) + (rows, slice(None))
            copies.append(
                pltpu.make_async_copy(
                    arg.at[place], buffer.at[place], arrived.at[index, part]
                )
            )
    for copy in copies:
        copy.start()

    def arrive(start):
        for copy in copies[:6] if start == 0 else copies[6:]:
            copy.wait()

    for which, block in enumerate(spread(columns[...], side)):
        wide[which] = block

    def load(which, strip):
        rows = strip_rows(strip)
        return jnp.concatenate([field(own, which, rows), wide[which, rows, :]], axis=1)

    krylov(load, strips, coef, kept, arrive)
    zero = jnp.zeros((STRIP, LANES), jnp.float32)
    breadth = kept.shape[2] - LANES
    totals = lax.fori_loop(
        1,
        strips - 1,
        lambda strip, totals: gathered(totals, kept, strip_rows(strip), breadth),
        (zero,) * PRODUCTS,
        unroll=2,
    )
    for index in range(PRODUCTS):
        sums[index] = totals[index]
    first, last = slice(0, STRIP), slice((strips - 1) * STRIP, strips * STRIP)
    second, third = slice(STRIP, 2 * STRIP), slice((strips - 2) * STRIP, (strips - 1) * STRIP)
    for index in range(COEFFICIENTS):
        handed[index] = coef[index, first, :]
        handed[COEFFICIENTS + index] = coef[index, last, :]
    for index in range(3):
        handed[NEAR + index] = coef[index, second, :]
        handed[NEAR + 3 + index] = coef[6 + index, third, :]
    handed[SOUTH] = load(5, 0)
    handed[FIRST] = kept[0, first, :]
    handed[FIRST + 1] = kept[0, last, :]
    for index in range(KEPT):
        handed[BASIS + index] = kept[index, second, :]
        handed[BASIS + KEPT + index] = kept[index, third, :]


def edge_kernel(
    handed, even, odd, even_corner, odd_corner, sums, kept, gram, joined, coef, outer
):
    breadth = even.shape[1]
    width = breadth + LANES
    side = lax.axis_index("gx")
    parity = lax.rem(lax.axis_index("gy"), 2)
    low_corner = spread(jnp.where(parity == 0, odd_corner[...], even_corner[...]), side)
    high_corner = spread(jnp.where(parity == 0, even_corner[...], odd_corner[...]), side)
    low_rows, high_rows = slice(0, STRIP), slice(STRIP, 2 * STRIP)
    place_low, place_high = 0, 0
    for which in range(FIELDS):
        joined[which, :, 0:breadth] = jnp.zeros((2 * STRIP, breadth), jnp.float32)
        joined[which, low_rows, breadth:width] = low_corner[which]
        joined[which, high_rows, breadth:width] = high_corner[which]
        count = LOW_ROWS[which]
        place = slice(place_low, place_low + count)
        joined[which, STRIP - count : STRIP, 0:breadth] = jnp.where(
            parity == 0, odd[place, :], even[place, :]
        )
        place_low += count
        count = HIGH_ROWS[which]
        place = slice(place_high, place_high + count)
        joined[which, STRIP : STRIP + count, 0:breadth] = jnp.where(
            parity == 0, even[place, :], odd[place, :]
        )
        place_high += count

    zero = jnp.zeros((STRIP, width), jnp.float32)
    values, _ = coefficients(lambda which: joined[which, low_rows, :], handed[SOUTH])
    for index, value in enumerate(values):
        coef[index, low_rows, :] = value
    values, south = coefficients(lambda which: joined[which, high_rows, :], zero)
    for index, value in enumerate(values):
        coef[index, high_rows, :] = value
    row = lax.broadcasted_iota(jnp.int32, zero.shape, 0)
    missing = (
        handed[COEFFICIENTS + 9]
        * (1.0 / SCALE)
        * jnp.where(row == STRIP - 1, pltpu.roll(south, STRIP - 1, 0), 0.0)
    )

    def getter(strip):
        if strip == 0:
            return lambda k: coef[k, low_rows, :]
        if strip == 3:
            return lambda k: coef[k, high_rows, :]
        if strip == 1:
            return lambda k: handed[k]
        return lambda k: handed[COEFFICIENTS + k] + (missing if k in (10, 14) else 0.0)

    getters = [getter(strip) for strip in range(4)]
    inner = [slice(0, STRIP), slice(STRIP, 2 * STRIP)]

    def write(index, strip, value):
        if strip in (1, 2):
            kept[index, inner[strip - 1], :] = value
        else:
            outer[index, low_rows if strip == 0 else high_rows, :] = value

    def read(index, strip):
        if strip in (1, 2):
            return kept[index, inner[strip - 1], :]
        return outer[index, low_rows if strip == 0 else high_rows, :]

    write(0, 0, joined[0, low_rows, :])
    write(0, 3, joined[0, high_rows, :])
    write(0, 1, handed[FIRST])
    write(0, 2, handed[FIRST + 1])
    for order in range(ITERS):
        smoothed = ITERS + 1 + order
        totals = [weighted(getters[strip], read(order, strip)) for strip in range(4)]
        rising = weighted(lambda k: handed[NEAR + k], handed[BASIS + order], (0,))[0]
        falling = weighted(
            lambda k: handed[NEAR + 3 + k], handed[BASIS + KEPT + order], (0,)
        )[0]
        above = [zero, totals[0][2], falling, totals[2][2]]
        below = [totals[1][0], rising, totals[3][0], zero]
        for strip in range(4):
            write(
                smoothed,
                strip,
                getters[strip](9)
                * (
                    totals[strip][1]
                    + row_above(totals[strip][2], above[strip])
                    + row_below(totals[strip][0], below[strip])
                ),
            )
        blocks = [read(smoothed, strip) for strip in range(4)]
        before = [zero, blocks[0], handed[BASIS + KEPT + smoothed], blocks[2]]
        after = [blocks[1], handed[BASIS + smoothed], blocks[3], zero]
        for strip in range(4) if order < ITERS - 1 else (1, 2):
            write(
                order + 1,
                strip,
                applied(
                    getters[strip],
                    blocks[strip],
                    before[strip],
                    after[strip],
                    read(order, strip),
                ),
            )
    totals = tuple(sums[i] for i in range(PRODUCTS))
    for rows in inner:
        totals = gathered(totals, kept, rows, breadth)
    gram[...] = jnp.zeros(gram.shape, jnp.float32)
    for index in range(PRODUCTS):
        total = jnp.sum(jnp.sum(totals[index], axis=0, keepdims=True), axis=1, keepdims=True)
        gram[index : index + 1, :] = jnp.broadcast_to(total, (1, LANES))


def recurrences(gram):
    shift, scale = SHIFT, SCALE
    residual = [1.0]
    direction = []
    steps = [0.0] * ITERS
    rz_before = None
    for order in range(ITERS):
        rz = None
        for i in range(order + 1):
            inner = None
            for j in range(order + 1):
                term = residual[j] * gram[i][j]
                inner = term if inner is None else inner + term
            inner = residual[i] * inner
            rz = inner if rz is None else rz + inner
        if order == 0:
            direction = [1.0]
        else:
            ratio = rz / rz_before
            direction = [
                residual[i] + ratio * direction[i] if i < order else residual[i]
                for i in range(order + 1)
            ]
        image = [0.0] * (order + 2)
        for i in range(order + 1):
            image[i] = image[i] + shift * direction[i]
            image[i + 1] = image[i + 1] + scale * direction[i]
        curvature = None
        for i in range(order + 2):
            inner = None
            for j in range(order + 1):
                term = direction[j] * gram[i][j]
                inner = term if inner is None else inner + term
            inner = image[i] * inner
            curvature = inner if curvature is None else curvature + inner
        step = rz / curvature
        for i in range(order + 1):
            steps[i] = steps[i] + step * direction[i]
        residual = [
            (residual[i] if i < order + 1 else 0.0) - step * image[i]
            for i in range(order + 2)
        ]
        rz_before = rz
    return steps, residual


def combine_kernel(gram_ref, kept, edges, solution_ref, residual_ref):
    height, breadth = solution_ref.shape
    gram = [
        [gram_ref[i * ITERS + j : i * ITERS + j + 1, :] for j in range(ITERS)]
        for i in range(ITERS + 1)
    ]
    steps, residual = recurrences(gram)

    def wide(value):
        value = jnp.broadcast_to(value, (STRIP, LANES))
        return jnp.concatenate([value] * (breadth // LANES), axis=1)

    def put(source, rows_from, rows_to):
        total = None
        for j in range(ITERS):
            term = wide(steps[j]) * source[ITERS + 1 + j, rows_from, 0:breadth]
            total = term if total is None else total + term
        solution_ref[rows_to, :] = total
        total = None
        for i in range(ITERS + 1):
            term = wide(residual[i]) * source[i, rows_from, 0:breadth]
            total = term if total is None else total + term
        residual_ref[rows_to, :] = total

    put(edges, slice(0, STRIP), slice(0, STRIP))
    put(edges, slice(STRIP, 2 * STRIP), slice(height - STRIP, height))

    def middle(strip, carried):
        rows = strip_rows(strip)
        put(kept, rows, rows)
        return carried

    lax.fori_loop(1, height // STRIP - 1, middle, 0)


def params(limit=VMEM_BYTES):
    return pltpu.CompilerParams(vmem_limit_bytes=limit)


def cost(flops, moved):
    return pl.CostEstimate(flops=flops, bytes_accessed=moved, transcendentals=0)


def whole(*shapes):
    return [pl.BlockSpec(shape, lambda step, n=len(shape): (0,) * n) for shape in shapes]


def body(right_side, faces, ratio, centre, offdiag, mask):
    height, breadth = right_side.shape
    width = breadth + LANES
    args = (right_side, mask, centre, ratio, faces, offdiag)
    f32 = jnp.float32
    gy = lax.axis_size("gy")
    swap = [(0, 1), (1, 0)]
    pairs = [(i, i ^ 1) for i in range(gy) if i ^ 1 < gy]
    between = [(i, (i + 1 ^ 1) - 1) for i in range(1, gy) if (i + 1 ^ 1) - 1 < gy]

    def diagonal(partners):
        return [(2 * a + c, 2 * b + 1 - c) for a, b in partners for c in (0, 1)]

    packed = jax.ShapeDtypeStruct((PACKED, breadth), f32)
    corner = jax.ShapeDtypeStruct((STRIP, LANES), f32)
    columns = jax.ShapeDtypeStruct((height, LANES), f32)
    even, odd, even_corner, odd_corner, columns = pl.pallas_call(
        pack_kernel,
        in_specs=[pl.BlockSpec(memory_space=pltpu.HBM)] * len(args),
        out_shape=(packed, packed, corner, corner, columns),
        scratch_shapes=[
            pltpu.VMEM((2,) + a.shape[:-2] + (STRIP, breadth), a.dtype) for a in args
        ]
        + [pltpu.VMEM(a.shape[:-1] + (LANES,), a.dtype) for a in args]
        + [
            pltpu.SemaphoreType.DMA((len(args), 2)),
            pltpu.SemaphoreType.DMA((len(args),)),
        ],
        compiler_params=params(PACK_VMEM_BYTES),
        cost_estimate=cost(0, 4 * 4 * PACKED * breadth),
        name="pack",
    )(*args)
    columns = lax.ppermute(columns, "gx", swap)
    even_in = lax.ppermute(even, "gy", pairs)
    even_corner = lax.ppermute(even_corner, ("gy", "gx"), diagonal(pairs))
    odd_in = lax.ppermute(odd, "gy", between)
    odd_corner = lax.ppermute(odd_corner, ("gy", "gx"), diagonal(between))

    cells = height * width
    kept, sums, handed = pl.pallas_call(
        tile_kernel,
        in_specs=[pl.BlockSpec(memory_space=pltpu.HBM)] * len(args)
        + [pl.BlockSpec(memory_space=pltpu.VMEM)],
        out_shape=(
            jax.ShapeDtypeStruct((KEPT, height, width), f32),
            jax.ShapeDtypeStruct((PRODUCTS, STRIP, LANES), f32),
            jax.ShapeDtypeStruct((HANDED, STRIP, width), f32),
        ),
        scratch_shapes=[
            pltpu.VMEM((COEFFICIENTS, height, width), f32),
            pltpu.VMEM((FIELDS, height, LANES), f32),
        ]
        + [pltpu.VMEM(a.shape, a.dtype) for a in args]
        + [pltpu.SemaphoreType.DMA((len(args), 2))],
        compiler_params=params(TILE_VMEM_BYTES),
        cost_estimate=cost(100 * cells, 4 * cells * (FIELDS + KEPT)),
        name="tile",
    )(*args, columns)

    sums, even_in, odd_in, even_corner, odd_corner = lax.optimization_barrier(
        (sums, even_in, odd_in, even_corner, odd_corner)
    )
    rows = 2 * STRIP
    edges, gram = pl.pallas_call(
        edge_kernel,
        out_shape=(
            jax.ShapeDtypeStruct((KEPT, rows, width), f32),
            jax.ShapeDtypeStruct((2 * STRIP, LANES), f32),
        ),
        scratch_shapes=[
            pltpu.VMEM((FIELDS, rows, width), f32),
            pltpu.VMEM((COEFFICIENTS, rows, width), f32),
            pltpu.VMEM((KEPT, rows, width), f32),
        ],
        compiler_params=params(),
        cost_estimate=cost(200 * rows * width, 4 * rows * width * (FIELDS + KEPT)),
        name="edge",
    )(handed, even_in, odd_in, even_corner, odd_corner, sums)

    gram = gram + lax.ppermute(gram, "gx", swap)
    reach = 1
    while reach < gy:
        gram = gram + lax.ppermute(gram, "gy", [(i, i ^ reach) for i in range(gy)])
        reach *= 2

    tile = jax.ShapeDtypeStruct((height, breadth), f32)
    return pl.pallas_call(
        combine_kernel,
        grid=(1,),
        in_specs=whole(gram.shape, kept.shape, edges.shape),
        out_specs=whole(tile.shape, tile.shape),
        out_shape=(tile, tile),
        compiler_params=params(),
        cost_estimate=cost(14 * height * breadth, 4 * height * breadth * (KEPT + 2)),
        name="combine",
    )(gram, kept, edges)


def solution(mesh):
    return jax.shard_map(
        body,
        mesh=mesh,
        in_specs=(
            P(("members", "gy"), "gx"),
            P(None, "gy", "gx"),
            P("gy", "gx"),
            P("gy", "gx"),
            P(None, "gy", "gx"),
            P("gy", "gx"),
        ),
        out_specs=(P(("members", "gy"), "gx"), P(("members", "gy"), "gx")),
        check_vma=False,
    )
```

```python
import functools

import jax
import jax.numpy as jnp
from jax import lax
from jax.experimental import pallas as pl
from jax.experimental.pallas import tpu as pltpu
from jax.sharding import PartitionSpec as P

ITERS = 3
SHIFT = 1.0
SCALE = 4.0
LANES = 128
STRIP = 8

neighbour_steps = [(-1, -1), (-1, 0), (-1, 1), (0, -1), (0, 1), (1, -1), (1, 0), (1, 1)]

FIELDS = 6 + len(neighbour_steps)
REACH = 2 * ITERS
LOW_ROWS = [REACH, REACH - 1, REACH - 1, REACH - 2, REACH - 2, REACH - 2] + [
    REACH - 1 + down for down, _ in neighbour_steps
]
HIGH_ROWS = [REACH, REACH - 1, REACH - 1, REACH - 2, REACH - 2, REACH - 1] + [
    REACH - 1 - down for down, _ in neighbour_steps
]
PACKED = -(-max(sum(LOW_ROWS), sum(HIGH_ROWS)) // STRIP) * STRIP
PRODUCTS = (ITERS + 1) * ITERS
KEPT = 2 * ITERS + 1
SLOT = 8
COEFFICIENTS = 15
NEAR = 2 * COEFFICIENTS
SOUTH = NEAR + 6
FIRST = SOUTH + 1
BASIS = FIRST + 2
HANDED = BASIS + 2 * KEPT
TILE_VMEM_BYTES = 40 * 1024 * 1024
VMEM_BYTES = 32 * 1024 * 1024
PACK_VMEM_BYTES = 16 * 1024 * 1024


def field(refs, which, rows):
    right_side, mask, centre, ratio, faces, offdiag = refs
    if which == 0:
        return mask[rows, :].astype(jnp.float32) * right_side[rows, :]
    if which == 1:
        return mask[rows, :].astype(jnp.float32)
    if which == 2:
        return centre[rows, :]
    if which == 3:
        return ratio[rows, :]
    if which < 6:
        return faces[which - 4, rows, :]
    return offdiag[which - 6, rows, :]


def trimmed(out, refs, counts, at_end):
    place = 0
    for which, count in enumerate(counts):
        rows = slice(STRIP - count, STRIP) if at_end else slice(0, count)
        out[place : place + count, :] = field(refs, which, rows)
        place += count
    if place < PACKED:
        out[place:PACKED, :] = jnp.zeros((PACKED - place, out.shape[1]), jnp.float32)


def lanes_of(shape):
    return lax.broadcasted_iota(jnp.int32, shape, len(shape) - 1)


def squeezed(near, side):
    start = jnp.where(side == 0, SLOT, 0)
    total = None
    for which in range(FIELDS):
        block = pltpu.roll(near(which), start + SLOT * which, 1)
        if total is None:
            lane = lanes_of(block.shape)
            total = jnp.zeros(block.shape, jnp.float32)
        inside = (lane >= SLOT * which) & (lane < SLOT * (which + 1))
        total = jnp.where(inside, block, total)
    return total


def spread(block, side):
    lane = lanes_of(block.shape)
    start = jnp.where(side == 0, LANES, LANES - SLOT)
    first = jnp.where(side == 0, 0, LANES - SLOT)
    inside = ((lane >= first) & (lane < first + SLOT)).astype(jnp.float32)
    return [
        pltpu.roll(block, start - SLOT * which, 1) * inside for which in range(FIELDS)
    ]


def pack_kernel(*refs):
    args = refs[0:6]
    even, odd, even_corner, odd_corner, columns = refs[6:11]
    ends, sides, end_arrived, side_arrived = refs[11:17], refs[17:23], refs[23], refs[24]
    height, breadth = args[0].shape
    side = lax.axis_index("gx")
    parity = lax.rem(lax.axis_index("gy"), 2)
    beside = pl.multiple_of(jnp.where(side == 0, breadth - LANES, 0), LANES)
    copies, more = [], []
    for index, (arg, end, edge) in enumerate(zip(args, ends, sides)):
        lead = (slice(None),) * (len(arg.shape) - 2)
        for which, start in enumerate((0, height - STRIP)):
            copies.append(
                pltpu.make_async_copy(
                    arg.at[lead + (pl.ds(start, STRIP), slice(None))],
                    end.at[which],
                    end_arrived.at[index, which],
                )
            )
        more.append(
            pltpu.make_async_copy(
                arg.at[lead + (slice(None), pl.ds(beside, LANES))],
                edge,
                side_arrived.at[index],
            )
        )
    for copy in copies + more:
        copy.start()
    for copy in copies:
        copy.wait()
    first = [end.at[0] for end in ends]
    last = [end.at[1] for end in ends]

    @pl.when(parity == 0)
    def _():
        trimmed(even, last, LOW_ROWS, True)
        trimmed(odd, first, HIGH_ROWS, False)

    @pl.when(parity != 0)
    def _():
        trimmed(even, first, HIGH_ROWS, False)
        trimmed(odd, last, LOW_ROWS, True)

    for copy in more:
        copy.wait()
    packed = squeezed(lambda which: field(sides, which, slice(None)), side)
    columns[...] = packed
    corner_first, corner_last = packed[0:STRIP, :], packed[height - STRIP : height, :]
    even_corner[...] = jnp.where(parity == 0, corner_last, corner_first)
    odd_corner[...] = jnp.where(parity == 0, corner_first, corner_last)


def row_above(block, before):
    row = lax.broadcasted_iota(jnp.int32, block.shape, 0)
    return jnp.where(row == 0, pltpu.roll(before, 1, 0), pltpu.roll(block, 1, 0))


def row_below(block, after):
    row = lax.broadcasted_iota(jnp.int32, block.shape, 0)
    last = STRIP - 1
    return jnp.where(row == last, pltpu.roll(after, last, 0), pltpu.roll(block, last, 0))


def strip_rows(strip):
    return pl.ds(pl.multiple_of(strip * STRIP, STRIP), STRIP)


def west_of(block):
    return pltpu.roll(block, 1, 1)


def east_of(block):
    return pltpu.roll(block, block.shape[1] - 1, 1)


def coefficients(get, south_after):
    result = [None] * COEFFICIENTS
    wet = get(1)
    result[4] = get(2)
    for index, (down, across) in enumerate(neighbour_steps):
        weight = get(6 + index)
        if across == 1:
            weight = west_of(weight)
        elif across == -1:
            weight = east_of(weight)
        result[(down + 1) * 3 + across + 1] = weight
    west = get(4)
    south = get(5)
    east = east_of(west)
    north = row_below(south, south_after)
    scaled = wet * (1.0 / SCALE)
    result[9] = wet
    result[10] = scaled * (west + east + south + north + get(3))
    result[11] = scaled * west
    result[12] = scaled * east
    result[13] = scaled * south
    result[14] = scaled * north
    return result, south


def weighted(get, block, downs=(0, 1, 2)):
    left, right = east_of(block), west_of(block)
    return [
        get(down * 3) * left + get(down * 3 + 1) * block + get(down * 3 + 2) * right
        for down in downs
    ]


def applied(get, block, before, after, old):
    return (
        get(10) * block
        - get(11) * west_of(block)
        - get(12) * east_of(block)
        - get(13) * row_above(block, before)
        - get(14) * row_below(block, after)
        - (SHIFT / SCALE) * old
    )


def gathered(totals, kept, rows, breadth):
    result = list(totals)
    for start in range(0, breadth, LANES):
        bases = [kept[i, rows, start : start + LANES] for i in range(KEPT)]
        for i in range(ITERS + 1):
            for j in range(ITERS):
                result[i * ITERS + j] += bases[i] * bases[ITERS + 1 + j]
    return tuple(result)


def krylov(load, strips, coef, kept, arrive):
    width = kept.shape[2]
    zero = jnp.zeros((STRIP, width), jnp.float32)

    def prepare(step, south_after):
        strip = strips - 1 - step
        rows = strip_rows(strip)
        kept[0, rows, :] = load(0, strip)
        values, south = coefficients(lambda which: load(which, strip), south_after)
        for index, value in enumerate(values):
            coef[index, rows, :] = value
        return south

    south = zero
    half = strips // 2
    for start in (0, half):
        arrive(start)
        south = lax.fori_loop(start, start + half, prepare, south, unroll=half)

    for order in range(ITERS):
        smoothed = ITERS + 1 + order

        def smooth(strip, carried):
            above, partial = carried
            rows = strip_rows(strip)
            totals = weighted(lambda k: coef[k, rows, :], kept[order, rows, :])
            row = lax.broadcasted_iota(jnp.int32, totals[0].shape, 0)
            rising = pltpu.roll(totals[0], STRIP - 1, 0)
            falling = pltpu.roll(totals[2], 1, 0)
            done = strip_rows(jnp.maximum(strip - 1, 0))
            kept[smoothed, done, :] = coef[9, done, :] * (
                partial + jnp.where(row == STRIP - 1, rising, 0.0)
            )
            partial = (
                totals[1]
                + jnp.where(row == 0, above, falling)
                + jnp.where(row == STRIP - 1, 0.0, rising)
            )
            return falling, partial

        _, partial = lax.fori_loop(0, strips, smooth, (zero, zero), unroll=strips)
        done = slice((strips - 1) * STRIP, strips * STRIP)
        kept[smoothed, done, :] = coef[9, done, :] * partial

        def operate(strip, carried):
            rows = strip_rows(strip)
            kept[order + 1, rows, :] = applied(
                lambda k: coef[k, rows, :],
                kept[smoothed, rows, :],
                kept[smoothed, strip_rows(jnp.maximum(strip - 1, 0)), :],
                kept[smoothed, strip_rows(jnp.minimum(strip + 1, strips - 1)), :],
                kept[order, rows, :],
            )
            return carried

        lax.fori_loop(0, strips, operate, 0, unroll=strips)


def tile_kernel(*refs):
    args, columns, kept, sums, handed, coef, wide = refs[0:6], *refs[6:12]
    own, arrived = refs[12:18], refs[18]
    strips = kept.shape[1] // STRIP
    half = strips // 2 * STRIP
    side = lax.axis_index("gx")
    copies = []
    for part in (1, 0):
        rows = pl.ds(part * half, half)
        for index, (arg, buffer) in enumerate(zip(args, own)):
            place = (slice(None),) * (len(arg.shape) - 2) + (rows, slice(None))
            copies.append(
                pltpu.make_async_copy(
                    arg.at[place], buffer.at[place], arrived.at[index, part]
                )
            )
    for copy in copies:
        copy.start()

    def arrive(start):
        for copy in copies[:6] if start == 0 else copies[6:]:
            copy.wait()

    for which, block in enumerate(spread(columns[...], side)):
        wide[which] = block

    def load(which, strip):
        rows = strip_rows(strip)
        return jnp.concatenate([field(own, which, rows), wide[which, rows, :]], axis=1)

    krylov(load, strips, coef, kept, arrive)
    zero = jnp.zeros((STRIP, LANES), jnp.float32)
    breadth = kept.shape[2] - LANES
    totals = lax.fori_loop(
        1,
        strips - 1,
        lambda strip, totals: gathered(totals, kept, strip_rows(strip), breadth),
        (zero,) * PRODUCTS,
        unroll=2,
    )
    for index in range(PRODUCTS):
        sums[index] = totals[index]
    first, last = slice(0, STRIP), slice((strips - 1) * STRIP, strips * STRIP)
    second, third = slice(STRIP, 2 * STRIP), slice((strips - 2) * STRIP, (strips - 1) * STRIP)
    for index in range(COEFFICIENTS):
        handed[index] = coef[index, first, :]
        handed[COEFFICIENTS + index] = coef[index, last, :]
    for index in range(3):
        handed[NEAR + index] = coef[index, second, :]
        handed[NEAR + 3 + index] = coef[6 + index, third, :]
    handed[SOUTH] = load(5, 0)
    handed[FIRST] = kept[0, first, :]
    handed[FIRST + 1] = kept[0, last, :]
    for index in range(KEPT):
        handed[BASIS + index] = kept[index, second, :]
        handed[BASIS + KEPT + index] = kept[index, third, :]


def edge_kernel(
    handed, even, odd, even_corner, odd_corner, sums, kept, gram, joined, coef, outer
):
    breadth = even.shape[1]
    width = breadth + LANES
    side = lax.axis_index("gx")
    parity = lax.rem(lax.axis_index("gy"), 2)
    low_corner = spread(jnp.where(parity == 0, odd_corner[...], even_corner[...]), side)
    high_corner = spread(jnp.where(parity == 0, even_corner[...], odd_corner[...]), side)
    low_rows, high_rows = slice(0, STRIP), slice(STRIP, 2 * STRIP)
    place_low, place_high = 0, 0
    for which in range(FIELDS):
        joined[which, :, 0:breadth] = jnp.zeros((2 * STRIP, breadth), jnp.float32)
        joined[which, low_rows, breadth:width] = low_corner[which]
        joined[which, high_rows, breadth:width] = high_corner[which]
        count = LOW_ROWS[which]
        place = slice(place_low, place_low + count)
        joined[which, STRIP - count : STRIP, 0:breadth] = jnp.where(
            parity == 0, odd[place, :], even[place, :]
        )
        place_low += count
        count = HIGH_ROWS[which]
        place = slice(place_high, place_high + count)
        joined[which, STRIP : STRIP + count, 0:breadth] = jnp.where(
            parity == 0, even[place, :], odd[place, :]
        )
        place_high += count

    zero = jnp.zeros((STRIP, width), jnp.float32)
    values, _ = coefficients(lambda which: joined[which, low_rows, :], handed[SOUTH])
    for index, value in enumerate(values):
        coef[index, low_rows, :] = value
    values, south = coefficients(lambda which: joined[which, high_rows, :], zero)
    for index, value in enumerate(values):
        coef[index, high_rows, :] = value
    row = lax.broadcasted_iota(jnp.int32, zero.shape, 0)
    missing = (
        handed[COEFFICIENTS + 9]
        * (1.0 / SCALE)
        * jnp.where(row == STRIP - 1, pltpu.roll(south, STRIP - 1, 0), 0.0)
    )

    def getter(strip):
        if strip == 0:
            return lambda k: coef[k, low_rows, :]
        if strip == 3:
            return lambda k: coef[k, high_rows, :]
        if strip == 1:
            return lambda k: handed[k]
        return lambda k: handed[COEFFICIENTS + k] + (missing if k in (10, 14) else 0.0)

    getters = [getter(strip) for strip in range(4)]
    inner = [slice(0, STRIP), slice(STRIP, 2 * STRIP)]

    def write(index, strip, value):
        if strip in (1, 2):
            kept[index, inner[strip - 1], :] = value
        else:
            outer[index, low_rows if strip == 0 else high_rows, :] = value

    def read(index, strip):
        if strip in (1, 2):
            return kept[index, inner[strip - 1], :]
        return outer[index, low_rows if strip == 0 else high_rows, :]

    write(0, 0, joined[0, low_rows, :])
    write(0, 3, joined[0, high_rows, :])
    write(0, 1, handed[FIRST])
    write(0, 2, handed[FIRST + 1])
    for order in range(ITERS):
        smoothed = ITERS + 1 + order
        totals = [weighted(getters[strip], read(order, strip)) for strip in range(4)]
        rising = weighted(lambda k: handed[NEAR + k], handed[BASIS + order], (0,))[0]
        falling = weighted(
            lambda k: handed[NEAR + 3 + k], handed[BASIS + KEPT + order], (0,)
        )[0]
        above = [zero, totals[0][2], falling, totals[2][2]]
        below = [totals[1][0], rising, totals[3][0], zero]
        for strip in range(4):
            write(
                smoothed,
                strip,
                getters[strip](9)
                * (
                    totals[strip][1]
                    + row_above(totals[strip][2], above[strip])
                    + row_below(totals[strip][0], below[strip])
                ),
            )
        blocks = [read(smoothed, strip) for strip in range(4)]
        before = [zero, blocks[0], handed[BASIS + KEPT + smoothed], blocks[2]]
        after = [blocks[1], handed[BASIS + smoothed], blocks[3], zero]
        for strip in range(4) if order < ITERS - 1 else (1, 2):
            write(
                order + 1,
                strip,
                applied(
                    getters[strip],
                    blocks[strip],
                    before[strip],
                    after[strip],
                    read(order, strip),
                ),
            )
    totals = tuple(sums[i] for i in range(PRODUCTS))
    for rows in inner:
        totals = gathered(totals, kept, rows, breadth)
    gram[...] = jnp.zeros(gram.shape, jnp.float32)
    for index in range(PRODUCTS):
        total = jnp.sum(jnp.sum(totals[index], axis=0, keepdims=True), axis=1, keepdims=True)
        gram[index : index + 1, :] = jnp.broadcast_to(total, (1, LANES))


def recurrences(gram):
    shift, scale = SHIFT, SCALE
    residual = [1.0]
    direction = []
    steps = [0.0] * ITERS
    rz_before = None
    for order in range(ITERS):
        rz = None
        for i in range(order + 1):
            inner = None
            for j in range(order + 1):
                term = residual[j] * gram[i][j]
                inner = term if inner is None else inner + term
            inner = residual[i] * inner
            rz = inner if rz is None else rz + inner
        if order == 0:
            direction = [1.0]
        else:
            ratio = rz / rz_before
            direction = [
                residual[i] + ratio * direction[i] if i < order else residual[i]
                for i in range(order + 1)
            ]
        image = [0.0] * (order + 2)
        for i in range(order + 1):
            image[i] = image[i] + shift * direction[i]
            image[i + 1] = image[i + 1] + scale * direction[i]
        curvature = None
        for i in range(order + 2):
            inner = None
            for j in range(order + 1):
                term = direction[j] * gram[i][j]
                inner = term if inner is None else inner + term
            inner = image[i] * inner
            curvature = inner if curvature is None else curvature + inner
        step = rz / curvature
        for i in range(order + 1):
            steps[i] = steps[i] + step * direction[i]
        residual = [
            (residual[i] if i < order + 1 else 0.0) - step * image[i]
            for i in range(order + 2)
        ]
        rz_before = rz
    return steps, residual


def combine_kernel(gram_ref, kept, edges, solution_ref, residual_ref):
    height, breadth = solution_ref.shape
    gram = [
        [gram_ref[i * ITERS + j : i * ITERS + j + 1, :] for j in range(ITERS)]
        for i in range(ITERS + 1)
    ]
    steps, residual = recurrences(gram)

    def wide(value):
        value = jnp.broadcast_to(value, (STRIP, LANES))
        return jnp.concatenate([value] * (breadth // LANES), axis=1)

    def put(source, rows_from, rows_to):
        total = None
        for j in range(ITERS):
            term = wide(steps[j]) * source[ITERS + 1 + j, rows_from, 0:breadth]
            total = term if total is None else total + term
        solution_ref[rows_to, :] = total
        total = None
        for i in range(ITERS + 1):
            term = wide(residual[i]) * source[i, rows_from, 0:breadth]
            total = term if total is None else total + term
        residual_ref[rows_to, :] = total

    put(edges, slice(0, STRIP), slice(0, STRIP))
    put(edges, slice(STRIP, 2 * STRIP), slice(height - STRIP, height))

    def middle(strip, carried):
        rows = strip_rows(strip)
        put(kept, rows, rows)
        return carried

    lax.fori_loop(1, height // STRIP - 1, middle, 0)


def params(limit=VMEM_BYTES):
    return pltpu.CompilerParams(vmem_limit_bytes=limit)


def cost(flops, moved):
    return pl.CostEstimate(flops=flops, bytes_accessed=moved, transcendentals=0)


def whole(*shapes):
    return [pl.BlockSpec(shape, lambda step, n=len(shape): (0,) * n) for shape in shapes]


def body(right_side, faces, ratio, centre, offdiag, mask):
    height, breadth = right_side.shape
    width = breadth + LANES
    args = [
        pltpu.with_memory_space_constraint(a, pltpu.HBM)
        for a in (right_side, mask, centre, ratio, faces, offdiag)
    ]
    f32 = jnp.float32
    gy = lax.axis_size("gy")
    swap = [(0, 1), (1, 0)]
    pairs = [(i, i ^ 1) for i in range(gy) if i ^ 1 < gy]
    between = [(i, (i + 1 ^ 1) - 1) for i in range(1, gy) if (i + 1 ^ 1) - 1 < gy]

    def diagonal(partners):
        return [(2 * a + c, 2 * b + 1 - c) for a, b in partners for c in (0, 1)]

    packed = jax.ShapeDtypeStruct((PACKED, breadth), f32)
    corner = jax.ShapeDtypeStruct((STRIP, LANES), f32)
    columns = jax.ShapeDtypeStruct((height, LANES), f32)
    even, odd, even_corner, odd_corner, columns = pl.pallas_call(
        pack_kernel,
        in_specs=[pl.BlockSpec(memory_space=pltpu.HBM)] * len(args),
        out_shape=(packed, packed, corner, corner, columns),
        scratch_shapes=[
            pltpu.VMEM((2,) + a.shape[:-2] + (STRIP, breadth), a.dtype) for a in args
        ]
        + [pltpu.VMEM(a.shape[:-1] + (LANES,), a.dtype) for a in args]
        + [
            pltpu.SemaphoreType.DMA((len(args), 2)),
            pltpu.SemaphoreType.DMA((len(args),)),
        ],
        compiler_params=params(PACK_VMEM_BYTES),
        cost_estimate=cost(0, 4 * 4 * PACKED * breadth),
        name="pack",
    )(*args)
    columns = lax.ppermute(columns, "gx", swap)
    even_in = lax.ppermute(even, "gy", pairs)
    even_corner = lax.ppermute(even_corner, ("gy", "gx"), diagonal(pairs))
    odd_in = lax.ppermute(odd, "gy", between)
    odd_corner = lax.ppermute(odd_corner, ("gy", "gx"), diagonal(between))

    cells = height * width
    kept, sums, handed = pl.pallas_call(
        tile_kernel,
        in_specs=[pl.BlockSpec(memory_space=pltpu.HBM)] * len(args)
        + [pl.BlockSpec(memory_space=pltpu.VMEM)],
        out_shape=(
            jax.ShapeDtypeStruct((KEPT, height, width), f32),
            jax.ShapeDtypeStruct((PRODUCTS, STRIP, LANES), f32),
            jax.ShapeDtypeStruct((HANDED, STRIP, width), f32),
        ),
        scratch_shapes=[
            pltpu.VMEM((COEFFICIENTS, height, width), f32),
            pltpu.VMEM((FIELDS, height, LANES), f32),
        ]
        + [pltpu.VMEM(a.shape, a.dtype) for a in args]
        + [pltpu.SemaphoreType.DMA((len(args), 2))],
        compiler_params=params(TILE_VMEM_BYTES),
        cost_estimate=cost(100 * cells, 4 * cells * (FIELDS + KEPT)),
        name="tile",
    )(*args, columns)

    sums, even_in, odd_in, even_corner, odd_corner = lax.optimization_barrier(
        (sums, even_in, odd_in, even_corner, odd_corner)
    )
    rows = 2 * STRIP
    edges, gram = pl.pallas_call(
        edge_kernel,
        out_shape=(
            jax.ShapeDtypeStruct((KEPT, rows, width), f32),
            jax.ShapeDtypeStruct((2 * STRIP, LANES), f32),
        ),
        scratch_shapes=[
            pltpu.VMEM((FIELDS, rows, width), f32),
            pltpu.VMEM((COEFFICIENTS, rows, width), f32),
            pltpu.VMEM((KEPT, rows, width), f32),
        ],
        compiler_params=params(),
        cost_estimate=cost(200 * rows * width, 4 * rows * width * (FIELDS + KEPT)),
        name="edge",
    )(handed, even_in, odd_in, even_corner, odd_corner, sums)

    gram = gram + lax.ppermute(gram, "gx", swap)
    reach = 1
    while reach < gy:
        gram = gram + lax.ppermute(gram, "gy", [(i, i ^ reach) for i in range(gy)])
        reach *= 2

    tile = jax.ShapeDtypeStruct((height, breadth), f32)
    return pl.pallas_call(
        combine_kernel,
        grid=(1,),
        in_specs=whole(gram.shape, kept.shape, edges.shape),
        out_specs=whole(tile.shape, tile.shape),
        out_shape=(tile, tile),
        compiler_params=params(),
        cost_estimate=cost(14 * height * breadth, 4 * height * breadth * (KEPT + 2)),
        name="combine",
    )(gram, kept, edges)


def solution(mesh):
    return jax.shard_map(
        body,
        mesh=mesh,
        in_specs=(
            P(("members", "gy"), "gx"),
            P(None, "gy", "gx"),
            P("gy", "gx"),
            P("gy", "gx"),
            P(None, "gy", "gx"),
            P("gy", "gx"),
        ),
        out_specs=(P(("members", "gy"), "gx"), P(("members", "gy"), "gx")),
        check_vma=False,
    )
```

```python
import functools

import jax
import jax.numpy as jnp
from jax import lax
from jax.experimental import pallas as pl
from jax.experimental.pallas import tpu as pltpu
from jax.sharding import PartitionSpec as P

ITERS = 3
SHIFT = 1.0
SCALE = 4.0
LANES = 128
STRIP = 8

neighbour_steps = [(-1, -1), (-1, 0), (-1, 1), (0, -1), (0, 1), (1, -1), (1, 0), (1, 1)]

FIELDS = 6 + len(neighbour_steps)
REACH = 2 * ITERS
LOW_ROWS = [REACH, REACH - 1, REACH - 1, REACH - 2, REACH - 2, REACH - 2] + [
    REACH - 1 + down for down, _ in neighbour_steps
]
HIGH_ROWS = [REACH, REACH - 1, REACH - 1, REACH - 2, REACH - 2, REACH - 1] + [
    REACH - 1 - down for down, _ in neighbour_steps
]
PACKED = -(-max(sum(LOW_ROWS), sum(HIGH_ROWS)) // STRIP) * STRIP
PRODUCTS = (ITERS + 1) * ITERS
KEPT = 2 * ITERS + 1
SLOT = 8
COEFFICIENTS = 15
NEAR = 2 * COEFFICIENTS
SOUTH = NEAR + 6
FIRST = SOUTH + 1
BASIS = FIRST + 2
HANDED = BASIS + 2 * KEPT
TILE_VMEM_BYTES = 40 * 1024 * 1024
VMEM_BYTES = 32 * 1024 * 1024
PACK_VMEM_BYTES = 16 * 1024 * 1024


def field(refs, which, rows):
    right_side, mask, centre, ratio, faces, offdiag = refs
    if which == 0:
        return mask[rows, :].astype(jnp.float32) * right_side[rows, :]
    if which == 1:
        return mask[rows, :].astype(jnp.float32)
    if which == 2:
        return centre[rows, :]
    if which == 3:
        return ratio[rows, :]
    if which < 6:
        return faces[which - 4, rows, :]
    return offdiag[which - 6, rows, :]


def trimmed(out, refs, counts, at_end):
    place = 0
    for which, count in enumerate(counts):
        rows = slice(STRIP - count, STRIP) if at_end else slice(0, count)
        out[place : place + count, :] = field(refs, which, rows)
        place += count
    if place < PACKED:
        out[place:PACKED, :] = jnp.zeros((PACKED - place, out.shape[1]), jnp.float32)


def lanes_of(shape):
    return lax.broadcasted_iota(jnp.int32, shape, len(shape) - 1)


def squeezed(near, side):
    start = jnp.where(side == 0, SLOT, 0)
    total = None
    for which in range(FIELDS):
        block = pltpu.roll(near(which), start + SLOT * which, 1)
        if total is None:
            lane = lanes_of(block.shape)
            total = jnp.zeros(block.shape, jnp.float32)
        inside = (lane >= SLOT * which) & (lane < SLOT * (which + 1))
        total = jnp.where(inside, block, total)
    return total


def spread(block, side):
    lane = lanes_of(block.shape)
    start = jnp.where(side == 0, LANES, LANES - SLOT)
    first = jnp.where(side == 0, 0, LANES - SLOT)
    inside = ((lane >= first) & (lane < first + SLOT)).astype(jnp.float32)
    return [
        pltpu.roll(block, start - SLOT * which, 1) * inside for which in range(FIELDS)
    ]


def pack_kernel(*refs):
    args = refs[0:6]
    even, odd, even_corner, odd_corner, columns = refs[6:11]
    ends, sides, end_arrived, side_arrived = refs[11:17], refs[17:23], refs[23], refs[24]
    height, breadth = args[0].shape
    side = lax.axis_index("gx")
    parity = lax.rem(lax.axis_index("gy"), 2)
    beside = pl.multiple_of(jnp.where(side == 0, breadth - LANES, 0), LANES)
    copies, more = [], []
    for index, (arg, end, edge) in enumerate(zip(args, ends, sides)):
        lead = (slice(None),) * (len(arg.shape) - 2)
        for which, start in enumerate((0, height - STRIP)):
            copies.append(
                pltpu.make_async_copy(
                    arg.at[lead + (pl.ds(start, STRIP), slice(None))],
                    end.at[which],
                    end_arrived.at[index, which],
                )
            )
        more.append(
            pltpu.make_async_copy(
                arg.at[lead + (slice(None), pl.ds(beside, LANES))],
                edge,
                side_arrived.at[index],
            )
        )
    for copy in copies + more:
        copy.start()
    for copy in copies:
        copy.wait()
    first = [end.at[0] for end in ends]
    last = [end.at[1] for end in ends]

    @pl.when(parity == 0)
    def _():
        trimmed(even, last, LOW_ROWS, True)
        trimmed(odd, first, HIGH_ROWS, False)

    @pl.when(parity != 0)
    def _():
        trimmed(even, first, HIGH_ROWS, False)
        trimmed(odd, last, LOW_ROWS, True)

    for copy in more:
        copy.wait()
    packed = squeezed(lambda which: field(sides, which, slice(None)), side)
    columns[...] = packed
    corner_first, corner_last = packed[0:STRIP, :], packed[height - STRIP : height, :]
    even_corner[...] = jnp.where(parity == 0, corner_last, corner_first)
    odd_corner[...] = jnp.where(parity == 0, corner_first, corner_last)


def row_above(block, before):
    row = lax.broadcasted_iota(jnp.int32, block.shape, 0)
    return jnp.where(row == 0, pltpu.roll(before, 1, 0), pltpu.roll(block, 1, 0))


def row_below(block, after):
    row = lax.broadcasted_iota(jnp.int32, block.shape, 0)
    last = STRIP - 1
    return jnp.where(row == last, pltpu.roll(after, last, 0), pltpu.roll(block, last, 0))


def strip_rows(strip):
    return pl.ds(pl.multiple_of(strip * STRIP, STRIP), STRIP)


def west_of(block):
    return pltpu.roll(block, 1, 1)


def east_of(block):
    return pltpu.roll(block, block.shape[1] - 1, 1)


def coefficients(get, south_after):
    result = [None] * COEFFICIENTS
    wet = get(1)
    result[4] = get(2)
    for index, (down, across) in enumerate(neighbour_steps):
        weight = get(6 + index)
        if across == 1:
            weight = west_of(weight)
        elif across == -1:
            weight = east_of(weight)
        result[(down + 1) * 3 + across + 1] = weight
    west = get(4)
    south = get(5)
    east = east_of(west)
    north = row_below(south, south_after)
    scaled = wet * (1.0 / SCALE)
    result[9] = wet
    result[10] = scaled * (west + east + south + north + get(3))
    result[11] = scaled * west
    result[12] = scaled * east
    result[13] = scaled * south
    result[14] = scaled * north
    return result, south


def weighted(get, block, downs=(0, 1, 2)):
    left, right = east_of(block), west_of(block)
    return [
        get(down * 3) * left + get(down * 3 + 1) * block + get(down * 3 + 2) * right
        for down in downs
    ]


def applied(get, block, before, after, old):
    return (
        get(10) * block
        - get(11) * west_of(block)
        - get(12) * east_of(block)
        - get(13) * row_above(block, before)
        - get(14) * row_below(block, after)
        - (SHIFT / SCALE) * old
    )


def gathered(totals, kept, rows, breadth):
    result = list(totals)
    for start in range(0, breadth, LANES):
        bases = [kept[i, rows, start : start + LANES] for i in range(KEPT)]
        for i in range(ITERS + 1):
            for j in range(ITERS):
                result[i * ITERS + j] += bases[i] * bases[ITERS + 1 + j]
    return tuple(result)


def krylov(load, strips, coef, kept):
    width = kept.shape[2]
    zero = jnp.zeros((STRIP, width), jnp.float32)

    def prepare(step, south_after):
        strip = strips - 1 - step
        rows = strip_rows(strip)
        kept[0, rows, :] = load(0, strip)
        values, south = coefficients(lambda which: load(which, strip), south_after)
        for index, value in enumerate(values):
            coef[index, rows, :] = value
        return south

    lax.fori_loop(0, strips, prepare, zero, unroll=strips)

    for order in range(ITERS):
        smoothed = ITERS + 1 + order

        def smooth(strip, carried):
            above, partial = carried
            rows = strip_rows(strip)
            totals = weighted(lambda k: coef[k, rows, :], kept[order, rows, :])
            row = lax.broadcasted_iota(jnp.int32, totals[0].shape, 0)
            rising = pltpu.roll(totals[0], STRIP - 1, 0)
            falling = pltpu.roll(totals[2], 1, 0)
            done = strip_rows(jnp.maximum(strip - 1, 0))
            kept[smoothed, done, :] = coef[9, done, :] * (
                partial + jnp.where(row == STRIP - 1, rising, 0.0)
            )
            partial = (
                totals[1]
                + jnp.where(row == 0, above, falling)
                + jnp.where(row == STRIP - 1, 0.0, rising)
            )
            return falling, partial

        _, partial = lax.fori_loop(0, strips, smooth, (zero, zero), unroll=strips)
        done = slice((strips - 1) * STRIP, strips * STRIP)
        kept[smoothed, done, :] = coef[9, done, :] * partial

        def operate(strip, carried):
            rows = strip_rows(strip)
            kept[order + 1, rows, :] = applied(
                lambda k: coef[k, rows, :],
                kept[smoothed, rows, :],
                kept[smoothed, strip_rows(jnp.maximum(strip - 1, 0)), :],
                kept[smoothed, strip_rows(jnp.minimum(strip + 1, strips - 1)), :],
                kept[order, rows, :],
            )
            return carried

        lax.fori_loop(0, strips, operate, 0, unroll=strips)


def tile_kernel(*refs):
    own, columns, kept, sums, handed, coef, wide = refs[0:6], *refs[6:12]
    strips = kept.shape[1] // STRIP
    side = lax.axis_index("gx")
    for which, block in enumerate(spread(columns[...], side)):
        wide[which] = block

    def load(which, strip):
        rows = strip_rows(strip)
        return jnp.concatenate([field(own, which, rows), wide[which, rows, :]], axis=1)

    krylov(load, strips, coef, kept)
    zero = jnp.zeros((STRIP, LANES), jnp.float32)
    breadth = kept.shape[2] - LANES
    totals = lax.fori_loop(
        1,
        strips - 1,
        lambda strip, totals: gathered(totals, kept, strip_rows(strip), breadth),
        (zero,) * PRODUCTS,
        unroll=2,
    )
    for index in range(PRODUCTS):
        sums[index] = totals[index]
    first, last = slice(0, STRIP), slice((strips - 1) * STRIP, strips * STRIP)
    second, third = slice(STRIP, 2 * STRIP), slice((strips - 2) * STRIP, (strips - 1) * STRIP)
    for index in range(COEFFICIENTS):
        handed[index] = coef[index, first, :]
        handed[COEFFICIENTS + index] = coef[index, last, :]
    for index in range(3):
        handed[NEAR + index] = coef[index, second, :]
        handed[NEAR + 3 + index] = coef[6 + index, third, :]
    handed[SOUTH] = load(5, 0)
    handed[FIRST] = kept[0, first, :]
    handed[FIRST + 1] = kept[0, last, :]
    for index in range(KEPT):
        handed[BASIS + index] = kept[index, second, :]
        handed[BASIS + KEPT + index] = kept[index, third, :]


def edge_kernel(
    handed, even, odd, even_corner, odd_corner, sums, kept, gram, joined, coef, outer
):
    breadth = even.shape[1]
    width = breadth + LANES
    side = lax.axis_index("gx")
    parity = lax.rem(lax.axis_index("gy"), 2)
    low_corner = spread(jnp.where(parity == 0, odd_corner[...], even_corner[...]), side)
    high_corner = spread(jnp.where(parity == 0, even_corner[...], odd_corner[...]), side)
    low_rows, high_rows = slice(0, STRIP), slice(STRIP, 2 * STRIP)
    place_low, place_high = 0, 0
    for which in range(FIELDS):
        joined[which, :, 0:breadth] = jnp.zeros((2 * STRIP, breadth), jnp.float32)
        joined[which, low_rows, breadth:width] = low_corner[which]
        joined[which, high_rows, breadth:width] = high_corner[which]
        count = LOW_ROWS[which]
        place = slice(place_low, place_low + count)
        joined[which, STRIP - count : STRIP, 0:breadth] = jnp.where(
            parity == 0, odd[place, :], even[place, :]
        )
        place_low += count
        count = HIGH_ROWS[which]
        place = slice(place_high, place_high + count)
        joined[which, STRIP : STRIP + count, 0:breadth] = jnp.where(
            parity == 0, even[place, :], odd[place, :]
        )
        place_high += count

    zero = jnp.zeros((STRIP, width), jnp.float32)
    values, _ = coefficients(lambda which: joined[which, low_rows, :], handed[SOUTH])
    for index, value in enumerate(values):
        coef[index, low_rows, :] = value
    values, south = coefficients(lambda which: joined[which, high_rows, :], zero)
    for index, value in enumerate(values):
        coef[index, high_rows, :] = value
    row = lax.broadcasted_iota(jnp.int32, zero.shape, 0)
    missing = (
        handed[COEFFICIENTS + 9]
        * (1.0 / SCALE)
        * jnp.where(row == STRIP - 1, pltpu.roll(south, STRIP - 1, 0), 0.0)
    )

    def getter(strip):
        if strip == 0:
            return lambda k: coef[k, low_rows, :]
        if strip == 3:
            return lambda k: coef[k, high_rows, :]
        if strip == 1:
            return lambda k: handed[k]
        return lambda k: handed[COEFFICIENTS + k] + (missing if k in (10, 14) else 0.0)

    getters = [getter(strip) for strip in range(4)]
    inner = [slice(0, STRIP), slice(STRIP, 2 * STRIP)]

    def write(index, strip, value):
        if strip in (1, 2):
            kept[index, inner[strip - 1], :] = value
        else:
            outer[index, low_rows if strip == 0 else high_rows, :] = value

    def read(index, strip):
        if strip in (1, 2):
            return kept[index, inner[strip - 1], :]
        return outer[index, low_rows if strip == 0 else high_rows, :]

    write(0, 0, joined[0, low_rows, :])
    write(0, 3, joined[0, high_rows, :])
    write(0, 1, handed[FIRST])
    write(0, 2, handed[FIRST + 1])
    for order in range(ITERS):
        smoothed = ITERS + 1 + order
        totals = [weighted(getters[strip], read(order, strip)) for strip in range(4)]
        rising = weighted(lambda k: handed[NEAR + k], handed[BASIS + order], (0,))[0]
        falling = weighted(
            lambda k: handed[NEAR + 3 + k], handed[BASIS + KEPT + order], (0,)
        )[0]
        above = [zero, totals[0][2], falling, totals[2][2]]
        below = [totals[1][0], rising, totals[3][0], zero]
        for strip in range(4):
            write(
                smoothed,
                strip,
                getters[strip](9)
                * (
                    totals[strip][1]
                    + row_above(totals[strip][2], above[strip])
                    + row_below(totals[strip][0], below[strip])
                ),
            )
        blocks = [read(smoothed, strip) for strip in range(4)]
        before = [zero, blocks[0], handed[BASIS + KEPT + smoothed], blocks[2]]
        after = [blocks[1], handed[BASIS + smoothed], blocks[3], zero]
        for strip in range(4) if order < ITERS - 1 else (1, 2):
            write(
                order + 1,
                strip,
                applied(
                    getters[strip],
                    blocks[strip],
                    before[strip],
                    after[strip],
                    read(order, strip),
                ),
            )
    totals = tuple(sums[i] for i in range(PRODUCTS))
    for rows in inner:
        totals = gathered(totals, kept, rows, breadth)
    gram[...] = jnp.zeros(gram.shape, jnp.float32)
    for index in range(PRODUCTS):
        total = jnp.sum(jnp.sum(totals[index], axis=0, keepdims=True), axis=1, keepdims=True)
        gram[index : index + 1, :] = jnp.broadcast_to(total, (1, LANES))


def recurrences(gram):
    shift, scale = SHIFT, SCALE
    residual = [1.0]
    direction = []
    steps = [0.0] * ITERS
    rz_before = None
    for order in range(ITERS):
        rz = None
        for i in range(order + 1):
            inner = None
            for j in range(order + 1):
                term = residual[j] * gram[i][j]
                inner = term if inner is None else inner + term
            inner = residual[i] * inner
            rz = inner if rz is None else rz + inner
        if order == 0:
            direction = [1.0]
        else:
            ratio = rz / rz_before
            direction = [
                residual[i] + ratio * direction[i] if i < order else residual[i]
                for i in range(order + 1)
            ]
        image = [0.0] * (order + 2)
        for i in range(order + 1):
            image[i] = image[i] + shift * direction[i]
            image[i + 1] = image[i + 1] + scale * direction[i]
        curvature = None
        for i in range(order + 2):
            inner = None
            for j in range(order + 1):
                term = direction[j] * gram[i][j]
                inner = term if inner is None else inner + term
            inner = image[i] * inner
            curvature = inner if curvature is None else curvature + inner
        step = rz / curvature
        for i in range(order + 1):
            steps[i] = steps[i] + step * direction[i]
        residual = [
            (residual[i] if i < order + 1 else 0.0) - step * image[i]
            for i in range(order + 2)
        ]
        rz_before = rz
    return steps, residual


def combine_kernel(gram_ref, kept, edges, solution_ref, residual_ref):
    height, breadth = solution_ref.shape
    gram = [
        [gram_ref[i * ITERS + j : i * ITERS + j + 1, :] for j in range(ITERS)]
        for i in range(ITERS + 1)
    ]
    steps, residual = recurrences(gram)

    def wide(value):
        value = jnp.broadcast_to(value, (STRIP, LANES))
        return jnp.concatenate([value] * (breadth // LANES), axis=1)

    def put(source, rows_from, rows_to):
        total = None
        for j in range(ITERS):
            term = wide(steps[j]) * source[ITERS + 1 + j, rows_from, 0:breadth]
            total = term if total is None else total + term
        solution_ref[rows_to, :] = total
        total = None
        for i in range(ITERS + 1):
            term = wide(residual[i]) * source[i, rows_from, 0:breadth]
            total = term if total is None else total + term
        residual_ref[rows_to, :] = total

    put(edges, slice(0, STRIP), slice(0, STRIP))
    put(edges, slice(STRIP, 2 * STRIP), slice(height - STRIP, height))

    def middle(strip, carried):
        rows = strip_rows(strip)
        put(kept, rows, rows)
        return carried

    lax.fori_loop(1, height // STRIP - 1, middle, 0)


def params(limit=VMEM_BYTES):
    return pltpu.CompilerParams(vmem_limit_bytes=limit)


def cost(flops, moved):
    return pl.CostEstimate(flops=flops, bytes_accessed=moved, transcendentals=0)


def whole(*shapes):
    return [pl.BlockSpec(shape, lambda step, n=len(shape): (0,) * n) for shape in shapes]


def body(right_side, faces, ratio, centre, offdiag, mask):
    height, breadth = right_side.shape
    width = breadth + LANES
    args = (right_side, mask, centre, ratio, faces, offdiag)
    held = [pltpu.with_memory_space_constraint(a, pltpu.HBM) for a in args]
    f32 = jnp.float32
    gy = lax.axis_size("gy")
    swap = [(0, 1), (1, 0)]
    pairs = [(i, i ^ 1) for i in range(gy) if i ^ 1 < gy]
    between = [(i, (i + 1 ^ 1) - 1) for i in range(1, gy) if (i + 1 ^ 1) - 1 < gy]

    def diagonal(partners):
        return [(2 * a + c, 2 * b + 1 - c) for a, b in partners for c in (0, 1)]

    packed = jax.ShapeDtypeStruct((PACKED, breadth), f32)
    corner = jax.ShapeDtypeStruct((STRIP, LANES), f32)
    columns = jax.ShapeDtypeStruct((height, LANES), f32)
    even, odd, even_corner, odd_corner, columns = pl.pallas_call(
        pack_kernel,
        in_specs=[pl.BlockSpec(memory_space=pltpu.HBM)] * len(args),
        out_shape=(packed, packed, corner, corner, columns),
        scratch_shapes=[
            pltpu.VMEM((2,) + a.shape[:-2] + (STRIP, breadth), a.dtype) for a in args
        ]
        + [pltpu.VMEM(a.shape[:-1] + (LANES,), a.dtype) for a in args]
        + [
            pltpu.SemaphoreType.DMA((len(args), 2)),
            pltpu.SemaphoreType.DMA((len(args),)),
        ],
        compiler_params=params(PACK_VMEM_BYTES),
        cost_estimate=cost(0, 4 * 4 * PACKED * breadth),
        name="pack",
    )(*held)
    columns = lax.ppermute(columns, "gx", swap)
    even_in = lax.ppermute(even, "gy", pairs)
    even_corner = lax.ppermute(even_corner, ("gy", "gx"), diagonal(pairs))
    odd_in = lax.ppermute(odd, "gy", between)
    odd_corner = lax.ppermute(odd_corner, ("gy", "gx"), diagonal(between))

    cells = height * width
    kept, sums, handed = pl.pallas_call(
        tile_kernel,
        out_shape=(
            jax.ShapeDtypeStruct((KEPT, height, width), f32),
            jax.ShapeDtypeStruct((PRODUCTS, STRIP, LANES), f32),
            jax.ShapeDtypeStruct((HANDED, STRIP, width), f32),
        ),
        scratch_shapes=[
            pltpu.VMEM((COEFFICIENTS, height, width), f32),
            pltpu.VMEM((FIELDS, height, LANES), f32),
        ],
        compiler_params=params(TILE_VMEM_BYTES),
        cost_estimate=cost(100 * cells, 4 * cells * (FIELDS + KEPT)),
        name="tile",
    )(*args, columns)

    sums, even_in, odd_in, even_corner, odd_corner = lax.optimization_barrier(
        (sums, even_in, odd_in, even_corner, odd_corner)
    )
    rows = 2 * STRIP
    edges, gram = pl.pallas_call(
        edge_kernel,
        out_shape=(
            jax.ShapeDtypeStruct((KEPT, rows, width), f32),
            jax.ShapeDtypeStruct((2 * STRIP, LANES), f32),
        ),
        scratch_shapes=[
            pltpu.VMEM((FIELDS, rows, width), f32),
            pltpu.VMEM((COEFFICIENTS, rows, width), f32),
            pltpu.VMEM((KEPT, rows, width), f32),
        ],
        compiler_params=params(),
        cost_estimate=cost(200 * rows * width, 4 * rows * width * (FIELDS + KEPT)),
        name="edge",
    )(handed, even_in, odd_in, even_corner, odd_corner, sums)

    gram = gram + lax.ppermute(gram, "gx", swap)
    reach = 1
    while reach < gy:
        gram = gram + lax.ppermute(gram, "gy", [(i, i ^ reach) for i in range(gy)])
        reach *= 2

    tile = jax.ShapeDtypeStruct((height, breadth), f32)
    return pl.pallas_call(
        combine_kernel,
        grid=(1,),
        in_specs=whole(gram.shape, kept.shape, edges.shape),
        out_specs=whole(tile.shape, tile.shape),
        out_shape=(tile, tile),
        compiler_params=params(),
        cost_estimate=cost(14 * height * breadth, 4 * height * breadth * (KEPT + 2)),
        name="combine",
    )(gram, kept, edges)


def solution(mesh):
    return jax.shard_map(
        body,
        mesh=mesh,
        in_specs=(
            P(("members", "gy"), "gx"),
            P(None, "gy", "gx"),
            P("gy", "gx"),
            P("gy", "gx"),
            P(None, "gy", "gx"),
            P("gy", "gx"),
        ),
        out_specs=(P(("members", "gy"), "gx"), P(("members", "gy"), "gx")),
        check_vma=False,
    )
```

```python
import functools

import jax
import jax.numpy as jnp
from jax import lax
from jax.experimental import pallas as pl
from jax.experimental.pallas import tpu as pltpu
from jax.sharding import PartitionSpec as P

ITERS = 3
SHIFT = 1.0
SCALE = 4.0
LANES = 128
STRIP = 8

neighbour_steps = [(-1, -1), (-1, 0), (-1, 1), (0, -1), (0, 1), (1, -1), (1, 0), (1, 1)]

FIELDS = 6 + len(neighbour_steps)
REACH = 2 * ITERS
LOW_ROWS = [REACH, REACH - 1, REACH - 1, REACH - 2, REACH - 2, REACH - 2] + [
    REACH - 1 + down for down, _ in neighbour_steps
]
HIGH_ROWS = [REACH, REACH - 1, REACH - 1, REACH - 2, REACH - 2, REACH - 1] + [
    REACH - 1 - down for down, _ in neighbour_steps
]
PACKED = -(-max(sum(LOW_ROWS), sum(HIGH_ROWS)) // STRIP) * STRIP
PRODUCTS = (ITERS + 1) * ITERS
KEPT = 2 * ITERS + 1
SLOT = 8
PARTS = 4
COEFFICIENTS = 15
NEAR = 2 * COEFFICIENTS
SOUTH = NEAR + 6
FIRST = SOUTH + 1
BASIS = FIRST + 2
HANDED = BASIS + 2 * KEPT
TILE_VMEM_BYTES = 40 * 1024 * 1024
VMEM_BYTES = 32 * 1024 * 1024
PACK_VMEM_BYTES = 16 * 1024 * 1024


def field(refs, which, rows):
    right_side, mask, centre, ratio, faces, offdiag = refs
    if which == 0:
        return mask[rows, :].astype(jnp.float32) * right_side[rows, :]
    if which == 1:
        return mask[rows, :].astype(jnp.float32)
    if which == 2:
        return centre[rows, :]
    if which == 3:
        return ratio[rows, :]
    if which < 6:
        return faces[which - 4, rows, :]
    return offdiag[which - 6, rows, :]


def trimmed(out, refs, counts, at_end):
    place = 0
    for which, count in enumerate(counts):
        rows = slice(STRIP - count, STRIP) if at_end else slice(0, count)
        out[place : place + count, :] = field(refs, which, rows)
        place += count
    if place < PACKED:
        out[place:PACKED, :] = jnp.zeros((PACKED - place, out.shape[1]), jnp.float32)


def lanes_of(shape):
    return lax.broadcasted_iota(jnp.int32, shape, len(shape) - 1)


def beside(refs, which, rows, side):
    breadth = refs[0].shape[1]
    west = field([ref.at[..., 0:LANES] for ref in refs], which, rows)
    east = field([ref.at[..., breadth - LANES : breadth] for ref in refs], which, rows)
    return jnp.where(side == 0, east, west)


def squeezed(near, side):
    start = jnp.where(side == 0, SLOT, 0)
    total = None
    for which in range(FIELDS):
        block = pltpu.roll(near(which), start + SLOT * which, 1)
        if total is None:
            lane = lanes_of(block.shape)
            total = jnp.zeros(block.shape, jnp.float32)
        inside = (lane >= SLOT * which) & (lane < SLOT * (which + 1))
        total = jnp.where(inside, block, total)
    return total


def spread(block, side):
    lane = lanes_of(block.shape)
    start = jnp.where(side == 0, LANES, LANES - SLOT)
    first = jnp.where(side == 0, 0, LANES - SLOT)
    inside = ((lane >= first) & (lane < first + SLOT)).astype(jnp.float32)
    return [
        pltpu.roll(block, start - SLOT * which, 1) * inside for which in range(FIELDS)
    ]


def pack_kernel(*refs):
    args = refs[0:6]
    even, odd, even_corner, odd_corner = refs[6:10]
    ends, arrived = refs[10:16], refs[16]
    height, breadth = args[0].shape
    side = lax.axis_index("gx")
    parity = lax.rem(lax.axis_index("gy"), 2)
    copies = []
    for index, (arg, end) in enumerate(zip(args, ends)):
        lead = (slice(None),) * (len(arg.shape) - 2)
        for which, start in enumerate((0, height - STRIP)):
            copies.append(
                pltpu.make_async_copy(
                    arg.at[lead + (pl.ds(start, STRIP), slice(None))],
                    end.at[which],
                    arrived.at[index, which],
                )
            )
    for copy in copies:
        copy.start()
    for copy in copies:
        copy.wait()
    first = [end.at[0] for end in ends]
    last = [end.at[1] for end in ends]
    rows = slice(0, STRIP)
    corner_first = squeezed(lambda which: beside(first, which, rows, side), side)
    corner_last = squeezed(lambda which: beside(last, which, rows, side), side)
    even_corner[...] = jnp.where(parity == 0, corner_last, corner_first)
    odd_corner[...] = jnp.where(parity == 0, corner_first, corner_last)

    @pl.when(parity == 0)
    def _():
        trimmed(even, last, LOW_ROWS, True)
        trimmed(odd, first, HIGH_ROWS, False)

    @pl.when(parity != 0)
    def _():
        trimmed(even, first, HIGH_ROWS, False)
        trimmed(odd, last, LOW_ROWS, True)


def columns_kernel(*refs):
    args, columns = refs[0:6], refs[7]
    side = lax.axis_index("gx")
    columns[...] = squeezed(lambda which: beside(args, which, slice(None), side), side)


def row_above(block, before):
    row = lax.broadcasted_iota(jnp.int32, block.shape, 0)
    return jnp.where(row == 0, pltpu.roll(before, 1, 0), pltpu.roll(block, 1, 0))


def row_below(block, after):
    row = lax.broadcasted_iota(jnp.int32, block.shape, 0)
    last = STRIP - 1
    return jnp.where(row == last, pltpu.roll(after, last, 0), pltpu.roll(block, last, 0))


def strip_rows(strip):
    return pl.ds(pl.multiple_of(strip * STRIP, STRIP), STRIP)


def west_of(block):
    return pltpu.roll(block, 1, 1)


def east_of(block):
    return pltpu.roll(block, block.shape[1] - 1, 1)


def coefficients(get, south_after):
    result = [None] * COEFFICIENTS
    wet = get(1)
    result[4] = get(2)
    for index, (down, across) in enumerate(neighbour_steps):
        weight = get(6 + index)
        if across == 1:
            weight = west_of(weight)
        elif across == -1:
            weight = east_of(weight)
        result[(down + 1) * 3 + across + 1] = weight
    west = get(4)
    south = get(5)
    east = east_of(west)
    north = row_below(south, south_after)
    scaled = wet * (1.0 / SCALE)
    result[9] = wet
    result[10] = scaled * (west + east + south + north + get(3))
    result[11] = scaled * west
    result[12] = scaled * east
    result[13] = scaled * south
    result[14] = scaled * north
    return result, south


def weighted(get, block, downs=(0, 1, 2)):
    left, right = east_of(block), west_of(block)
    return [
        get(down * 3) * left + get(down * 3 + 1) * block + get(down * 3 + 2) * right
        for down in downs
    ]


def applied(get, block, before, after, old):
    return (
        get(10) * block
        - get(11) * west_of(block)
        - get(12) * east_of(block)
        - get(13) * row_above(block, before)
        - get(14) * row_below(block, after)
        - (SHIFT / SCALE) * old
    )


def gathered(totals, kept, rows, breadth):
    result = list(totals)
    for start in range(0, breadth, LANES):
        bases = [kept[i, rows, start : start + LANES] for i in range(KEPT)]
        for i in range(ITERS + 1):
            for j in range(ITERS):
                result[i * ITERS + j] += bases[i] * bases[ITERS + 1 + j]
    return tuple(result)


def krylov(load, strips, coef, kept):
    width = kept.shape[2]
    zero = jnp.zeros((STRIP, width), jnp.float32)

    def prepare(step, south_after):
        strip = strips - 1 - step
        rows = strip_rows(strip)
        kept[0, rows, :] = load(0, strip)
        values, south = coefficients(lambda which: load(which, strip), south_after)
        for index, value in enumerate(values):
            coef[index, rows, :] = value
        return south

    lax.fori_loop(0, strips, prepare, zero, unroll=strips)

    for order in range(ITERS):
        smoothed = ITERS + 1 + order

        def smooth(strip, carried):
            above, partial = carried
            rows = strip_rows(strip)
            totals = weighted(lambda k: coef[k, rows, :], kept[order, rows, :])
            row = lax.broadcasted_iota(jnp.int32, totals[0].shape, 0)
            rising = pltpu.roll(totals[0], STRIP - 1, 0)
            falling = pltpu.roll(totals[2], 1, 0)
            done = strip_rows(jnp.maximum(strip - 1, 0))
            kept[smoothed, done, :] = coef[9, done, :] * (
                partial + jnp.where(row == STRIP - 1, rising, 0.0)
            )
            partial = (
                totals[1]
                + jnp.where(row == 0, above, falling)
                + jnp.where(row == STRIP - 1, 0.0, rising)
            )
            return falling, partial

        _, partial = lax.fori_loop(0, strips, smooth, (zero, zero), unroll=strips)
        done = slice((strips - 1) * STRIP, strips * STRIP)
        kept[smoothed, done, :] = coef[9, done, :] * partial

        def operate(strip, carried):
            rows = strip_rows(strip)
            kept[order + 1, rows, :] = applied(
                lambda k: coef[k, rows, :],
                kept[smoothed, rows, :],
                kept[smoothed, strip_rows(jnp.maximum(strip - 1, 0)), :],
                kept[smoothed, strip_rows(jnp.minimum(strip + 1, strips - 1)), :],
                kept[order, rows, :],
            )
            return carried

        lax.fori_loop(0, strips, operate, 0, unroll=strips)


def tile_kernel(*refs):
    own, columns, kept, sums, handed, coef, wide = refs[0:6], *refs[6:12]
    strips = kept.shape[1] // STRIP
    side = lax.axis_index("gx")
    for which, block in enumerate(spread(columns[...], side)):
        wide[which] = block

    def load(which, strip):
        rows = strip_rows(strip)
        return jnp.concatenate([field(own, which, rows), wide[which, rows, :]], axis=1)

    krylov(load, strips, coef, kept)
    zero = jnp.zeros((STRIP, LANES), jnp.float32)
    breadth = kept.shape[2] - LANES
    totals = lax.fori_loop(
        1,
        strips - 1,
        lambda strip, totals: gathered(totals, kept, strip_rows(strip), breadth),
        (zero,) * PRODUCTS,
        unroll=2,
    )
    for index in range(PRODUCTS):
        sums[index] = totals[index]
    first, last = slice(0, STRIP), slice((strips - 1) * STRIP, strips * STRIP)
    second, third = slice(STRIP, 2 * STRIP), slice((strips - 2) * STRIP, (strips - 1) * STRIP)
    for index in range(COEFFICIENTS):
        handed[index] = coef[index, first, :]
        handed[COEFFICIENTS + index] = coef[index, last, :]
    for index in range(3):
        handed[NEAR + index] = coef[index, second, :]
        handed[NEAR + 3 + index] = coef[6 + index, third, :]
    handed[SOUTH] = load(5, 0)
    handed[FIRST] = kept[0, first, :]
    handed[FIRST + 1] = kept[0, last, :]
    for index in range(KEPT):
        handed[BASIS + index] = kept[index, second, :]
        handed[BASIS + KEPT + index] = kept[index, third, :]


def edge_kernel(
    handed, even, odd, even_corner, odd_corner, sums, kept, gram, joined, coef, outer
):
    breadth = even.shape[1]
    width = breadth + LANES
    side = lax.axis_index("gx")
    parity = lax.rem(lax.axis_index("gy"), 2)
    low_corner = spread(jnp.where(parity == 0, odd_corner[...], even_corner[...]), side)
    high_corner = spread(jnp.where(parity == 0, even_corner[...], odd_corner[...]), side)
    low_rows, high_rows = slice(0, STRIP), slice(STRIP, 2 * STRIP)
    place_low, place_high = 0, 0
    for which in range(FIELDS):
        joined[which, :, 0:breadth] = jnp.zeros((2 * STRIP, breadth), jnp.float32)
        joined[which, low_rows, breadth:width] = low_corner[which]
        joined[which, high_rows, breadth:width] = high_corner[which]
        count = LOW_ROWS[which]
        place = slice(place_low, place_low + count)
        joined[which, STRIP - count : STRIP, 0:breadth] = jnp.where(
            parity == 0, odd[place, :], even[place, :]
        )
        place_low += count
        count = HIGH_ROWS[which]
        place = slice(place_high, place_high + count)
        joined[which, STRIP : STRIP + count, 0:breadth] = jnp.where(
            parity == 0, even[place, :], odd[place, :]
        )
        place_high += count

    zero = jnp.zeros((STRIP, width), jnp.float32)
    values, _ = coefficients(lambda which: joined[which, low_rows, :], handed[SOUTH])
    for index, value in enumerate(values):
        coef[index, low_rows, :] = value
    values, south = coefficients(lambda which: joined[which, high_rows, :], zero)
    for index, value in enumerate(values):
        coef[index, high_rows, :] = value
    row = lax.broadcasted_iota(jnp.int32, zero.shape, 0)
    missing = (
        handed[COEFFICIENTS + 9]
        * (1.0 / SCALE)
        * jnp.where(row == STRIP - 1, pltpu.roll(south, STRIP - 1, 0), 0.0)
    )

    def getter(strip):
        if strip == 0:
            return lambda k: coef[k, low_rows, :]
        if strip == 3:
            return lambda k: coef[k, high_rows, :]
        if strip == 1:
            return lambda k: handed[k]
        return lambda k: handed[COEFFICIENTS + k] + (missing if k in (10, 14) else 0.0)

    getters = [getter(strip) for strip in range(4)]
    inner = [slice(0, STRIP), slice(STRIP, 2 * STRIP)]

    def write(index, strip, value):
        if strip in (1, 2):
            kept[index, inner[strip - 1], :] = value
        else:
            outer[index, low_rows if strip == 0 else high_rows, :] = value

    def read(index, strip):
        if strip in (1, 2):
            return kept[index, inner[strip - 1], :]
        return outer[index, low_rows if strip == 0 else high_rows, :]

    write(0, 0, joined[0, low_rows, :])
    write(0, 3, joined[0, high_rows, :])
    write(0, 1, handed[FIRST])
    write(0, 2, handed[FIRST + 1])
    for order in range(ITERS):
        smoothed = ITERS + 1 + order
        totals = [weighted(getters[strip], read(order, strip)) for strip in range(4)]
        rising = weighted(lambda k: handed[NEAR + k], handed[BASIS + order], (0,))[0]
        falling = weighted(
            lambda k: handed[NEAR + 3 + k], handed[BASIS + KEPT + order], (0,)
        )[0]
        above = [zero, totals[0][2], falling, totals[2][2]]
        below = [totals[1][0], rising, totals[3][0], zero]
        for strip in range(4):
            write(
                smoothed,
                strip,
                getters[strip](9)
                * (
                    totals[strip][1]
                    + row_above(totals[strip][2], above[strip])
                    + row_below(totals[strip][0], below[strip])
                ),
            )
        blocks = [read(smoothed, strip) for strip in range(4)]
        before = [zero, blocks[0], handed[BASIS + KEPT + smoothed], blocks[2]]
        after = [blocks[1], handed[BASIS + smoothed], blocks[3], zero]
        for strip in range(4) if order < ITERS - 1 else (1, 2):
            write(
                order + 1,
                strip,
                applied(
                    getters[strip],
                    blocks[strip],
                    before[strip],
                    after[strip],
                    read(order, strip),
                ),
            )
    totals = tuple(sums[i] for i in range(PRODUCTS))
    for rows in inner:
        totals = gathered(totals, kept, rows, breadth)
    gram[...] = jnp.zeros(gram.shape, jnp.float32)
    for index in range(PRODUCTS):
        total = jnp.sum(jnp.sum(totals[index], axis=0, keepdims=True), axis=1, keepdims=True)
        gram[index : index + 1, :] = jnp.broadcast_to(total, (1, LANES))


def recurrences(gram):
    shift, scale = SHIFT, SCALE
    residual = [1.0]
    direction = []
    steps = [0.0] * ITERS
    rz_before = None
    for order in range(ITERS):
        rz = None
        for i in range(order + 1):
            inner = None
            for j in range(order + 1):
                term = residual[j] * gram[i][j]
                inner = term if inner is None else inner + term
            inner = residual[i] * inner
            rz = inner if rz is None else rz + inner
        if order == 0:
            direction = [1.0]
        else:
            ratio = rz / rz_before
            direction = [
                residual[i] + ratio * direction[i] if i < order else residual[i]
                for i in range(order + 1)
            ]
        image = [0.0] * (order + 2)
        for i in range(order + 1):
            image[i] = image[i] + shift * direction[i]
            image[i + 1] = image[i + 1] + scale * direction[i]
        curvature = None
        for i in range(order + 2):
            inner = None
            for j in range(order + 1):
                term = direction[j] * gram[i][j]
                inner = term if inner is None else inner + term
            inner = image[i] * inner
            curvature = inner if curvature is None else curvature + inner
        step = rz / curvature
        for i in range(order + 1):
            steps[i] = steps[i] + step * direction[i]
        residual = [
            (residual[i] if i < order + 1 else 0.0) - step * image[i]
            for i in range(order + 2)
        ]
        rz_before = rz
    return steps, residual


def combine_kernel(gram_ref, kept, edges, solution_out, residual_out, *scratch):
    solution_ref, residual_ref, left = scratch
    height, breadth = solution_ref.shape
    part = height // PARTS
    gram = [
        [gram_ref[i * ITERS + j : i * ITERS + j + 1, :] for j in range(ITERS)]
        for i in range(ITERS + 1)
    ]
    steps, residual = recurrences(gram)

    def wide(value):
        value = jnp.broadcast_to(value, (STRIP, LANES))
        return jnp.concatenate([value] * (breadth // LANES), axis=1)

    def put(source, rows_from, rows_to):
        total = None
        for j in range(ITERS):
            term = wide(steps[j]) * source[ITERS + 1 + j, rows_from, 0:breadth]
            total = term if total is None else total + term
        solution_ref[rows_to, :] = total
        total = None
        for i in range(ITERS + 1):
            term = wide(residual[i]) * source[i, rows_from, 0:breadth]
            total = term if total is None else total + term
        residual_ref[rows_to, :] = total

    copies = []
    for step in range(PARTS):
        for strip in range(step * part // STRIP, (step + 1) * part // STRIP):
            rows = slice(strip * STRIP, (strip + 1) * STRIP)
            if strip == 0:
                put(edges, slice(0, STRIP), rows)
            elif strip == height // STRIP - 1:
                put(edges, slice(STRIP, 2 * STRIP), rows)
            else:
                put(kept, rows, rows)
        rows = pl.ds(step * part, part)
        for index, (source, target) in enumerate(
            ((solution_ref, solution_out), (residual_ref, residual_out))
        ):
            copy = pltpu.make_async_copy(
                source.at[rows, :], target.at[rows, :], left.at[index, step]
            )
            copy.start()
            copies.append(copy)
    for copy in copies:
        copy.wait()


def params(limit=VMEM_BYTES):
    return pltpu.CompilerParams(vmem_limit_bytes=limit)


def cost(flops, moved):
    return pl.CostEstimate(flops=flops, bytes_accessed=moved, transcendentals=0)


def body(right_side, faces, ratio, centre, offdiag, mask):
    height, breadth = right_side.shape
    width = breadth + LANES
    args = (right_side, mask, centre, ratio, faces, offdiag)
    held = [pltpu.with_memory_space_constraint(a, pltpu.HBM) for a in args]
    f32 = jnp.float32
    gy = lax.axis_size("gy")
    swap = [(0, 1), (1, 0)]
    pairs = [(i, i ^ 1) for i in range(gy) if i ^ 1 < gy]
    between = [(i, (i + 1 ^ 1) - 1) for i in range(1, gy) if (i + 1 ^ 1) - 1 < gy]

    def diagonal(partners):
        return [(2 * a + c, 2 * b + 1 - c) for a, b in partners for c in (0, 1)]

    packed = jax.ShapeDtypeStruct((PACKED, breadth), f32)
    corner = jax.ShapeDtypeStruct((STRIP, LANES), f32)
    columns = jax.ShapeDtypeStruct((height, LANES), f32)
    even, odd, even_corner, odd_corner = pl.pallas_call(
        pack_kernel,
        in_specs=[pl.BlockSpec(memory_space=pltpu.HBM)] * len(args),
        out_shape=(packed, packed, corner, corner),
        scratch_shapes=[
            pltpu.VMEM((2,) + a.shape[:-2] + (STRIP, breadth), a.dtype) for a in args
        ]
        + [pltpu.SemaphoreType.DMA((len(args), 2))],
        compiler_params=params(PACK_VMEM_BYTES),
        cost_estimate=cost(0, 4 * 4 * PACKED * breadth),
        name="pack",
    )(*held)
    columns = pl.pallas_call(
        columns_kernel,
        in_specs=[pl.BlockSpec(memory_space=pltpu.VMEM)] * len(args)
        + [pl.BlockSpec(memory_space=pl.ANY)],
        out_shape=columns,
        compiler_params=params(PACK_VMEM_BYTES),
        cost_estimate=cost(0, 4 * FIELDS * height * LANES),
        name="columns",
    )(*args, odd_corner)
    columns = lax.ppermute(columns, "gx", swap)
    even_in = lax.ppermute(even, "gy", pairs)
    even_corner = lax.ppermute(even_corner, ("gy", "gx"), diagonal(pairs))
    odd_in = lax.ppermute(odd, "gy", between)
    odd_corner = lax.ppermute(odd_corner, ("gy", "gx"), diagonal(between))

    cells = height * width
    kept, sums, handed = pl.pallas_call(
        tile_kernel,
        out_shape=(
            jax.ShapeDtypeStruct((KEPT, height, width), f32),
            jax.ShapeDtypeStruct((PRODUCTS, STRIP, LANES), f32),
            jax.ShapeDtypeStruct((HANDED, STRIP, width), f32),
        ),
        scratch_shapes=[
            pltpu.VMEM((COEFFICIENTS, height, width), f32),
            pltpu.VMEM((FIELDS, height, LANES), f32),
        ],
        compiler_params=params(TILE_VMEM_BYTES),
        cost_estimate=cost(100 * cells, 4 * cells * (FIELDS + KEPT)),
        name="tile",
    )(*args, columns)

    sums, even_in, odd_in, even_corner, odd_corner = lax.optimization_barrier(
        (sums, even_in, odd_in, even_corner, odd_corner)
    )
    rows = 2 * STRIP
    edges, gram = pl.pallas_call(
        edge_kernel,
        out_shape=(
            jax.ShapeDtypeStruct((KEPT, rows, width), f32),
            jax.ShapeDtypeStruct((2 * STRIP, LANES), f32),
        ),
        scratch_shapes=[
            pltpu.VMEM((FIELDS, rows, width), f32),
            pltpu.VMEM((COEFFICIENTS, rows, width), f32),
            pltpu.VMEM((KEPT, rows, width), f32),
        ],
        compiler_params=params(),
        cost_estimate=cost(200 * rows * width, 4 * rows * width * (FIELDS + KEPT)),
        name="edge",
    )(handed, even_in, odd_in, even_corner, odd_corner, sums)

    gram = gram + lax.ppermute(gram, "gx", swap)
    reach = 1
    while reach < gy:
        gram = gram + lax.ppermute(gram, "gy", [(i, i ^ reach) for i in range(gy)])
        reach *= 2

    tile = jax.ShapeDtypeStruct((height, breadth), f32)
    return pl.pallas_call(
        combine_kernel,
        out_specs=(pl.BlockSpec(memory_space=pltpu.HBM),) * 2,
        out_shape=(tile, tile),
        scratch_shapes=[pltpu.VMEM(tile.shape, f32)] * 2
        + [pltpu.SemaphoreType.DMA((2, PARTS))],
        compiler_params=params(),
        cost_estimate=cost(14 * height * breadth, 4 * height * breadth * (KEPT + 2)),
        name="combine",
    )(gram, kept, edges)


def solution(mesh):
    return jax.shard_map(
        body,
        mesh=mesh,
        in_specs=(
            P(("members", "gy"), "gx"),
            P(None, "gy", "gx"),
            P("gy", "gx"),
            P("gy", "gx"),
            P(None, "gy", "gx"),
            P("gy", "gx"),
        ),
        out_specs=(P(("members", "gy"), "gx"), P(("members", "gy"), "gx")),
        check_vma=False,
    )
```

```python
import functools

import jax
import jax.numpy as jnp
from jax import lax
from jax.experimental import pallas as pl
from jax.experimental.pallas import tpu as pltpu
from jax.sharding import PartitionSpec as P

ITERS = 3
SHIFT = 1.0
SCALE = 4.0
LANES = 128
STRIP = 8

neighbour_steps = [(-1, -1), (-1, 0), (-1, 1), (0, -1), (0, 1), (1, -1), (1, 0), (1, 1)]

FIELDS = 6 + len(neighbour_steps)
REACH = 2 * ITERS
LOW_ROWS = [REACH, REACH - 1, REACH - 1, REACH - 2, REACH - 2, REACH - 2] + [
    REACH - 1 + down for down, _ in neighbour_steps
]
HIGH_ROWS = [REACH, REACH - 1, REACH - 1, REACH - 2, REACH - 2, REACH - 1] + [
    REACH - 1 - down for down, _ in neighbour_steps
]
PACKED = max(sum(LOW_ROWS), sum(HIGH_ROWS))
PRODUCTS = (ITERS + 1) * ITERS
KEPT = 2 * ITERS + 1
SLOT = 8
PARTS = 4
COEFFICIENTS = 15
NEAR = 2 * COEFFICIENTS
SOUTH = NEAR + 6
FIRST = SOUTH + 1
BASIS = FIRST + 2
HANDED = BASIS + 2 * KEPT
TILE_VMEM_BYTES = 40 * 1024 * 1024
VMEM_BYTES = 32 * 1024 * 1024
PACK_VMEM_BYTES = 16 * 1024 * 1024


def field(refs, which, rows):
    right_side, mask, centre, ratio, faces, offdiag = refs
    if which == 0:
        return mask[rows, :].astype(jnp.float32) * right_side[rows, :]
    if which == 1:
        return mask[rows, :].astype(jnp.float32)
    if which == 2:
        return centre[rows, :]
    if which == 3:
        return ratio[rows, :]
    if which < 6:
        return faces[which - 4, rows, :]
    return offdiag[which - 6, rows, :]


def stacked(place, count, breadth):
    for block in range(breadth // LANES):
        start = block * PACKED + place
        yield slice(start, start + count), slice(block * LANES, (block + 1) * LANES)


def trimmed(out, refs, counts, at_end):
    breadth = out.shape[0] // PACKED * LANES
    place = 0
    for which, count in enumerate(counts):
        rows = slice(STRIP - count, STRIP) if at_end else slice(0, count)
        value = field(refs, which, rows)
        for target, lanes in stacked(place, count, breadth):
            out[target, :] = value[:, lanes]
        place += count
    if place < PACKED:
        zero = jnp.zeros((PACKED - place, LANES), jnp.float32)
        for target, _ in stacked(place, PACKED - place, breadth):
            out[target, :] = zero


def lanes_of(shape):
    return lax.broadcasted_iota(jnp.int32, shape, len(shape) - 1)


def beside(refs, which, rows, side):
    breadth = refs[0].shape[1]
    west = field([ref.at[..., 0:LANES] for ref in refs], which, rows)
    east = field([ref.at[..., breadth - LANES : breadth] for ref in refs], which, rows)
    return jnp.where(side == 0, east, west)


def squeezed(near, side):
    start = jnp.where(side == 0, SLOT, 0)
    total = None
    for which in range(FIELDS):
        block = pltpu.roll(near(which), start + SLOT * which, 1)
        if total is None:
            lane = lanes_of(block.shape)
            total = jnp.zeros(block.shape, jnp.float32)
        inside = (lane >= SLOT * which) & (lane < SLOT * (which + 1))
        total = jnp.where(inside, block, total)
    return total


def spread(block, side):
    lane = lanes_of(block.shape)
    start = jnp.where(side == 0, LANES, LANES - SLOT)
    first = jnp.where(side == 0, 0, LANES - SLOT)
    inside = ((lane >= first) & (lane < first + SLOT)).astype(jnp.float32)
    return [
        pltpu.roll(block, start - SLOT * which, 1) * inside for which in range(FIELDS)
    ]


def pack_kernel(*refs):
    args = refs[0:6]
    even, odd, even_corner, odd_corner = refs[6:10]
    ends, arrived = refs[10:16], refs[16]
    height, breadth = args[0].shape
    side = lax.axis_index("gx")
    parity = lax.rem(lax.axis_index("gy"), 2)
    copies = []
    for index, (arg, end) in enumerate(zip(args, ends)):
        lead = (slice(None),) * (len(arg.shape) - 2)
        for which, start in enumerate((0, height - STRIP)):
            copies.append(
                pltpu.make_async_copy(
                    arg.at[lead + (pl.ds(start, STRIP), slice(None))],
                    end.at[which],
                    arrived.at[index, which],
                )
            )
    for copy in copies:
        copy.start()
    for copy in copies:
        copy.wait()
    first = [end.at[0] for end in ends]
    last = [end.at[1] for end in ends]
    rows = slice(0, STRIP)
    corner_first = squeezed(lambda which: beside(first, which, rows, side), side)
    corner_last = squeezed(lambda which: beside(last, which, rows, side), side)
    even_corner[...] = jnp.where(parity == 0, corner_last, corner_first)
    odd_corner[...] = jnp.where(parity == 0, corner_first, corner_last)

    @pl.when(parity == 0)
    def _():
        trimmed(even, last, LOW_ROWS, True)
        trimmed(odd, first, HIGH_ROWS, False)

    @pl.when(parity != 0)
    def _():
        trimmed(even, first, HIGH_ROWS, False)
        trimmed(odd, last, LOW_ROWS, True)


def columns_kernel(*refs):
    args, columns = refs[0:6], refs[7]
    side = lax.axis_index("gx")
    columns[...] = squeezed(lambda which: beside(args, which, slice(None), side), side)


def row_above(block, before):
    row = lax.broadcasted_iota(jnp.int32, block.shape, 0)
    return jnp.where(row == 0, pltpu.roll(before, 1, 0), pltpu.roll(block, 1, 0))


def row_below(block, after):
    row = lax.broadcasted_iota(jnp.int32, block.shape, 0)
    last = STRIP - 1
    return jnp.where(row == last, pltpu.roll(after, last, 0), pltpu.roll(block, last, 0))


def strip_rows(strip):
    return pl.ds(pl.multiple_of(strip * STRIP, STRIP), STRIP)


def west_of(block):
    return pltpu.roll(block, 1, 1)


def east_of(block):
    return pltpu.roll(block, block.shape[1] - 1, 1)


def coefficients(get, south_after):
    result = [None] * COEFFICIENTS
    wet = get(1)
    result[4] = get(2)
    for index, (down, across) in enumerate(neighbour_steps):
        weight = get(6 + index)
        if across == 1:
            weight = west_of(weight)
        elif across == -1:
            weight = east_of(weight)
        result[(down + 1) * 3 + across + 1] = weight
    west = get(4)
    south = get(5)
    east = east_of(west)
    north = row_below(south, south_after)
    scaled = wet * (1.0 / SCALE)
    result[9] = wet
    result[10] = scaled * (west + east + south + north + get(3))
    result[11] = scaled * west
    result[12] = scaled * east
    result[13] = scaled * south
    result[14] = scaled * north
    return result, south


def weighted(get, block, downs=(0, 1, 2)):
    left, right = east_of(block), west_of(block)
    return [
        get(down * 3) * left + get(down * 3 + 1) * block + get(down * 3 + 2) * right
        for down in downs
    ]


def applied(get, block, before, after, old):
    return (
        get(10) * block
        - get(11) * west_of(block)
        - get(12) * east_of(block)
        - get(13) * row_above(block, before)
        - get(14) * row_below(block, after)
        - (SHIFT / SCALE) * old
    )


def gathered(totals, kept, rows, breadth):
    result = list(totals)
    for start in range(0, breadth, LANES):
        bases = [kept[i, rows, start : start + LANES] for i in range(KEPT)]
        for i in range(ITERS + 1):
            for j in range(ITERS):
                result[i * ITERS + j] += bases[i] * bases[ITERS + 1 + j]
    return tuple(result)


def krylov(load, strips, coef, kept):
    width = kept.shape[2]
    zero = jnp.zeros((STRIP, width), jnp.float32)

    def prepare(step, south_after):
        strip = strips - 1 - step
        rows = strip_rows(strip)
        kept[0, rows, :] = load(0, strip)
        values, south = coefficients(lambda which: load(which, strip), south_after)
        for index, value in enumerate(values):
            coef[index, rows, :] = value
        return south

    lax.fori_loop(0, strips, prepare, zero, unroll=strips)

    for order in range(ITERS):
        smoothed = ITERS + 1 + order

        def smooth(strip, carried):
            above, partial = carried
            rows = strip_rows(strip)
            totals = weighted(lambda k: coef[k, rows, :], kept[order, rows, :])
            row = lax.broadcasted_iota(jnp.int32, totals[0].shape, 0)
            rising = pltpu.roll(totals[0], STRIP - 1, 0)
            falling = pltpu.roll(totals[2], 1, 0)
            done = strip_rows(jnp.maximum(strip - 1, 0))
            kept[smoothed, done, :] = coef[9, done, :] * (
                partial + jnp.where(row == STRIP - 1, rising, 0.0)
            )
            partial = (
                totals[1]
                + jnp.where(row == 0, above, falling)
                + jnp.where(row == STRIP - 1, 0.0, rising)
            )
            return falling, partial

        _, partial = lax.fori_loop(0, strips, smooth, (zero, zero), unroll=strips)
        done = slice((strips - 1) * STRIP, strips * STRIP)
        kept[smoothed, done, :] = coef[9, done, :] * partial

        def operate(strip, carried):
            rows = strip_rows(strip)
            kept[order + 1, rows, :] = applied(
                lambda k: coef[k, rows, :],
                kept[smoothed, rows, :],
                kept[smoothed, strip_rows(jnp.maximum(strip - 1, 0)), :],
                kept[smoothed, strip_rows(jnp.minimum(strip + 1, strips - 1)), :],
                kept[order, rows, :],
            )
            return carried

        lax.fori_loop(0, strips, operate, 0, unroll=strips)


def tile_kernel(*refs):
    own, columns, kept, sums, handed, coef, wide = refs[0:6], *refs[6:12]
    strips = kept.shape[1] // STRIP
    side = lax.axis_index("gx")
    for which, block in enumerate(spread(columns[...], side)):
        wide[which] = block

    def load(which, strip):
        rows = strip_rows(strip)
        return jnp.concatenate([field(own, which, rows), wide[which, rows, :]], axis=1)

    krylov(load, strips, coef, kept)
    zero = jnp.zeros((STRIP, LANES), jnp.float32)
    breadth = kept.shape[2] - LANES
    totals = lax.fori_loop(
        1,
        strips - 1,
        lambda strip, totals: gathered(totals, kept, strip_rows(strip), breadth),
        (zero,) * PRODUCTS,
        unroll=7,
    )
    for index in range(PRODUCTS):
        sums[index] = totals[index]
    first, last = slice(0, STRIP), slice((strips - 1) * STRIP, strips * STRIP)
    second, third = slice(STRIP, 2 * STRIP), slice((strips - 2) * STRIP, (strips - 1) * STRIP)
    for index in range(COEFFICIENTS):
        handed[index] = coef[index, first, :]
        handed[COEFFICIENTS + index] = coef[index, last, :]
    for index in range(3):
        handed[NEAR + index] = coef[index, second, :]
        handed[NEAR + 3 + index] = coef[6 + index, third, :]
    handed[SOUTH] = load(5, 0)
    handed[FIRST] = kept[0, first, :]
    handed[FIRST + 1] = kept[0, last, :]
    for index in range(KEPT):
        handed[BASIS + index] = kept[index, second, :]
        handed[BASIS + KEPT + index] = kept[index, third, :]


def edge_kernel(
    handed, even, odd, even_corner, odd_corner, sums, kept, gram, joined, coef, outer
):
    breadth = even.shape[0] // PACKED * LANES
    width = breadth + LANES
    side = lax.axis_index("gx")
    parity = lax.rem(lax.axis_index("gy"), 2)
    low_corner = spread(jnp.where(parity == 0, odd_corner[...], even_corner[...]), side)
    high_corner = spread(jnp.where(parity == 0, even_corner[...], odd_corner[...]), side)
    low_rows, high_rows = slice(0, STRIP), slice(STRIP, 2 * STRIP)
    place_low, place_high = 0, 0
    for which in range(FIELDS):
        joined[which, :, 0:breadth] = jnp.zeros((2 * STRIP, breadth), jnp.float32)
        joined[which, low_rows, breadth:width] = low_corner[which]
        joined[which, high_rows, breadth:width] = high_corner[which]
        count = LOW_ROWS[which]
        for place, lanes in stacked(place_low, count, breadth):
            joined[which, STRIP - count : STRIP, lanes] = jnp.where(
                parity == 0, odd[place, :], even[place, :]
            )
        place_low += count
        count = HIGH_ROWS[which]
        for place, lanes in stacked(place_high, count, breadth):
            joined[which, STRIP : STRIP + count, lanes] = jnp.where(
                parity == 0, even[place, :], odd[place, :]
            )
        place_high += count

    zero = jnp.zeros((STRIP, width), jnp.float32)
    values, _ = coefficients(lambda which: joined[which, low_rows, :], handed[SOUTH])
    for index, value in enumerate(values):
        coef[index, low_rows, :] = value
    values, south = coefficients(lambda which: joined[which, high_rows, :], zero)
    for index, value in enumerate(values):
        coef[index, high_rows, :] = value
    row = lax.broadcasted_iota(jnp.int32, zero.shape, 0)
    missing = (
        handed[COEFFICIENTS + 9]
        * (1.0 / SCALE)
        * jnp.where(row == STRIP - 1, pltpu.roll(south, STRIP - 1, 0), 0.0)
    )

    def getter(strip):
        if strip == 0:
            return lambda k: coef[k, low_rows, :]
        if strip == 3:
            return lambda k: coef[k, high_rows, :]
        if strip == 1:
            return lambda k: handed[k]
        return lambda k: handed[COEFFICIENTS + k] + (missing if k in (10, 14) else 0.0)

    getters = [getter(strip) for strip in range(4)]
    inner = [slice(0, STRIP), slice(STRIP, 2 * STRIP)]

    def write(index, strip, value):
        if strip in (1, 2):
            kept[index, inner[strip - 1], :] = value
        else:
            outer[index, low_rows if strip == 0 else high_rows, :] = value

    def read(index, strip):
        if strip in (1, 2):
            return kept[index, inner[strip - 1], :]
        return outer[index, low_rows if strip == 0 else high_rows, :]

    write(0, 0, joined[0, low_rows, :])
    write(0, 3, joined[0, high_rows, :])
    write(0, 1, handed[FIRST])
    write(0, 2, handed[FIRST + 1])
    for order in range(ITERS):
        smoothed = ITERS + 1 + order
        totals = [weighted(getters[strip], read(order, strip)) for strip in range(4)]
        rising = weighted(lambda k: handed[NEAR + k], handed[BASIS + order], (0,))[0]
        falling = weighted(
            lambda k: handed[NEAR + 3 + k], handed[BASIS + KEPT + order], (0,)
        )[0]
        above = [zero, totals[0][2], falling, totals[2][2]]
        below = [totals[1][0], rising, totals[3][0], zero]
        for strip in range(4):
            write(
                smoothed,
                strip,
                getters[strip](9)
                * (
                    totals[strip][1]
                    + row_above(totals[strip][2], above[strip])
                    + row_below(totals[strip][0], below[strip])
                ),
            )
        blocks = [read(smoothed, strip) for strip in range(4)]
        before = [zero, blocks[0], handed[BASIS + KEPT + smoothed], blocks[2]]
        after = [blocks[1], handed[BASIS + smoothed], blocks[3], zero]
        for strip in range(4) if order < ITERS - 1 else (1, 2):
            write(
                order + 1,
                strip,
                applied(
                    getters[strip],
                    blocks[strip],
                    before[strip],
                    after[strip],
                    read(order, strip),
                ),
            )
    totals = tuple(sums[i] for i in range(PRODUCTS))
    for rows in inner:
        totals = gathered(totals, kept, rows, breadth)
    gram[...] = jnp.zeros(gram.shape, jnp.float32)
    for index in range(PRODUCTS):
        total = jnp.sum(jnp.sum(totals[index], axis=0, keepdims=True), axis=1, keepdims=True)
        gram[index : index + 1, :] = jnp.broadcast_to(total, (1, LANES))


def recurrences(gram):
    shift, scale = SHIFT, SCALE
    residual = [1.0]
    direction = []
    steps = [0.0] * ITERS
    rz_before = None
    for order in range(ITERS):
        rz = None
        for i in range(order + 1):
            inner = None
            for j in range(order + 1):
                term = residual[j] * gram[i][j]
                inner = term if inner is None else inner + term
            inner = residual[i] * inner
            rz = inner if rz is None else rz + inner
        if order == 0:
            direction = [1.0]
        else:
            ratio = rz / rz_before
            direction = [
                residual[i] + ratio * direction[i] if i < order else residual[i]
                for i in range(order + 1)
            ]
        image = [0.0] * (order + 2)
        for i in range(order + 1):
            image[i] = image[i] + shift * direction[i]
            image[i + 1] = image[i + 1] + scale * direction[i]
        curvature = None
        for i in range(order + 2):
            inner = None
            for j in range(order + 1):
                term = direction[j] * gram[i][j]
                inner = term if inner is None else inner + term
            inner = image[i] * inner
            curvature = inner if curvature is None else curvature + inner
        step = rz / curvature
        for i in range(order + 1):
            steps[i] = steps[i] + step * direction[i]
        residual = [
            (residual[i] if i < order + 1 else 0.0) - step * image[i]
            for i in range(order + 2)
        ]
        rz_before = rz
    return steps, residual


def combine_kernel(gram_ref, kept, edges, solution_out, residual_out, *scratch):
    solution_ref, residual_ref, left = scratch
    height, breadth = solution_ref.shape
    part = height // PARTS
    gram = [
        [gram_ref[i * ITERS + j : i * ITERS + j + 1, :] for j in range(ITERS)]
        for i in range(ITERS + 1)
    ]
    steps, residual = recurrences(gram)

    def wide(value):
        value = jnp.broadcast_to(value, (STRIP, LANES))
        return jnp.concatenate([value] * (breadth // LANES), axis=1)

    def put(source, rows_from, rows_to):
        total = None
        for j in range(ITERS):
            term = wide(steps[j]) * source[ITERS + 1 + j, rows_from, 0:breadth]
            total = term if total is None else total + term
        solution_ref[rows_to, :] = total
        total = None
        for i in range(ITERS + 1):
            term = wide(residual[i]) * source[i, rows_from, 0:breadth]
            total = term if total is None else total + term
        residual_ref[rows_to, :] = total

    copies = []
    for step in range(PARTS):
        for strip in range(step * part // STRIP, (step + 1) * part // STRIP):
            rows = slice(strip * STRIP, (strip + 1) * STRIP)
            if strip == 0:
                put(edges, slice(0, STRIP), rows)
            elif strip == height // STRIP - 1:
                put(edges, slice(STRIP, 2 * STRIP), rows)
            else:
                put(kept, rows, rows)
        rows = pl.ds(step * part, part)
        for index, (source, target) in enumerate(
            ((solution_ref, solution_out), (residual_ref, residual_out))
        ):
            copy = pltpu.make_async_copy(
                source.at[rows, :], target.at[rows, :], left.at[index, step]
            )
            copy.start()
            copies.append(copy)
    for copy in copies:
        copy.wait()


def params(limit=VMEM_BYTES):
    return pltpu.CompilerParams(vmem_limit_bytes=limit)


def cost(flops, moved):
    return pl.CostEstimate(flops=flops, bytes_accessed=moved, transcendentals=0)


def body(right_side, faces, ratio, centre, offdiag, mask):
    height, breadth = right_side.shape
    width = breadth + LANES
    args = (right_side, mask, centre, ratio, faces, offdiag)
    held = [pltpu.with_memory_space_constraint(a, pltpu.HBM) for a in args]
    f32 = jnp.float32
    gy = lax.axis_size("gy")
    swap = [(0, 1), (1, 0)]
    pairs = [(i, i ^ 1) for i in range(gy) if i ^ 1 < gy]
    between = [(i, (i + 1 ^ 1) - 1) for i in range(1, gy) if (i + 1 ^ 1) - 1 < gy]

    def diagonal(partners):
        return [(2 * a + c, 2 * b + 1 - c) for a, b in partners for c in (0, 1)]

    packed = jax.ShapeDtypeStruct((breadth // LANES * PACKED, LANES), f32)
    corner = jax.ShapeDtypeStruct((STRIP, LANES), f32)
    columns = jax.ShapeDtypeStruct((height, LANES), f32)
    even, odd, even_corner, odd_corner = pl.pallas_call(
        pack_kernel,
        in_specs=[pl.BlockSpec(memory_space=pltpu.HBM)] * len(args),
        out_shape=(packed, packed, corner, corner),
        scratch_shapes=[
            pltpu.VMEM((2,) + a.shape[:-2] + (STRIP, breadth), a.dtype) for a in args
        ]
        + [pltpu.SemaphoreType.DMA((len(args), 2))],
        compiler_params=params(PACK_VMEM_BYTES),
        cost_estimate=cost(0, 4 * 4 * PACKED * breadth),
        name="pack",
    )(*held)
    columns = pl.pallas_call(
        columns_kernel,
        in_specs=[pl.BlockSpec(memory_space=pltpu.VMEM)] * len(args)
        + [pl.BlockSpec(memory_space=pl.ANY)],
        out_shape=columns,
        compiler_params=params(PACK_VMEM_BYTES),
        cost_estimate=cost(0, 4 * FIELDS * height * LANES),
        name="columns",
    )(*args, odd_corner)
    columns = lax.ppermute(columns, "gx", swap)
    even_in = lax.ppermute(even, "gy", pairs)
    even_corner = lax.ppermute(even_corner, ("gy", "gx"), diagonal(pairs))
    odd_in = lax.ppermute(odd, "gy", between)
    odd_corner = lax.ppermute(odd_corner, ("gy", "gx"), diagonal(between))

    cells = height * width
    kept, sums, handed = pl.pallas_call(
        tile_kernel,
        out_shape=(
            jax.ShapeDtypeStruct((KEPT, height, width), f32),
            jax.ShapeDtypeStruct((PRODUCTS, STRIP, LANES), f32),
            jax.ShapeDtypeStruct((HANDED, STRIP, width), f32),
        ),
        scratch_shapes=[
            pltpu.VMEM((COEFFICIENTS, height, width), f32),
            pltpu.VMEM((FIELDS, height, LANES), f32),
        ],
        compiler_params=params(TILE_VMEM_BYTES),
        cost_estimate=cost(100 * cells, 4 * cells * (FIELDS + KEPT)),
        name="tile",
    )(*args, columns)

    sums, even_in, odd_in, even_corner, odd_corner = lax.optimization_barrier(
        (sums, even_in, odd_in, even_corner, odd_corner)
    )
    rows = 2 * STRIP
    edges, gram = pl.pallas_call(
        edge_kernel,
        out_shape=(
            jax.ShapeDtypeStruct((KEPT, rows, width), f32),
            jax.ShapeDtypeStruct((2 * STRIP, LANES), f32),
        ),
        scratch_shapes=[
            pltpu.VMEM((FIELDS, rows, width), f32),
            pltpu.VMEM((COEFFICIENTS, rows, width), f32),
            pltpu.VMEM((KEPT, rows, width), f32),
        ],
        compiler_params=params(),
        cost_estimate=cost(200 * rows * width, 4 * rows * width * (FIELDS + KEPT)),
        name="edge",
    )(handed, even_in, odd_in, even_corner, odd_corner, sums)

    gram = gram + lax.ppermute(gram, "gx", swap)
    reach = 1
    while reach < gy:
        gram = gram + lax.ppermute(gram, "gy", [(i, i ^ reach) for i in range(gy)])
        reach *= 2

    tile = jax.ShapeDtypeStruct((height, breadth), f32)
    return pl.pallas_call(
        combine_kernel,
        out_specs=(pl.BlockSpec(memory_space=pltpu.HBM),) * 2,
        out_shape=(tile, tile),
        scratch_shapes=[pltpu.VMEM(tile.shape, f32)] * 2
        + [pltpu.SemaphoreType.DMA((2, PARTS))],
        compiler_params=params(),
        cost_estimate=cost(14 * height * breadth, 4 * height * breadth * (KEPT + 2)),
        name="combine",
    )(gram, kept, edges)


def solution(mesh):
    return jax.shard_map(
        body,
        mesh=mesh,
        in_specs=(
            P(("members", "gy"), "gx"),
            P(None, "gy", "gx"),
            P("gy", "gx"),
            P("gy", "gx"),
            P(None, "gy", "gx"),
            P("gy", "gx"),
        ),
        out_specs=(P(("members", "gy"), "gx"), P(("members", "gy"), "gx")),
        check_vma=False,
    )
```

```python
import functools

import jax
import jax.numpy as jnp
from jax import lax
from jax.experimental import pallas as pl
from jax.experimental.pallas import tpu as pltpu
from jax.sharding import PartitionSpec as P

ITERS = 3
SHIFT = 0.7
SCALE = 4.0
LANES = 128
STRIP = 8

neighbour_steps = [(-1, -1), (-1, 0), (-1, 1), (0, -1), (0, 1), (1, -1), (1, 0), (1, 1)]

FIELDS = 6 + len(neighbour_steps)
REACH = 2 * ITERS
LOW_ROWS = [REACH, REACH - 1, REACH - 1, REACH - 2, REACH - 2, REACH - 2] + [
    REACH - 1 + down for down, _ in neighbour_steps
]
HIGH_ROWS = [REACH, REACH - 1, REACH - 1, REACH - 2, REACH - 2, REACH - 1] + [
    REACH - 1 - down for down, _ in neighbour_steps
]
PACKED = max(sum(LOW_ROWS), sum(HIGH_ROWS))
PRODUCTS = (ITERS + 1) * ITERS
KEPT = 2 * ITERS + 1
SLOT = 8
PARTS = 4
COEFFICIENTS = 15
NEAR = 2 * COEFFICIENTS
SOUTH = NEAR + 6
FIRST = SOUTH + 1
BASIS = FIRST + 2
HANDED = BASIS + 2 * KEPT
TILE_VMEM_BYTES = 40 * 1024 * 1024
VMEM_BYTES = 32 * 1024 * 1024
PACK_VMEM_BYTES = 16 * 1024 * 1024


def field(refs, which, rows):
    right_side, mask, centre, ratio, faces, offdiag = refs
    if which == 0:
        return mask[rows, :].astype(jnp.float32) * right_side[rows, :]
    if which == 1:
        return mask[rows, :].astype(jnp.float32)
    if which == 2:
        return centre[rows, :]
    if which == 3:
        return ratio[rows, :]
    if which < 6:
        return faces[which - 4, rows, :]
    return offdiag[which - 6, rows, :]


def stacked(place, count, breadth):
    for block in range(breadth // LANES):
        start = block * PACKED + place
        yield slice(start, start + count), slice(block * LANES, (block + 1) * LANES)


def trimmed(out, refs, counts, at_end):
    breadth = out.shape[0] // PACKED * LANES
    place = 0
    for which, count in enumerate(counts):
        rows = slice(STRIP - count, STRIP) if at_end else slice(0, count)
        value = field(refs, which, rows)
        for target, lanes in stacked(place, count, breadth):
            out[target, :] = value[:, lanes]
        place += count
    if place < PACKED:
        zero = jnp.zeros((PACKED - place, LANES), jnp.float32)
        for target, _ in stacked(place, PACKED - place, breadth):
            out[target, :] = zero


def lanes_of(shape):
    return lax.broadcasted_iota(jnp.int32, shape, len(shape) - 1)


def beside(refs, which, rows, side):
    breadth = refs[0].shape[1]
    west = field([ref.at[..., 0:LANES] for ref in refs], which, rows)
    east = field([ref.at[..., breadth - LANES : breadth] for ref in refs], which, rows)
    return jnp.where(side == 0, east, west)


def squeezed(near, side):
    start = jnp.where(side == 0, SLOT, 0)
    total = None
    for which in range(FIELDS):
        block = pltpu.roll(near(which), start + SLOT * which, 1)
        if total is None:
            lane = lanes_of(block.shape)
            total = jnp.zeros(block.shape, jnp.float32)
        inside = (lane >= SLOT * which) & (lane < SLOT * (which + 1))
        total = jnp.where(inside, block, total)
    return total


def spread(block, side):
    lane = lanes_of(block.shape)
    start = jnp.where(side == 0, LANES, LANES - SLOT)
    first = jnp.where(side == 0, 0, LANES - SLOT)
    inside = ((lane >= first) & (lane < first + SLOT)).astype(jnp.float32)
    return [
        pltpu.roll(block, start - SLOT * which, 1) * inside for which in range(FIELDS)
    ]


def pack_kernel(*refs):
    args = refs[0:6]
    even, odd, even_corner, odd_corner = refs[6:10]
    ends, arrived = refs[10:16], refs[16]
    height, breadth = args[0].shape
    side = lax.axis_index("gx")
    parity = lax.rem(lax.axis_index("gy"), 2)
    copies = []
    for index, (arg, end) in enumerate(zip(args, ends)):
        lead = (slice(None),) * (len(arg.shape) - 2)
        for which, start in enumerate((0, height - STRIP)):
            copies.append(
                pltpu.make_async_copy(
                    arg.at[lead + (pl.ds(start, STRIP), slice(None))],
                    end.at[which],
                    arrived.at[index, which],
                )
            )
    for copy in copies:
        copy.start()
    for copy in copies:
        copy.wait()
    first = [end.at[0] for end in ends]
    last = [end.at[1] for end in ends]
    rows = slice(0, STRIP)
    corner_first = squeezed(lambda which: beside(first, which, rows, side), side)
    corner_last = squeezed(lambda which: beside(last, which, rows, side), side)
    even_corner[...] = jnp.where(parity == 0, corner_last, corner_first)
    odd_corner[...] = jnp.where(parity == 0, corner_first, corner_last)

    @pl.when(parity == 0)
    def _():
        trimmed(even, last, LOW_ROWS, True)
        trimmed(odd, first, HIGH_ROWS, False)

    @pl.when(parity != 0)
    def _():
        trimmed(even, first, HIGH_ROWS, False)
        trimmed(odd, last, LOW_ROWS, True)


def columns_kernel(*refs):
    args, columns = refs[0:6], refs[7]
    side = lax.axis_index("gx")
    columns[...] = squeezed(lambda which: beside(args, which, slice(None), side), side)


def row_above(block, before):
    row = lax.broadcasted_iota(jnp.int32, block.shape, 0)
    return jnp.where(row == 0, pltpu.roll(before, 1, 0), pltpu.roll(block, 1, 0))


def row_below(block, after):
    row = lax.broadcasted_iota(jnp.int32, block.shape, 0)
    last = STRIP - 1
    return jnp.where(row == last, pltpu.roll(after, last, 0), pltpu.roll(block, last, 0))


def strip_rows(strip):
    return pl.ds(pl.multiple_of(strip * STRIP, STRIP), STRIP)


def west_of(block):
    return pltpu.roll(block, 1, 1)


def east_of(block):
    return pltpu.roll(block, block.shape[1] - 1, 1)


def coefficients(get, south_after):
    result = [None] * COEFFICIENTS
    wet = get(1)
    result[4] = get(2)
    for index, (down, across) in enumerate(neighbour_steps):
        weight = get(6 + index)
        if across == 1:
            weight = west_of(weight)
        elif across == -1:
            weight = east_of(weight)
        result[(down + 1) * 3 + across + 1] = weight
    west = get(4)
    south = get(5)
    east = east_of(west)
    north = row_below(south, south_after)
    scaled = wet * (1.0 / SCALE)
    result[9] = wet
    result[10] = scaled * (west + east + south + north + get(3))
    result[11] = scaled * west
    result[12] = scaled * east
    result[13] = scaled * south
    result[14] = scaled * north
    return result, south


def weighted(get, block, downs=(0, 1, 2)):
    left, right = east_of(block), west_of(block)
    return [
        get(down * 3) * left + get(down * 3 + 1) * block + get(down * 3 + 2) * right
        for down in downs
    ]


def applied(get, block, before, after, old):
    return (
        get(10) * block
        - get(11) * west_of(block)
        - get(12) * east_of(block)
        - get(13) * row_above(block, before)
        - get(14) * row_below(block, after)
        - (SHIFT / SCALE) * old
    )


def gathered(totals, kept, rows, breadth):
    result = list(totals)
    for start in range(0, breadth, LANES):
        bases = [kept[i, rows, start : start + LANES] for i in range(KEPT)]
        for i in range(ITERS + 1):
            for j in range(ITERS):
                result[i * ITERS + j] += bases[i] * bases[ITERS + 1 + j]
    return tuple(result)


def krylov(load, strips, coef, kept):
    width = kept.shape[2]
    zero = jnp.zeros((STRIP, width), jnp.float32)

    def prepare(step, south_after):
        strip = strips - 1 - step
        rows = strip_rows(strip)
        kept[0, rows, :] = load(0, strip)
        values, south = coefficients(lambda which: load(which, strip), south_after)
        for index, value in enumerate(values):
            coef[index, rows, :] = value
        return south

    lax.fori_loop(0, strips, prepare, zero, unroll=strips)

    for order in range(ITERS):
        smoothed = ITERS + 1 + order

        def smooth(strip, carried):
            above, partial = carried
            rows = strip_rows(strip)
            totals = weighted(lambda k: coef[k, rows, :], kept[order, rows, :])
            row = lax.broadcasted_iota(jnp.int32, totals[0].shape, 0)
            rising = pltpu.roll(totals[0], STRIP - 1, 0)
            falling = pltpu.roll(totals[2], 1, 0)
            done = strip_rows(jnp.maximum(strip - 1, 0))
            kept[smoothed, done, :] = coef[9, done, :] * (
                partial + jnp.where(row == STRIP - 1, rising, 0.0)
            )
            partial = (
                totals[1]
                + jnp.where(row == 0, above, falling)
                + jnp.where(row == STRIP - 1, 0.0, rising)
            )
            return falling, partial

        _, partial = lax.fori_loop(0, strips, smooth, (zero, zero), unroll=strips)
        done = slice((strips - 1) * STRIP, strips * STRIP)
        kept[smoothed, done, :] = coef[9, done, :] * partial

        def operate(strip, carried):
            rows = strip_rows(strip)
            kept[order + 1, rows, :] = applied(
                lambda k: coef[k, rows, :],
                kept[smoothed, rows, :],
                kept[smoothed, strip_rows(jnp.maximum(strip - 1, 0)), :],
                kept[smoothed, strip_rows(jnp.minimum(strip + 1, strips - 1)), :],
                kept[order, rows, :],
            )
            return carried

        lax.fori_loop(0, strips, operate, 0, unroll=strips)


def tile_kernel(*refs):
    own, columns, kept, sums, handed, coef, wide = refs[0:6], *refs[6:12]
    strips = kept.shape[1] // STRIP
    side = lax.axis_index("gx")
    for which, block in enumerate(spread(columns[...], side)):
        wide[which] = block

    def load(which, strip):
        rows = strip_rows(strip)
        return jnp.concatenate([field(own, which, rows), wide[which, rows, :]], axis=1)

    krylov(load, strips, coef, kept)
    zero = jnp.zeros((STRIP, LANES), jnp.float32)
    breadth = kept.shape[2] - LANES
    totals = lax.fori_loop(
        1,
        strips - 1,
        lambda strip, totals: gathered(totals, kept, strip_rows(strip), breadth),
        (zero,) * PRODUCTS,
        unroll=7,
    )
    for index in range(PRODUCTS):
        sums[index] = totals[index]
    first, last = slice(0, STRIP), slice((strips - 1) * STRIP, strips * STRIP)
    second, third = slice(STRIP, 2 * STRIP), slice((strips - 2) * STRIP, (strips - 1) * STRIP)
    for index in range(COEFFICIENTS):
        handed[index] = coef[index, first, :]
        handed[COEFFICIENTS + index] = coef[index, last, :]
    for index in range(3):
        handed[NEAR + index] = coef[index, second, :]
        handed[NEAR + 3 + index] = coef[6 + index, third, :]
    handed[SOUTH] = load(5, 0)
    handed[FIRST] = kept[0, first, :]
    handed[FIRST + 1] = kept[0, last, :]
    for index in range(KEPT):
        handed[BASIS + index] = kept[index, second, :]
        handed[BASIS + KEPT + index] = kept[index, third, :]


def edge_kernel(
    handed, even, odd, even_corner, odd_corner, sums, kept, gram, joined, coef, outer
):
    breadth = even.shape[0] // PACKED * LANES
    width = breadth + LANES
    side = lax.axis_index("gx")
    parity = lax.rem(lax.axis_index("gy"), 2)
    low_corner = spread(jnp.where(parity == 0, odd_corner[...], even_corner[...]), side)
    high_corner = spread(jnp.where(parity == 0, even_corner[...], odd_corner[...]), side)
    low_rows, high_rows = slice(0, STRIP), slice(STRIP, 2 * STRIP)
    place_low, place_high = 0, 0
    for which in range(FIELDS):
        joined[which, :, 0:breadth] = jnp.zeros((2 * STRIP, breadth), jnp.float32)
        joined[which, low_rows, breadth:width] = low_corner[which]
        joined[which, high_rows, breadth:width] = high_corner[which]
        count = LOW_ROWS[which]
        for place, lanes in stacked(place_low, count, breadth):
            joined[which, STRIP - count : STRIP, lanes] = jnp.where(
                parity == 0, odd[place, :], even[place, :]
            )
        place_low += count
        count = HIGH_ROWS[which]
        for place, lanes in stacked(place_high, count, breadth):
            joined[which, STRIP : STRIP + count, lanes] = jnp.where(
                parity == 0, even[place, :], odd[place, :]
            )
        place_high += count

    zero = jnp.zeros((STRIP, width), jnp.float32)
    values, _ = coefficients(lambda which: joined[which, low_rows, :], handed[SOUTH])
    for index, value in enumerate(values):
        coef[index, low_rows, :] = value
    values, south = coefficients(lambda which: joined[which, high_rows, :], zero)
    for index, value in enumerate(values):
        coef[index, high_rows, :] = value
    row = lax.broadcasted_iota(jnp.int32, zero.shape, 0)
    missing = (
        handed[COEFFICIENTS + 9]
        * (1.0 / SCALE)
        * jnp.where(row == STRIP - 1, pltpu.roll(south, STRIP - 1, 0), 0.0)
    )

    def getter(strip):
        if strip == 0:
            return lambda k: coef[k, low_rows, :]
        if strip == 3:
            return lambda k: coef[k, high_rows, :]
        if strip == 1:
            return lambda k: handed[k]
        return lambda k: handed[COEFFICIENTS + k] + (missing if k in (10, 14) else 0.0)

    getters = [getter(strip) for strip in range(4)]
    inner = [slice(0, STRIP), slice(STRIP, 2 * STRIP)]

    def write(index, strip, value):
        if strip in (1, 2):
            kept[index, inner[strip - 1], :] = value
        else:
            outer[index, low_rows if strip == 0 else high_rows, :] = value

    def read(index, strip):
        if strip in (1, 2):
            return kept[index, inner[strip - 1], :]
        return outer[index, low_rows if strip == 0 else high_rows, :]

    write(0, 0, joined[0, low_rows, :])
    write(0, 3, joined[0, high_rows, :])
    write(0, 1, handed[FIRST])
    write(0, 2, handed[FIRST + 1])
    for order in range(ITERS):
        smoothed = ITERS + 1 + order
        totals = [weighted(getters[strip], read(order, strip)) for strip in range(4)]
        rising = weighted(lambda k: handed[NEAR + k], handed[BASIS + order], (0,))[0]
        falling = weighted(
            lambda k: handed[NEAR + 3 + k], handed[BASIS + KEPT + order], (0,)
        )[0]
        above = [zero, totals[0][2], falling, totals[2][2]]
        below = [totals[1][0], rising, totals[3][0], zero]
        for strip in range(4):
            write(
                smoothed,
                strip,
                getters[strip](9)
                * (
                    totals[strip][1]
                    + row_above(totals[strip][2], above[strip])
                    + row_below(totals[strip][0], below[strip])
                ),
            )
        blocks = [read(smoothed, strip) for strip in range(4)]
        before = [zero, blocks[0], handed[BASIS + KEPT + smoothed], blocks[2]]
        after = [blocks[1], handed[BASIS + smoothed], blocks[3], zero]
        for strip in range(4) if order < ITERS - 1 else (1, 2):
            write(
                order + 1,
                strip,
                applied(
                    getters[strip],
                    blocks[strip],
                    before[strip],
                    after[strip],
                    read(order, strip),
                ),
            )
    totals = tuple(sums[i] for i in range(PRODUCTS))
    for rows in inner:
        totals = gathered(totals, kept, rows, breadth)
    gram[...] = jnp.zeros(gram.shape, jnp.float32)
    for index in range(PRODUCTS):
        total = jnp.sum(jnp.sum(totals[index], axis=0, keepdims=True), axis=1, keepdims=True)
        gram[index : index + 1, :] = jnp.broadcast_to(total, (1, LANES))


def recurrences(gram):
    shift, scale = SHIFT, SCALE
    residual = [1.0]
    direction = []
    steps = [0.0] * ITERS
    rz_before = None
    for order in range(ITERS):
        rz = None
        for i in range(order + 1):
            inner = None
            for j in range(order + 1):
                term = residual[j] * gram[i][j]
                inner = term if inner is None else inner + term
            inner = residual[i] * inner
            rz = inner if rz is None else rz + inner
        if order == 0:
            direction = [1.0]
        else:
            ratio = rz / rz_before
            direction = [
                residual[i] + ratio * direction[i] if i < order else residual[i]
                for i in range(order + 1)
            ]
        image = [0.0] * (order + 2)
        for i in range(order + 1):
            image[i] = image[i] + shift * direction[i]
            image[i + 1] = image[i + 1] + scale * direction[i]
        curvature = None
        for i in range(order + 2):
            inner = None
            for j in range(order + 1):
                term = direction[j] * gram[i][j]
                inner = term if inner is None else inner + term
            inner = image[i] * inner
            curvature = inner if curvature is None else curvature + inner
        step = rz / curvature
        for i in range(order + 1):
            steps[i] = steps[i] + step * direction[i]
        residual = [
            (residual[i] if i < order + 1 else 0.0) - step * image[i]
            for i in range(order + 2)
        ]
        rz_before = rz
    return steps, residual


def combine_kernel(gram_ref, kept, edges, solution_out, residual_out, *scratch):
    solution_ref, residual_ref, left = scratch
    height, breadth = solution_ref.shape
    part = height // PARTS
    gram = [
        [gram_ref[i * ITERS + j : i * ITERS + j + 1, :] for j in range(ITERS)]
        for i in range(ITERS + 1)
    ]
    steps, residual = recurrences(gram)

    def wide(value):
        value = jnp.broadcast_to(value, (STRIP, LANES))
        return jnp.concatenate([value] * (breadth // LANES), axis=1)

    def put(source, rows_from, rows_to):
        total = None
        for j in range(ITERS):
            term = wide(steps[j]) * source[ITERS + 1 + j, rows_from, 0:breadth]
            total = term if total is None else total + term
        solution_ref[rows_to, :] = total
        total = None
        for i in range(ITERS + 1):
            term = wide(residual[i]) * source[i, rows_from, 0:breadth]
            total = term if total is None else total + term
        residual_ref[rows_to, :] = total

    copies = []
    for step in range(PARTS):
        for strip in range(step * part // STRIP, (step + 1) * part // STRIP):
            rows = slice(strip * STRIP, (strip + 1) * STRIP)
            if strip == 0:
                put(edges, slice(0, STRIP), rows)
            elif strip == height // STRIP - 1:
                put(edges, slice(STRIP, 2 * STRIP), rows)
            else:
                put(kept, rows, rows)
        rows = pl.ds(step * part, part)
        for index, (source, target) in enumerate(
            ((solution_ref, solution_out), (residual_ref, residual_out))
        ):
            copy = pltpu.make_async_copy(
                source.at[rows, :], target.at[rows, :], left.at[index, step]
            )
            copy.start()
            copies.append(copy)
    for copy in copies:
        copy.wait()


def params(limit=VMEM_BYTES):
    return pltpu.CompilerParams(vmem_limit_bytes=limit)


def cost(flops, moved):
    return pl.CostEstimate(flops=flops, bytes_accessed=moved, transcendentals=0)


def body(right_side, faces, ratio, centre, offdiag, mask):
    height, breadth = right_side.shape
    width = breadth + LANES
    args = (right_side, mask, centre, ratio, faces, offdiag)
    held = [pltpu.with_memory_space_constraint(a, pltpu.HBM) for a in args]
    f32 = jnp.float32
    gy = lax.axis_size("gy")
    swap = [(0, 1), (1, 0)]
    pairs = [(i, i ^ 1) for i in range(gy) if i ^ 1 < gy]
    between = [(i, (i + 1 ^ 1) - 1) for i in range(1, gy) if (i + 1 ^ 1) - 1 < gy]

    def diagonal(partners):
        return [(2 * a + c, 2 * b + 1 - c) for a, b in partners for c in (0, 1)]

    packed = jax.ShapeDtypeStruct((breadth // LANES * PACKED, LANES), f32)
    corner = jax.ShapeDtypeStruct((STRIP, LANES), f32)
    columns = jax.ShapeDtypeStruct((height, LANES), f32)
    even, odd, even_corner, odd_corner = pl.pallas_call(
        pack_kernel,
        in_specs=[pl.BlockSpec(memory_space=pltpu.HBM)] * len(args),
        out_shape=(packed, packed, corner, corner),
        scratch_shapes=[
            pltpu.VMEM((2,) + a.shape[:-2] + (STRIP, breadth), a.dtype) for a in args
        ]
        + [pltpu.SemaphoreType.DMA((len(args), 2))],
        compiler_params=params(PACK_VMEM_BYTES),
        cost_estimate=cost(0, 4 * 4 * PACKED * breadth),
        name="pack",
    )(*held)
    columns = pl.pallas_call(
        columns_kernel,
        in_specs=[pl.BlockSpec(memory_space=pltpu.VMEM)] * len(args)
        + [pl.BlockSpec(memory_space=pl.ANY)],
        out_shape=columns,
        compiler_params=params(PACK_VMEM_BYTES),
        cost_estimate=cost(0, 4 * FIELDS * height * LANES),
        name="columns",
    )(*args, odd_corner)
    columns = lax.ppermute(columns, "gx", swap)
    even_in = lax.ppermute(even, "gy", pairs)
    even_corner = lax.ppermute(even_corner, ("gy", "gx"), diagonal(pairs))
    odd_in = lax.ppermute(odd, "gy", between)
    odd_corner = lax.ppermute(odd_corner, ("gy", "gx"), diagonal(between))

    cells = height * width
    kept, sums, handed = pl.pallas_call(
        tile_kernel,
        out_shape=(
            jax.ShapeDtypeStruct((KEPT, height, width), f32),
            jax.ShapeDtypeStruct((PRODUCTS, STRIP, LANES), f32),
            jax.ShapeDtypeStruct((HANDED, STRIP, width), f32),
        ),
        scratch_shapes=[
            pltpu.VMEM((COEFFICIENTS, height, width), f32),
            pltpu.VMEM((FIELDS, height, LANES), f32),
        ],
        compiler_params=params(TILE_VMEM_BYTES),
        cost_estimate=cost(100 * cells, 4 * cells * (FIELDS + KEPT)),
        name="tile",
    )(*args, columns)

    sums, even_in, odd_in, even_corner, odd_corner = lax.optimization_barrier(
        (sums, even_in, odd_in, even_corner, odd_corner)
    )
    rows = 2 * STRIP
    edges, gram = pl.pallas_call(
        edge_kernel,
        out_shape=(
            jax.ShapeDtypeStruct((KEPT, rows, width), f32),
            jax.ShapeDtypeStruct((2 * STRIP, LANES), f32),
        ),
        scratch_shapes=[
            pltpu.VMEM((FIELDS, rows, width), f32),
            pltpu.VMEM((COEFFICIENTS, rows, width), f32),
            pltpu.VMEM((KEPT, rows, width), f32),
        ],
        compiler_params=params(),
        cost_estimate=cost(200 * rows * width, 4 * rows * width * (FIELDS + KEPT)),
        name="edge",
    )(handed, even_in, odd_in, even_corner, odd_corner, sums)

    gram = gram + lax.ppermute(gram, "gx", swap)
    reach = 1
    while reach < gy:
        gram = gram + lax.ppermute(gram, "gy", [(i, i ^ reach) for i in range(gy)])
        reach *= 2

    tile = jax.ShapeDtypeStruct((height, breadth), f32)
    return pl.pallas_call(
        combine_kernel,
        out_specs=(pl.BlockSpec(memory_space=pltpu.HBM),) * 2,
        out_shape=(tile, tile),
        scratch_shapes=[pltpu.VMEM(tile.shape, f32)] * 2
        + [pltpu.SemaphoreType.DMA((2, PARTS))],
        compiler_params=params(),
        cost_estimate=cost(14 * height * breadth, 4 * height * breadth * (KEPT + 2)),
        name="combine",
    )(gram, kept, edges)


def solution(mesh):
    return jax.shard_map(
        body,
        mesh=mesh,
        in_specs=(
            P(("members", "gy"), "gx"),
            P(None, "gy", "gx"),
            P("gy", "gx"),
            P("gy", "gx"),
            P(None, "gy", "gx"),
            P("gy", "gx"),
        ),
        out_specs=(P(("members", "gy"), "gx"), P(("members", "gy"), "gx")),
        check_vma=False,
    )
```

```python
import functools

import jax
import jax.numpy as jnp
from jax import lax
from jax.experimental import pallas as pl
from jax.experimental.pallas import tpu as pltpu
from jax.sharding import PartitionSpec as P

ITERS = 3
SHIFT = 0.7
SCALE = 4.0
LANES = 128
STRIP = 8

neighbour_steps = [(-1, -1), (-1, 0), (-1, 1), (0, -1), (0, 1), (1, -1), (1, 0), (1, 1)]

FIELDS = 6 + len(neighbour_steps)
REACH = 2 * ITERS
LOW_ROWS = [REACH, REACH - 1, REACH - 1, REACH - 2, REACH - 2, REACH - 2] + [
    REACH - 1 + down for down, _ in neighbour_steps
]
HIGH_ROWS = [REACH, REACH - 1, REACH - 1, REACH - 2, REACH - 2, REACH - 1] + [
    REACH - 1 - down for down, _ in neighbour_steps
]
PACKED = max(sum(LOW_ROWS), sum(HIGH_ROWS))
PRODUCTS = (ITERS + 1) * ITERS
KEPT = 2 * ITERS + 1
SLOT = 8
PARTS = 4
COEFFICIENTS = 15
NEAR = 2 * COEFFICIENTS
SOUTH = NEAR + 6
FIRST = SOUTH + 1
BASIS = FIRST + 2
HANDED = BASIS + 2 * KEPT
TILE_VMEM_BYTES = 40 * 1024 * 1024
VMEM_BYTES = 32 * 1024 * 1024
PACK_VMEM_BYTES = 16 * 1024 * 1024


def field(refs, which, rows):
    right_side, mask, centre, ratio, faces, offdiag = refs
    if which == 0:
        return mask[rows, :].astype(jnp.float32) * right_side[rows, :]
    if which == 1:
        return mask[rows, :].astype(jnp.float32)
    if which == 2:
        return centre[rows, :]
    if which == 3:
        return ratio[rows, :]
    if which < 6:
        return faces[which - 4, rows, :]
    return offdiag[which - 6, rows, :]


def stacked(place, count, breadth):
    for block in range(breadth // LANES):
        start = block * PACKED + place
        yield slice(start, start + count), slice(block * LANES, (block + 1) * LANES)


def trimmed(out, refs, counts, at_end):
    breadth = out.shape[0] // PACKED * LANES
    place = 0
    for which, count in enumerate(counts):
        rows = slice(STRIP - count, STRIP) if at_end else slice(0, count)
        value = field(refs, which, rows)
        for target, lanes in stacked(place, count, breadth):
            out[target, :] = value[:, lanes]
        place += count
    if place < PACKED:
        zero = jnp.zeros((PACKED - place, LANES), jnp.float32)
        for target, _ in stacked(place, PACKED - place, breadth):
            out[target, :] = zero


def lanes_of(shape):
    return lax.broadcasted_iota(jnp.int32, shape, len(shape) - 1)


def beside(refs, which, rows, side):
    breadth = refs[0].shape[1]
    west = field([ref.at[..., 0:LANES] for ref in refs], which, rows)
    east = field([ref.at[..., breadth - LANES : breadth] for ref in refs], which, rows)
    return jnp.where(side == 0, east, west)


def squeezed(near, side):
    start = jnp.where(side == 0, SLOT, 0)
    total = None
    for which in range(FIELDS):
        block = pltpu.roll(near(which), start + SLOT * which, 1)
        if total is None:
            lane = lanes_of(block.shape)
            total = jnp.zeros(block.shape, jnp.float32)
        inside = (lane >= SLOT * which) & (lane < SLOT * (which + 1))
        total = jnp.where(inside, block, total)
    return total


def spread(block, side):
    lane = lanes_of(block.shape)
    start = jnp.where(side == 0, LANES, LANES - SLOT)
    first = jnp.where(side == 0, 0, LANES - SLOT)
    inside = ((lane >= first) & (lane < first + SLOT)).astype(jnp.float32)
    return [
        pltpu.roll(block, start - SLOT * which, 1) * inside for which in range(FIELDS)
    ]


def pack_kernel(*refs):
    args = refs[0:6]
    even, odd, even_corner, odd_corner = refs[6:10]
    ends, arrived = refs[10:16], refs[16]
    height, breadth = args[0].shape
    side = lax.axis_index("gx")
    parity = lax.rem(lax.axis_index("gy"), 2)
    copies = []
    for index, (arg, end) in enumerate(zip(args, ends)):
        lead = (slice(None),) * (len(arg.shape) - 2)
        for which, start in enumerate((0, height - STRIP)):
            copies.append(
                pltpu.make_async_copy(
                    arg.at[lead + (pl.ds(start, STRIP), slice(None))],
                    end.at[which],
                    arrived.at[index, which],
                )
            )
    for copy in copies:
        copy.start()
    for copy in copies:
        copy.wait()
    first = [end.at[0] for end in ends]
    last = [end.at[1] for end in ends]
    rows = slice(0, STRIP)
    corner_first = squeezed(lambda which: beside(first, which, rows, side), side)
    corner_last = squeezed(lambda which: beside(last, which, rows, side), side)
    even_corner[...] = jnp.where(parity == 0, corner_last, corner_first)
    odd_corner[...] = jnp.where(parity == 0, corner_first, corner_last)

    @pl.when(parity == 0)
    def _():
        trimmed(even, last, LOW_ROWS, True)
        trimmed(odd, first, HIGH_ROWS, False)

    @pl.when(parity != 0)
    def _():
        trimmed(even, first, HIGH_ROWS, False)
        trimmed(odd, last, LOW_ROWS, True)


def columns_kernel(*refs):
    args, columns = refs[0:6], refs[7]
    side = lax.axis_index("gx")
    columns[...] = squeezed(lambda which: beside(args, which, slice(None), side), side)


def row_above(block, before):
    row = lax.broadcasted_iota(jnp.int32, block.shape, 0)
    return jnp.where(row == 0, pltpu.roll(before, 1, 0), pltpu.roll(block, 1, 0))


def row_below(block, after):
    row = lax.broadcasted_iota(jnp.int32, block.shape, 0)
    last = STRIP - 1
    return jnp.where(row == last, pltpu.roll(after, last, 0), pltpu.roll(block, last, 0))


def strip_rows(strip):
    return pl.ds(pl.multiple_of(strip * STRIP, STRIP), STRIP)


def west_of(block):
    return pltpu.roll(block, 1, 1)


def east_of(block):
    return pltpu.roll(block, block.shape[1] - 1, 1)


def coefficients(get, south_after):
    result = [None] * COEFFICIENTS
    wet = get(1)
    result[4] = get(2)
    for index, (down, across) in enumerate(neighbour_steps):
        weight = get(6 + index)
        if across == 1:
            weight = west_of(weight)
        elif across == -1:
            weight = east_of(weight)
        result[(down + 1) * 3 + across + 1] = weight
    west = get(4)
    south = get(5)
    east = east_of(west)
    north = row_below(south, south_after)
    scaled = wet * (1.0 / SCALE)
    result[9] = wet
    result[10] = scaled * (west + east + south + north + get(3))
    result[11] = scaled * west
    result[12] = scaled * east
    result[13] = scaled * south
    result[14] = scaled * north
    return result, south


def weighted(get, block, downs=(0, 1, 2)):
    left, right = east_of(block), west_of(block)
    return [
        get(down * 3) * left + get(down * 3 + 1) * block + get(down * 3 + 2) * right
        for down in downs
    ]


def applied(get, block, before, after, old):
    return (
        get(10) * block
        - get(11) * west_of(block)
        - get(12) * east_of(block)
        - get(13) * row_above(block, before)
        - get(14) * row_below(block, after)
        - (SHIFT / SCALE) * old
    )


def gathered(totals, kept, rows, breadth):
    result = list(totals)
    for start in range(0, breadth, LANES):
        bases = [kept[i, rows, start : start + LANES] for i in range(KEPT)]
        for i in range(ITERS + 1):
            for j in range(ITERS):
                result[i * ITERS + j] += bases[i] * bases[ITERS + 1 + j]
    return tuple(result)


def krylov(load, strips, coef, kept):
    width = kept.shape[2]
    zero = jnp.zeros((STRIP, width), jnp.float32)

    def prepare(step, south_after):
        strip = strips - 1 - step
        rows = strip_rows(strip)
        kept[0, rows, :] = load(0, strip)
        values, south = coefficients(lambda which: load(which, strip), south_after)
        for index, value in enumerate(values):
            coef[index, rows, :] = value
        return south

    lax.fori_loop(0, strips, prepare, zero, unroll=strips)

    for order in range(ITERS):
        smoothed = ITERS + 1 + order

        def smooth(strip, carried):
            above, partial = carried
            rows = strip_rows(strip)
            totals = weighted(lambda k: coef[k, rows, :], kept[order, rows, :])
            row = lax.broadcasted_iota(jnp.int32, totals[0].shape, 0)
            rising = pltpu.roll(totals[0], STRIP - 1, 0)
            falling = pltpu.roll(totals[2], 1, 0)
            done = strip_rows(jnp.maximum(strip - 1, 0))
            kept[smoothed, done, :] = coef[9, done, :] * (
                partial + jnp.where(row == STRIP - 1, rising, 0.0)
            )
            partial = (
                totals[1]
                + jnp.where(row == 0, above, falling)
                + jnp.where(row == STRIP - 1, 0.0, rising)
            )
            return falling, partial

        _, partial = lax.fori_loop(0, strips, smooth, (zero, zero), unroll=strips)
        done = slice((strips - 1) * STRIP, strips * STRIP)
        kept[smoothed, done, :] = coef[9, done, :] * partial

        def operate(strip, carried):
            rows = strip_rows(strip)
            kept[order + 1, rows, :] = applied(
                lambda k: coef[k, rows, :],
                kept[smoothed, rows, :],
                kept[smoothed, strip_rows(jnp.maximum(strip - 1, 0)), :],
                kept[smoothed, strip_rows(jnp.minimum(strip + 1, strips - 1)), :],
                kept[order, rows, :],
            )
            return carried

        lax.fori_loop(0, strips, operate, 0, unroll=strips)


def tile_kernel(*refs):
    own, columns, kept, sums, handed, coef, wide = refs[0:6], *refs[6:12]
    strips = kept.shape[1] // STRIP
    side = lax.axis_index("gx")
    for which, block in enumerate(spread(columns[...], side)):
        wide[which] = block

    def load(which, strip):
        rows = strip_rows(strip)
        return jnp.concatenate([field(own, which, rows), wide[which, rows, :]], axis=1)

    krylov(load, strips, coef, kept)
    zero = jnp.zeros((STRIP, LANES), jnp.float32)
    breadth = kept.shape[2] - LANES
    totals = lax.fori_loop(
        1,
        strips - 1,
        lambda strip, totals: gathered(totals, kept, strip_rows(strip), breadth),
        (zero,) * PRODUCTS,
        unroll=7,
    )
    for index in range(PRODUCTS):
        sums[index] = totals[index]
    first, last = slice(0, STRIP), slice((strips - 1) * STRIP, strips * STRIP)
    second, third = slice(STRIP, 2 * STRIP), slice((strips - 2) * STRIP, (strips - 1) * STRIP)
    for index in range(COEFFICIENTS):
        handed[index] = coef[index, first, :]
        handed[COEFFICIENTS + index] = coef[index, last, :]
    for index in range(3):
        handed[NEAR + index] = coef[index, second, :]
        handed[NEAR + 3 + index] = coef[6 + index, third, :]
    handed[SOUTH] = load(5, 0)
    handed[FIRST] = kept[0, first, :]
    handed[FIRST + 1] = kept[0, last, :]
    for index in range(KEPT):
        handed[BASIS + index] = kept[index, second, :]
        handed[BASIS + KEPT + index] = kept[index, third, :]


def edge_kernel(
    handed, even, odd, even_corner, odd_corner, sums, kept, gram, joined, coef, outer
):
    breadth = even.shape[0] // PACKED * LANES
    width = breadth + LANES
    side = lax.axis_index("gx")
    parity = lax.rem(lax.axis_index("gy"), 2)
    low_corner = spread(jnp.where(parity == 0, odd_corner[...], even_corner[...]), side)
    high_corner = spread(jnp.where(parity == 0, even_corner[...], odd_corner[...]), side)
    low_rows, high_rows = slice(0, STRIP), slice(STRIP, 2 * STRIP)
    place_low, place_high = 0, 0
    for which in range(FIELDS):
        joined[which, :, 0:breadth] = jnp.zeros((2 * STRIP, breadth), jnp.float32)
        joined[which, low_rows, breadth:width] = low_corner[which]
        joined[which, high_rows, breadth:width] = high_corner[which]
        count = LOW_ROWS[which]
        for place, lanes in stacked(place_low, count, breadth):
            joined[which, STRIP - count : STRIP, lanes] = jnp.where(
                parity == 0, odd[place, :], even[place, :]
            )
        place_low += count
        count = HIGH_ROWS[which]
        for place, lanes in stacked(place_high, count, breadth):
            joined[which, STRIP : STRIP + count, lanes] = jnp.where(
                parity == 0, even[place, :], odd[place, :]
            )
        place_high += count

    zero = jnp.zeros((STRIP, width), jnp.float32)
    values, _ = coefficients(lambda which: joined[which, low_rows, :], handed[SOUTH])
    for index, value in enumerate(values):
        coef[index, low_rows, :] = value
    values, south = coefficients(lambda which: joined[which, high_rows, :], zero)
    for index, value in enumerate(values):
        coef[index, high_rows, :] = value
    row = lax.broadcasted_iota(jnp.int32, zero.shape, 0)
    missing = (
        handed[COEFFICIENTS + 9]
        * (1.0 / SCALE)
        * jnp.where(row == STRIP - 1, pltpu.roll(south, STRIP - 1, 0), 0.0)
    )

    def getter(strip):
        if strip == 0:
            return lambda k: coef[k, low_rows, :]
        if strip == 3:
            return lambda k: coef[k, high_rows, :]
        if strip == 1:
            return lambda k: handed[k]
        return lambda k: handed[COEFFICIENTS + k] + (missing if k in (10, 14) else 0.0)

    getters = [getter(strip) for strip in range(4)]
    inner = [slice(0, STRIP), slice(STRIP, 2 * STRIP)]

    def write(index, strip, value):
        if strip in (1, 2):
            kept[index, inner[strip - 1], :] = value
        else:
            outer[index, low_rows if strip == 0 else high_rows, :] = value

    def read(index, strip):
        if strip in (1, 2):
            return kept[index, inner[strip - 1], :]
        return outer[index, low_rows if strip == 0 else high_rows, :]

    write(0, 0, joined[0, low_rows, :])
    write(0, 3, joined[0, high_rows, :])
    write(0, 1, handed[FIRST])
    write(0, 2, handed[FIRST + 1])
    for order in range(ITERS):
        smoothed = ITERS + 1 + order
        totals = [weighted(getters[strip], read(order, strip)) for strip in range(4)]
        rising = weighted(lambda k: handed[NEAR + k], handed[BASIS + order], (0,))[0]
        falling = weighted(
            lambda k: handed[NEAR + 3 + k], handed[BASIS + KEPT + order], (0,)
        )[0]
        above = [zero, totals[0][2], falling, totals[2][2]]
        below = [totals[1][0], rising, totals[3][0], zero]
        for strip in range(4):
            write(
                smoothed,
                strip,
                getters[strip](9)
                * (
                    totals[strip][1]
                    + row_above(totals[strip][2], above[strip])
                    + row_below(totals[strip][0], below[strip])
                ),
            )
        blocks = [read(smoothed, strip) for strip in range(4)]
        before = [zero, blocks[0], handed[BASIS + KEPT + smoothed], blocks[2]]
        after = [blocks[1], handed[BASIS + smoothed], blocks[3], zero]
        for strip in range(4) if order < ITERS - 1 else (1, 2):
            write(
                order + 1,
                strip,
                applied(
                    getters[strip],
                    blocks[strip],
                    before[strip],
                    after[strip],
                    read(order, strip),
                ),
            )
    totals = tuple(sums[i] for i in range(PRODUCTS))
    for rows in inner:
        totals = gathered(totals, kept, rows, breadth)
    gram[...] = jnp.zeros(gram.shape, jnp.float32)
    for index in range(PRODUCTS):
        total = jnp.sum(jnp.sum(totals[index], axis=0, keepdims=True), axis=1, keepdims=True)
        gram[index : index + 1, :] = jnp.broadcast_to(total, (1, LANES))


def recurrences(gram):
    shift, scale = SHIFT, SCALE
    residual = [1.0]
    direction = []
    steps = [0.0] * ITERS
    rz_before = None
    for order in range(ITERS):
        rz = None
        for i in range(order + 1):
            inner = None
            for j in range(order + 1):
                term = residual[j] * gram[i][j]
                inner = term if inner is None else inner + term
            inner = residual[i] * inner
            rz = inner if rz is None else rz + inner
        if order == 0:
            direction = [1.0]
        else:
            ratio = rz / rz_before
            direction = [
                residual[i] + ratio * direction[i] if i < order else residual[i]
                for i in range(order + 1)
            ]
        image = [0.0] * (order + 2)
        for i in range(order + 1):
            image[i] = image[i] + shift * direction[i]
            image[i + 1] = image[i + 1] + scale * direction[i]
        curvature = None
        for i in range(order + 2):
            inner = None
            for j in range(order + 1):
                term = direction[j] * gram[i][j]
                inner = term if inner is None else inner + term
            inner = image[i] * inner
            curvature = inner if curvature is None else curvature + inner
        step = rz / curvature
        for i in range(order + 1):
            steps[i] = steps[i] + step * direction[i]
        residual = [
            (residual[i] if i < order + 1 else 0.0) - step * image[i]
            for i in range(order + 2)
        ]
        rz_before = rz
    return steps, residual


def combine_kernel(gram_ref, kept, edges, solution_out, residual_out, *scratch):
    solution_ref, residual_ref, left = scratch
    height, breadth = solution_ref.shape
    part = height // PARTS
    gram = [
        [gram_ref[i * ITERS + j : i * ITERS + j + 1, :] for j in range(ITERS)]
        for i in range(ITERS + 1)
    ]
    steps, residual = recurrences(gram)

    def wide(value):
        value = jnp.broadcast_to(value, (STRIP, LANES))
        return jnp.concatenate([value] * (breadth // LANES), axis=1)

    def put(source, rows_from, rows_to):
        total = None
        for j in range(ITERS):
            term = wide(steps[j]) * source[ITERS + 1 + j, rows_from, 0:breadth]
            total = term if total is None else total + term
        solution_ref[rows_to, :] = total
        total = None
        for i in range(ITERS + 1):
            term = wide(residual[i]) * source[i, rows_from, 0:breadth]
            total = term if total is None else total + term
        residual_ref[rows_to, :] = total

    copies = []
    for step in range(PARTS):
        for strip in range(step * part // STRIP, (step + 1) * part // STRIP):
            rows = slice(strip * STRIP, (strip + 1) * STRIP)
            if strip == 0:
                put(edges, slice(0, STRIP), rows)
            elif strip == height // STRIP - 1:
                put(edges, slice(STRIP, 2 * STRIP), rows)
            else:
                put(kept, rows, rows)
        rows = pl.ds(step * part, part)
        for index, (source, target) in enumerate(
            ((solution_ref, solution_out), (residual_ref, residual_out))
        ):
            copy = pltpu.make_async_copy(
                source.at[rows, :], target.at[rows, :], left.at[index, step]
            )
            copy.start()
            copies.append(copy)
    for copy in copies:
        copy.wait()


def params(limit=VMEM_BYTES):
    return pltpu.CompilerParams(vmem_limit_bytes=limit)


def cost(flops, moved):
    return pl.CostEstimate(flops=flops, bytes_accessed=moved, transcendentals=0)


def body(right_side, faces, ratio, centre, offdiag, mask):
    height, breadth = right_side.shape
    width = breadth + LANES
    args = (right_side, mask, centre, ratio, faces, offdiag)
    held = [pltpu.with_memory_space_constraint(a, pltpu.HBM) for a in args]
    f32 = jnp.float32
    gy = lax.axis_size("gy")
    swap = [(0, 1), (1, 0)]
    pairs = [(i, i ^ 1) for i in range(gy) if i ^ 1 < gy]
    between = [(i, (i + 1 ^ 1) - 1) for i in range(1, gy) if (i + 1 ^ 1) - 1 < gy]

    def diagonal(partners):
        return [(2 * a + c, 2 * b + 1 - c) for a, b in partners for c in (0, 1)]

    packed = jax.ShapeDtypeStruct((breadth // LANES * PACKED, LANES), f32)
    corner = jax.ShapeDtypeStruct((STRIP, LANES), f32)
    columns = jax.ShapeDtypeStruct((height, LANES), f32)
    even, odd, even_corner, odd_corner = pl.pallas_call(
        pack_kernel,
        in_specs=[pl.BlockSpec(memory_space=pltpu.HBM)] * len(args),
        out_shape=(packed, packed, corner, corner),
        scratch_shapes=[
            pltpu.VMEM((2,) + a.shape[:-2] + (STRIP, breadth), a.dtype) for a in args
        ]
        + [pltpu.SemaphoreType.DMA((len(args), 2))],
        compiler_params=params(PACK_VMEM_BYTES),
        cost_estimate=cost(0, 4 * 4 * PACKED * breadth),
        name="pack",
    )(*held)
    columns = pl.pallas_call(
        columns_kernel,
        in_specs=[pl.BlockSpec(memory_space=pltpu.VMEM)] * len(args)
        + [pl.BlockSpec(memory_space=pl.ANY)],
        out_shape=columns,
        compiler_params=params(PACK_VMEM_BYTES),
        cost_estimate=cost(0, 4 * FIELDS * height * LANES),
        name="columns",
    )(*args, odd_corner)
    columns = lax.ppermute(columns, "gx", swap)
    even_in = lax.ppermute(even, "gy", pairs)
    even_corner = lax.ppermute(even_corner, ("gy", "gx"), diagonal(pairs))
    odd_in = lax.ppermute(odd, "gy", between)
    odd_corner = lax.ppermute(odd_corner, ("gy", "gx"), diagonal(between))

    cells = height * width
    kept, sums, handed = pl.pallas_call(
        tile_kernel,
        out_shape=(
            jax.ShapeDtypeStruct((KEPT, height, width), f32),
            jax.ShapeDtypeStruct((PRODUCTS, STRIP, LANES), f32),
            jax.ShapeDtypeStruct((HANDED, STRIP, width), f32),
        ),
        scratch_shapes=[
            pltpu.VMEM((COEFFICIENTS, height, width), f32),
            pltpu.VMEM((FIELDS, height, LANES), f32),
        ],
        compiler_params=params(TILE_VMEM_BYTES),
        cost_estimate=cost(100 * cells, 4 * cells * (FIELDS + KEPT)),
        name="tile",
    )(*args, columns)

    sums, even_in, odd_in, even_corner, odd_corner = lax.optimization_barrier(
        (sums, even_in, odd_in, even_corner, odd_corner)
    )
    rows = 2 * STRIP
    edges, gram = pl.pallas_call(
        edge_kernel,
        out_shape=(
            jax.ShapeDtypeStruct((KEPT, rows, width), f32),
            jax.ShapeDtypeStruct((2 * STRIP, LANES), f32),
        ),
        scratch_shapes=[
            pltpu.VMEM((FIELDS, rows, width), f32),
            pltpu.VMEM((COEFFICIENTS, rows, width), f32),
            pltpu.VMEM((KEPT, rows, width), f32),
        ],
        compiler_params=params(),
        cost_estimate=cost(200 * rows * width, 4 * rows * width * (FIELDS + KEPT)),
        name="edge",
    )(handed, even_in, odd_in, even_corner, odd_corner, sums)

    reach = 1
    while reach < gy:
        gram = gram + lax.ppermute(gram, "gy", [(i, i ^ reach) for i in range(gy)])
        reach *= 2

    gram = gram + lax.ppermute(gram, "gx", swap)

    tile = jax.ShapeDtypeStruct((height, breadth), f32)
    return pl.pallas_call(
        combine_kernel,
        out_specs=(pl.BlockSpec(memory_space=pltpu.HBM),) * 2,
        out_shape=(tile, tile),
        scratch_shapes=[pltpu.VMEM(tile.shape, f32)] * 2
        + [pltpu.SemaphoreType.DMA((2, PARTS))],
        compiler_params=params(),
        cost_estimate=cost(14 * height * breadth, 4 * height * breadth * (KEPT + 2)),
        name="combine",
    )(gram, kept, edges)


def solution(mesh):
    return jax.shard_map(
        body,
        mesh=mesh,
        in_specs=(
            P(("members", "gy"), "gx"),
            P(None, "gy", "gx"),
            P("gy", "gx"),
            P("gy", "gx"),
            P(None, "gy", "gx"),
            P("gy", "gx"),
        ),
        out_specs=(P(("members", "gy"), "gx"), P(("members", "gy"), "gx")),
        check_vma=False,
    )
```
